128 devices in a mesh: row: 8 (over z, y_hi), col: 16 (over x, y_lo, core).
Axes of the slice: x: 4, y: 4 (y_hi: 2, y_lo: 2; y = y_hi * 2 + y_lo), z: 4, core: 2. Of those that a mesh axis runs over, the one named last changes fastest.
Arguments:
- features: bfloat16 [64, 512, 512], P('row', 'col'), may hold values from -6 to 6
- cotangent: bfloat16 [64, 512, 512], P('row', 'col'), may hold values from -6 to 6
- dw_kernel: float32 [49, 512], replicated, may hold values from -0.875 to 0.875
- dw_bias: float32 [512], replicated, may hold values from -3 to 3
- norm_gain_vector: float32 [512], replicated, may hold values from 0.25 to 1.75
- norm_bias: float32 [512], replicated, may hold values from -3 to 3
- pw_in_weight: bfloat16 [512, 2048], replicated, may hold values from -0.25 to 0.25
- pw_in_bias: float32 [2048], replicated, may hold values from -3 to 3
- pw_out_weight: bfloat16 [2048, 512], replicated, may hold values from -0.125 to 0.125
- pw_out_bias: float32 [512], replicated, may hold values from -3 to 3
- layer_scale: float32 [512], replicated, may hold values from 0.25 to 1
Outputs:
- block_out: bfloat16 [64, 512, 512], P('row', 'col')
- grad_features: bfloat16 [64, 512, 512], P('row', 'col')
- grad_pw_in: float32 [512, 2048], P(('row', 'col'))
- grad_pw_out: float32 [2048, 512], P(('row', 'col'))
- grad_channel: float32 [54, 512], P(None, ('row', 'col'))
- grad_pw_in_bias: float32 [2048], P(('row', 'col'))
The draws below stay inside these ranges and needn't reach their ends.
All inputs are finite; a program needn't handle non-finite values.
Results may differ from the reference program's by a relative error of at most 0.013.
Values may be sent and summed in bfloat16 or wider, within the bound.
No kernel may reach another device: no remote copies, remote signals or barrier semaphores. Data moves between devices by JAX's collectives and lax.ppermute only.
A program may use at most 64 MiB of HBM per device.

```python
import math
import jax
import jax.numpy as jnp
from jax import lax

CHANNELS = 512
HIDDEN_SIZE = 2048
KSIZE = 7
TILE_H = 8
HEIGHT = 64
WIDTH = 512
TOKENS = 32768
N_ROW = 8


def spiked(array, own_key, source, target, shards_of, factor):
    def block_of(axis_at):
        return (jnp.arange(array.shape[axis_at]) // (array.shape[axis_at] // shards_of)).reshape((-1,) + (1,) * (array.ndim - 1 - axis_at))

    near = jax.random.permutation(own_key, shards_of)[block_of(target)]
    other_side = (block_of(target) + shards_of // 2) % shards_of
    return jnp.where((block_of(source) == near) | (block_of(source) == other_side), factor * array, array)


def level_of(stream_key, extent, shards, smallest, high):
    loudness, own = 1.0, jax.random.fold_in(stream_key, 6)
    for position, shards_of in shards:
        steps = jnp.exp(jax.random.uniform(jax.random.fold_in(own, position), (shards_of,), jnp.float32, smallest / len(shards), high / len(shards)))
        loudness = loudness * jnp.repeat(steps, extent[position] // shards_of).reshape([-1 if axis == position else 1 for axis in range(len(extent))])
    return loudness


def scatter_about(rng, dims, scale, reach, shards=(), held_as=jnp.bfloat16):
    result = scale * jax.random.normal(rng, dims, jnp.float32)
    if shards:
        result = result * level_of(rng, dims, shards, -0.22, 0.18)
    return jnp.clip(result, -reach, reach).astype(held_as)


def noise_with(stream_key, extent, spread, reach, cuts, heavy, kind=jnp.bfloat16):
    array = spread * jax.random.normal(stream_key, extent, jnp.float32)
    if cuts:
        array = array * level_of(stream_key, extent, cuts, -0.22, 0.18)
    return jnp.clip(spiked(array, jax.random.fold_in(stream_key, 3), *heavy), -reach, reach).astype(kind)


def setup_inputs(seed: int = 0) -> dict:
    seeds = jax.random.split(jax.random.key(seed), 12)
    features = scatter_about(seeds[0], (HEIGHT, WIDTH, CHANNELS), 1.0, 6.0, ((0, 8), (1, 16)))
    cotangent = noise_with(seeds[1], (HEIGHT, WIDTH, CHANNELS), 1.0, 6.0, ((0, 8), (1, 16)), (1, 2, 16, 2.0))
    dw_kernel = scatter_about(seeds[2], (KSIZE * KSIZE, CHANNELS), (KSIZE * KSIZE) ** -0.5, 0.875, (), jnp.float32)
    dw_bias = scatter_about(seeds[3], (CHANNELS,), 0.5, 3.0, (), jnp.float32)
    norm_gain_vector = jnp.clip(1.0 + 0.15 * jax.random.normal(seeds[4], (CHANNELS,), jnp.float32), 0.25, 1.75)
    norm_bias = scatter_about(seeds[5], (CHANNELS,), 0.5, 3.0, (), jnp.float32)
    pw_in_weight = scatter_about(seeds[6], (CHANNELS, HIDDEN_SIZE), CHANNELS ** -0.5, 0.25)
    pw_in_bias = scatter_about(seeds[7], (HIDDEN_SIZE,), 0.5, 3.0, (), jnp.float32)
    pw_out_weight = scatter_about(seeds[8], (HIDDEN_SIZE, CHANNELS), HIDDEN_SIZE ** -0.5, 0.125)
    pw_out_bias = scatter_about(seeds[9], (CHANNELS,), 0.5, 3.0, (), jnp.float32)
    layer_scale = jnp.clip(jnp.exp(jax.random.uniform(seeds[10], (CHANNELS,), jnp.float32, math.log(0.25), math.log(1.0))), 0.25, 1.0)
    return {"features": features, "cotangent": cotangent, "dw_kernel": dw_kernel, "dw_bias": dw_bias, "norm_gain_vector": norm_gain_vector, "norm_bias": norm_bias, "pw_in_weight": pw_in_weight, "pw_in_bias": pw_in_bias, "pw_out_weight": pw_out_weight, "pw_out_bias": pw_out_bias, "layer_scale": layer_scale}


def gelu_plain(value):
    return 0.5 * value * (1.0 + jax.scipy.special.erf(value * 0.7071067811865476))

def gelu_slope(value):
    cumul = 0.5 * (1.0 + jax.scipy.special.erf(value * 0.7071067811865476))
    return cumul + value * jnp.exp(-0.5 * value * value) * 0.3989422804014327

def interior_rows(left, right):
    return lax.dot_general(left, right, (((0,), (0,)), ((), ())), preferred_element_type=jnp.float32)

def inner_cols(left, right):
    return lax.dot_general(left, right, (((1,), (1,)), ((), ())), preferred_element_type=jnp.float32)

def depthwise(padded, dw_kernel, dw_bias, height, width):
    total = jnp.zeros((height, width, padded.shape[2]), jnp.float32)
    for row_tap in range(7):
        for col_tap in range(7):
            piece = padded[row_tap:row_tap + height, col_tap:col_tap + width, :].astype(jnp.float32)
            total = total + piece * dw_kernel[7 * row_tap + col_tap]
    return total + dw_bias

def transposed(d_padded, dw_kernel, height, width):
    total = jnp.zeros((height, width, d_padded.shape[2]), jnp.float32)
    for row_tap in range(7):
        for col_tap in range(7):
            piece = d_padded[6 - row_tap:6 - row_tap + height, 6 - col_tap:6 - col_tap + width, :].astype(jnp.float32)
            total = total + piece * dw_kernel[7 * row_tap + col_tap]
    return total

def kernel_terms(padded, convolution_gradient, height, width):
    d_float = convolution_gradient.astype(jnp.float32)
    rows_out = []
    for row_tap in range(7):
        for col_tap in range(7):
            piece = padded[row_tap:row_tap + height, col_tap:col_tap + width, :].astype(jnp.float32)
            rows_out.append(lax.optimization_barrier(jnp.sum(piece * d_float, axis=(0, 1))))
    return jnp.stack(rows_out, axis=0)

def pointwise(conv_rows, feat_rows, cot_rows, norm_gain_vector, norm_bias, pw_in_weight, pw_in_bias, pw_out_weight, pw_out_bias, layer_scale):
    mean_c = lax.optimization_barrier(jnp.mean(conv_rows, axis=-1, keepdims=True))
    centred = conv_rows - mean_c
    inverse_deviation = lax.rsqrt(lax.optimization_barrier(jnp.mean(centred * centred, axis=-1, keepdims=True)) + 1e-06)
    centered_input = centred * inverse_deviation
    normed = (centered_input * norm_gain_vector + norm_bias).astype(jnp.bfloat16)
    pre_act = jnp.dot(normed, pw_in_weight, preferred_element_type=jnp.float32) + pw_in_bias
    act = gelu_plain(pre_act).astype(jnp.bfloat16)
    branch = jnp.dot(act, pw_out_weight, preferred_element_type=jnp.float32) + pw_out_bias
    block_rows = (feat_rows.astype(jnp.float32) + layer_scale * branch).astype(jnp.bfloat16)
    cot_float = cot_rows.astype(jnp.float32)
    g_scale = lax.optimization_barrier(jnp.sum(cot_float * branch, axis=0))
    d_branch = (cot_float * layer_scale).astype(jnp.bfloat16)
    g_out_bias = lax.optimization_barrier(jnp.sum(d_branch.astype(jnp.float32), axis=0))
    d_act = inner_cols(d_branch, pw_out_weight)
    d_pre = (d_act * gelu_slope(pre_act)).astype(jnp.bfloat16)
    g_in_bias = lax.optimization_barrier(jnp.sum(d_pre.astype(jnp.float32), axis=0))
    normalized_gradient = inner_cols(d_pre, pw_in_weight)
    g_gain = lax.optimization_barrier(jnp.sum(normalized_gradient * centered_input, axis=0))
    g_nbias = lax.optimization_barrier(jnp.sum(normalized_gradient, axis=0))
    centered_input_gradient = normalized_gradient * norm_gain_vector
    convolution_gradient = inverse_deviation * (centered_input_gradient - lax.optimization_barrier(jnp.mean(centered_input_gradient, axis=-1, keepdims=True)) - centered_input * lax.optimization_barrier(jnp.mean(centered_input_gradient * centered_input, axis=-1, keepdims=True)))
    convolution_gradient = convolution_gradient.astype(jnp.bfloat16)
    return (block_rows, convolution_gradient, normed, act, d_branch, d_pre, (g_in_bias, g_out_bias, g_scale, g_gain, g_nbias))

def reference(features, cotangent, dw_kernel, dw_bias, norm_gain_vector, norm_bias, pw_in_weight, pw_in_bias, pw_out_weight, pw_out_bias, layer_scale):
    padded = jnp.pad(features, ((3, 3), (3, 3), (0, 0)))
    conv_out = depthwise(padded, dw_kernel, dw_bias, HEIGHT, WIDTH)
    band_len = TILE_H * WIDTH
    conv_bands = conv_out.reshape(N_ROW, band_len, CHANNELS)
    feat_bands = features.reshape(N_ROW, band_len, CHANNELS)
    cot_bands = cotangent.reshape(N_ROW, band_len, CHANNELS)

    def one_band(carry, pieces):
        conv_rows, feat_rows, cot_rows = pieces
        block_rows, convolution_gradient, normed, act, d_branch, d_pre, smalls = pointwise(conv_rows, feat_rows, cot_rows, norm_gain_vector, norm_bias, pw_in_weight, pw_in_bias, pw_out_weight, pw_out_bias, layer_scale)
        grad_in = carry[0] + interior_rows(normed, d_pre)
        grad_out = carry[1] + interior_rows(act, d_branch)
        rest = tuple((total + term for total, term in zip(carry[2], smalls)))
        return ((grad_in, grad_out, rest), (block_rows, convolution_gradient))
    zeros_c = jnp.zeros((CHANNELS,), jnp.float32)
    init = (jnp.zeros((CHANNELS, HIDDEN_SIZE), jnp.float32), jnp.zeros((HIDDEN_SIZE, CHANNELS), jnp.float32), (jnp.zeros((HIDDEN_SIZE,), jnp.float32), zeros_c, zeros_c, zeros_c, zeros_c))
    carry, (block_bands, d_bands) = lax.scan(one_band, init, (conv_bands, feat_bands, cot_bands))
    block_out = block_bands.reshape(HEIGHT, WIDTH, CHANNELS)
    convolution_gradient = d_bands.reshape(HEIGHT, WIDTH, CHANNELS)
    d_padded = jnp.pad(convolution_gradient, ((3, 3), (3, 3), (0, 0)))
    grad_features = (cotangent.astype(jnp.float32) + transposed(d_padded, dw_kernel, HEIGHT, WIDTH)).astype(jnp.bfloat16)
    factor = 1.0 / jnp.sqrt(jnp.float32(TOKENS))
    g_in_bias, g_out_bias, g_scale, g_gain, g_nbias = carry[2]
    kernel_rows = kernel_terms(padded, convolution_gradient, HEIGHT, WIDTH)
    bias_gradient = lax.optimization_barrier(jnp.sum(convolution_gradient.astype(jnp.float32), axis=(0, 1)))
    channel_rows = jnp.concatenate([kernel_rows, jnp.stack([bias_gradient, g_gain, g_nbias, g_out_bias, g_scale], axis=0)], axis=0)
    return (block_out, grad_features, carry[0] * factor, carry[1] * factor, channel_rows * factor, g_in_bias * factor)
```

```python
import math

import jax
import jax.numpy as jnp
from jax import lax
from jax.sharding import Mesh
from jax.sharding import PartitionSpec as P

CHIPS = ("z", "yh", "x", "yl")
EVERY = CHIPS + ("c",)
ROW = ("z", "yh")
COL = ("x", "yl", "c")


def with_halo(cells, sides, width):
    for axis, dim in sides:
        count = lax.axis_size(axis)
        ends = count - 1
        head = lax.slice_in_dim(cells, 0, width, axis=dim)
        tail = lax.slice_in_dim(cells, cells.shape[dim] - width, cells.shape[dim], axis=dim)
        cells = jnp.concatenate(
            [
                lax.ppermute(tail, axis, [(i, (i + 1) % count) for i in range(ends)]),
                cells,
                lax.ppermute(head, axis, [((i + 1) % count, i) for i in range(ends)]),
            ],
            axis=dim,
        )
    return cells


def gelu_plain(value):
    return 0.5 * value * (1.0 + jax.scipy.special.erf(value * 0.7071067811865476))


def gelu_slope(value):
    cumul = 0.5 * (1.0 + jax.scipy.special.erf(value * 0.7071067811865476))
    return cumul + value * jnp.exp(-0.5 * value * value) * 0.3989422804014327


def interior_rows(left, right):
    return lax.dot_general(
        left, right, (((0,), (0,)), ((), ())), preferred_element_type=jnp.float32
    )


def inner_cols(left, right):
    return lax.dot_general(
        left, right, (((1,), (1,)), ((), ())), preferred_element_type=jnp.float32
    )


def extend(field):
    return with_halo(field, ((ROW, 0), (COL, 1)), 3)


def kernel_entry(dw_kernel, index):
    return lax.dynamic_index_in_dim(dw_kernel, index, 0, keepdims=False)


def depthwise(padded, dw_kernel, dw_bias, height, width):

    def depthwise_step(row_tap, total):
        band = lax.dynamic_slice_in_dim(padded, row_tap, height, 0).astype(jnp.float32)
        for col_tap in range(7):
            total = total + band[:, col_tap : col_tap + width, :] * kernel_entry(
                dw_kernel, 7 * row_tap + col_tap
            )
        return total

    total = lax.fori_loop(
        0, 7, depthwise_step, jnp.zeros((height, width, padded.shape[2]), jnp.float32)
    )
    return total + dw_bias


def transposed(d_padded, dw_kernel, height, width):

    def transposed_step(row_tap, total):
        band = lax.dynamic_slice_in_dim(d_padded, 6 - row_tap, height, 0).astype(jnp.float32)
        for col_tap in range(7):
            total = total + band[:, 6 - col_tap : 6 - col_tap + width, :] * kernel_entry(
                dw_kernel, 7 * row_tap + col_tap
            )
        return total

    return lax.fori_loop(
        0, 7, transposed_step, jnp.zeros((height, width, d_padded.shape[2]), jnp.float32)
    )


def kernel_terms(padded, convolution_gradient, height, width):
    d_float = convolution_gradient.astype(jnp.float32)

    def kernel_step(row_tap, stacked):
        band = lax.dynamic_slice_in_dim(padded, row_tap, height, 0).astype(jnp.float32)
        seven = jnp.stack(
            [
                jnp.sum(band[:, col_tap : col_tap + width, :] * d_float, axis=(0, 1))
                for col_tap in range(7)
            ],
            axis=0,
        )
        return lax.dynamic_update_slice_in_dim(stacked, seven, 7 * row_tap, 0)

    return lax.fori_loop(0, 7, kernel_step, jnp.zeros((49, padded.shape[2]), jnp.float32))


def pointwise(
    conv_rows,
    feat_rows,
    cot_rows,
    norm_gain_vector,
    norm_bias,
    pw_in_weight,
    pw_in_bias,
    pw_out_weight,
    pw_out_bias,
    layer_scale,
):
    mean_c = jnp.mean(conv_rows, axis=-1, keepdims=True)
    centred = conv_rows - mean_c
    inverse_deviation = lax.rsqrt(jnp.mean(centred * centred, axis=-1, keepdims=True) + 1e-06)
    centered_input = centred * inverse_deviation
    normed = (centered_input * norm_gain_vector + norm_bias).astype(jnp.bfloat16)
    pre_act = jnp.dot(normed, pw_in_weight, preferred_element_type=jnp.float32) + pw_in_bias
    act = gelu_plain(pre_act).astype(jnp.bfloat16)
    branch = jnp.dot(act, pw_out_weight, preferred_element_type=jnp.float32) + pw_out_bias
    block_rows = (feat_rows.astype(jnp.float32) + layer_scale * branch).astype(jnp.bfloat16)
    cot_float = cot_rows.astype(jnp.float32)
    g_scale = jnp.sum(cot_float * branch, axis=0)
    d_branch = (cot_float * layer_scale).astype(jnp.bfloat16)
    g_out_bias = jnp.sum(d_branch.astype(jnp.float32), axis=0)
    d_act = inner_cols(d_branch, pw_out_weight)
    d_pre = (d_act * gelu_slope(pre_act)).astype(jnp.bfloat16)
    g_in_bias = jnp.sum(d_pre.astype(jnp.float32), axis=0)
    normalized_gradient = inner_cols(d_pre, pw_in_weight)
    g_gain = jnp.sum(normalized_gradient * centered_input, axis=0)
    g_nbias = jnp.sum(normalized_gradient, axis=0)
    centered_input_gradient = normalized_gradient * norm_gain_vector
    convolution_gradient = inverse_deviation * (
        centered_input_gradient
        - jnp.mean(centered_input_gradient, axis=-1, keepdims=True)
        - centered_input
        * jnp.mean(centered_input_gradient * centered_input, axis=-1, keepdims=True)
    )
    convolution_gradient = convolution_gradient.astype(jnp.bfloat16)
    return (
        block_rows,
        convolution_gradient,
        normed,
        act,
        d_branch,
        d_pre,
        (g_in_bias, g_out_bias, g_scale, g_gain, g_nbias),
    )


def shards(
    features,
    cotangent,
    dw_kernel,
    dw_bias,
    norm_gain_vector,
    norm_bias,
    pw_in_weight,
    pw_in_bias,
    pw_out_weight,
    pw_out_bias,
    layer_scale,
):
    tile_rows, tile_cols, channels = features.shape
    hidden = pw_in_weight.shape[1]
    count = tile_rows * tile_cols
    devices_all = lax.axis_size(EVERY)
    tokens = count * devices_all
    factor = 1.0 / math.sqrt(tokens)
    padded = extend(features)
    conv_out = depthwise(padded, dw_kernel, dw_bias, tile_rows, tile_cols)
    block_rows, convolution_gradient, normed, act, d_branch, d_pre, smalls = pointwise(
        conv_out.reshape(count, channels),
        features.reshape(count, channels),
        cotangent.reshape(count, channels),
        norm_gain_vector,
        norm_bias,
        pw_in_weight,
        pw_in_bias,
        pw_out_weight,
        pw_out_bias,
        layer_scale,
    )
    core = lax.axis_index("c")
    out_term = interior_rows(act, d_branch).reshape(64, 2, 16, channels)
    in_term = interior_rows(normed, d_pre).reshape(64, 2, 4, 4, channels)
    in_term = in_term.reshape(64, 2, 16, channels)
    both = jnp.concatenate([out_term, in_term], axis=2).astype(jnp.bfloat16)
    mine = lax.dynamic_index_in_dim(both, core, 1, keepdims=False)
    theirs = lax.dynamic_index_in_dim(both, 1 - core, 1, keepdims=False)
    met = lax.ppermute(theirs, "c", [(0, 1), (1, 0)])
    chip_sum = (mine.astype(jnp.float32) + met.astype(jnp.float32)).astype(jnp.bfloat16)
    spread = lax.all_to_all(chip_sum, CHIPS, 0, 0, tiled=True)
    summed = jnp.sum(spread.astype(jnp.float32), axis=0) * factor
    grad_out = summed[:16]
    grad_in = summed[16:].reshape(4, hidden)
    d_tile = convolution_gradient.reshape(tile_rows, tile_cols, channels)
    d_padded = extend(d_tile)
    grad_features = (
        cotangent.astype(jnp.float32) + transposed(d_padded, dw_kernel, tile_rows, tile_cols)
    ).astype(jnp.bfloat16)
    g_in_bias, g_out_bias, g_scale, g_gain, g_nbias = smalls
    kernel_rows = kernel_terms(padded, d_tile, tile_rows, tile_cols)
    bias_gradient = jnp.sum(d_tile.astype(jnp.float32), axis=(0, 1))
    channel_rows = (
        jnp.concatenate(
            [kernel_rows, jnp.stack([bias_gradient, g_gain, g_nbias, g_out_bias, g_scale], axis=0)],
            axis=0,
        )
        * factor
    )
    small = jnp.concatenate(
        [
            channel_rows.T.reshape(128, 4, 54),
            (g_in_bias * factor).reshape(128, 4, 4),
            jnp.zeros((128, 4, 70), jnp.float32),
        ],
        axis=2,
    )
    small = jnp.sum(lax.all_to_all(small, EVERY, 0, 0, tiled=True), axis=0)
    return (
        block_rows.reshape(tile_rows, tile_cols, channels),
        grad_features,
        grad_in,
        grad_out,
        small[:, :54].T,
        small[:, 54:58].reshape(-1),
    )


def solution(mesh):
    fine = Mesh(mesh.devices.reshape(4, 2, 4, 2, 2), EVERY)
    return jax.shard_map(
        shards,
        mesh=fine,
        in_specs=(P(ROW, COL, None), P(ROW, COL, None)) + (P(),) * 9,
        out_specs=(
            P(ROW, COL, None),
            P(ROW, COL, None),
            P(EVERY, None),
            P(EVERY, None),
            P(None, EVERY),
            P(EVERY),
        ),
        check_vma=False,
    )
```

```python
import math

import jax
import jax.numpy as jnp
from jax import lax
from jax.experimental import pallas as pl
from jax.experimental.pallas import tpu as pltpu
from jax.sharding import Mesh
from jax.sharding import PartitionSpec as P

CHIPS = ("z", "yh", "x", "yl")
EVERY = CHIPS + ("c",)
ROW = ("z", "yh")
COL = ("x", "yl", "c")
ROWS, COLS, CH, HID, CHUNK = 8, 32, 512, 2048, 512
COUNT = ROWS * COLS
STEPS = HID // CHUNK
PAD = (ROWS + 6, COLS + 8, CH)
F32, BF16 = jnp.float32, jnp.bfloat16
VMEM_BYTES = 40 * 1024 * 1024


def dot_nn(left, right):
    return lax.dot_general(left, right, (((1,), (0,)), ((), ())), preferred_element_type=F32)


def dot_nt(left, right):
    return lax.dot_general(left, right, (((1,), (1,)), ((), ())), preferred_element_type=F32)


def dot_tn(left, right):
    return lax.dot_general(left, right, (((0,), (0,)), ((), ())), preferred_element_type=F32)


def assemble(pad, tile, top, bottom, left, right):
    pad[0:3, 3 : 3 + COLS, :] = top[...].astype(F32)
    pad[3 : 3 + ROWS, 3 : 3 + COLS, :] = tile[...].astype(F32)
    pad[3 + ROWS : 6 + ROWS, 3 : 3 + COLS, :] = bottom[...].astype(F32)
    pad[:, 0:3, :] = left[...].astype(F32)
    pad[:, 3 + COLS : 6 + COLS, :] = right[...].astype(F32)


def lanes_of(block):
    return pl.ds(pl.multiple_of(block * 128, 128), 128)


def depthwise(pad, taps, finish, flip):
    def block(cb, carry):
        lanes = lanes_of(cb)
        totals = [jnp.zeros((ROWS, 8, 128), F32) for _ in range(COLS // 8)]
        for s in range(7):
            weights = []
            for r in range(7):
                tap = 7 * (6 - r) + 6 - s if flip else 7 * r + s
                weights.append(taps[tap : tap + 1, lanes].reshape(1, 1, 128))
            for cg in range(COLS // 8):
                band = pad[:, 8 * cg + s : 8 * cg + s + 8, lanes]
                for r in range(7):
                    totals[cg] = totals[cg] + band[r : r + ROWS] * weights[r]
        for cg in range(COLS // 8):
            finish(cg, lanes, totals[cg])
        return carry

    lax.fori_loop(0, CH // 128, block, 0)


def grads_kernel(
    core_ref, tile, top, bottom, left, right, cot, taps, dw_bias, gain, shift, scale,
    w_in, b_in, w_out,
    pad, x_hat, rstd, act_out, d_pre_out, g_in_bias, mine, theirs,
    conv, normed, d_branch, g_in,
):
    step = pl.program_id(0)
    core = core_ref[0]

    @pl.when(step == 0)
    def _():
        assemble(pad, tile, top, bottom, left, right)

        def finish(cg, lanes, total):
            conv[:, 8 * cg : 8 * cg + 8, lanes] = total

        depthwise(pad, taps, finish, False)
        rows = conv[...].reshape(COUNT, CH) + dw_bias[...]
        centred = rows - jnp.mean(rows, axis=-1, keepdims=True)
        inverse = lax.rsqrt(jnp.mean(centred * centred, axis=-1, keepdims=True) + 1e-06)
        hat = centred * inverse
        x_hat[...] = hat
        rstd[...] = inverse
        normed[...] = (hat * gain[...] + shift[...]).astype(BF16)
        d_branch[...] = (cot[...].astype(F32) * scale[...]).astype(BF16)

    pre_act = dot_nn(normed[...], w_in[...]) + b_in[...]
    cumul = 0.5 * (1.0 + lax.erf(pre_act * 0.7071067811865476))
    act = (pre_act * cumul).astype(BF16)
    slope = cumul + pre_act * jnp.exp(-0.5 * pre_act * pre_act) * 0.3989422804014327
    d_pre = (dot_nt(d_branch[...], w_out[...]) * slope).astype(BF16)
    act_out[...] = act
    d_pre_out[...] = d_pre
    g_in_bias[...] = jnp.sum(d_pre.astype(F32), axis=0, keepdims=True)
    term = dot_tn(act, d_branch[...]).reshape(CHUNK // 32, 2, 16, CH)
    chips = pl.ds(step * (CHUNK // 32), CHUNK // 32)
    first = core == 0
    mine[chips, 0:16, :] = jnp.where(first, term[:, 0], term[:, 1]).astype(BF16)
    theirs[chips, 0:16, :] = jnp.where(first, term[:, 1], term[:, 0]).astype(BF16)
    g_in[step] = dot_tn(normed[...], d_pre)

    @pl.when(step == STEPS - 1)
    def _():
        upper = lax.broadcasted_iota(jnp.int32, (8, 8, CHUNK), 1) < 4

        def group(g, carry):
            rows = pl.ds(pl.multiple_of(g * 64, 64), 64)
            kept, given = [], []
            for u in range(2):
                low = g_in[2 * u, rows, :].reshape(8, 8, CHUNK)
                high = g_in[2 * u + 1, rows, :].reshape(8, 8, CHUNK)
                low_turned, high_turned = pltpu.roll(low, 4, 1), pltpu.roll(high, 4, 1)
                zero = jnp.where(upper, low, high_turned)
                one = jnp.where(upper, low_turned, high)
                kept.append(jnp.where(first, zero, one))
                given.append(jnp.where(first, one, zero))
            at = pl.ds(pl.multiple_of(g * 8, 8), 8)
            mine[at, 16:32, :] = jnp.concatenate(kept, axis=1).astype(BF16)
            theirs[at, 16:32, :] = jnp.concatenate(given, axis=1).astype(BF16)
            return carry

        lax.fori_loop(0, 8, group, 0)


def whole(shape):
    return pl.BlockSpec(shape, lambda *_: (0,) * len(shape))


def grads(core, tile, top, bottom, left, right, cot, taps, dw_bias, gain, shift, scale, w_in, b_in, w_out):
    message = (64, 32, CH)
    return pl.pallas_call(
        grads_kernel,
        grid=(STEPS,),
        in_specs=[
            pl.BlockSpec(memory_space=pltpu.SMEM),
            whole((ROWS, COLS, CH)),
            whole((3, COLS, CH)),
            whole((3, COLS, CH)),
            whole((ROWS + 6, 3, CH)),
            whole((ROWS + 6, 3, CH)),
            whole((COUNT, CH)),
            whole((49, CH)),
            whole((1, CH)),
            whole((1, CH)),
            whole((1, CH)),
            whole((1, CH)),
            pl.BlockSpec((CH, CHUNK), lambda t: (0, t)),
            pl.BlockSpec((1, CHUNK), lambda t: (0, t)),
            pl.BlockSpec((CHUNK, CH), lambda t: (t, 0)),
        ],
        out_specs=[
            whole(PAD),
            whole((COUNT, CH)),
            whole((COUNT, 1)),
            pl.BlockSpec((COUNT, CHUNK), lambda t: (0, t)),
            pl.BlockSpec((COUNT, CHUNK), lambda t: (0, t)),
            pl.BlockSpec((1, CHUNK), lambda t: (0, t)),
            whole(message),
            whole(message),
        ],
        out_shape=[
            jax.ShapeDtypeStruct(PAD, F32),
            jax.ShapeDtypeStruct((COUNT, CH), F32),
            jax.ShapeDtypeStruct((COUNT, 1), F32),
            jax.ShapeDtypeStruct((COUNT, HID), BF16),
            jax.ShapeDtypeStruct((COUNT, HID), BF16),
            jax.ShapeDtypeStruct((1, HID), F32),
            jax.ShapeDtypeStruct(message, BF16),
            jax.ShapeDtypeStruct(message, BF16),
        ],
        scratch_shapes=[
            pltpu.VMEM((ROWS, COLS, CH), F32),
            pltpu.VMEM((COUNT, CH), BF16),
            pltpu.VMEM((COUNT, CH), BF16),
            pltpu.VMEM((STEPS, CH, CHUNK), F32),
        ],
        compiler_params=pltpu.CompilerParams(vmem_limit_bytes=VMEM_BYTES),
        cost_estimate=pl.CostEstimate(flops=2_200_000_000, bytes_accessed=12_000_000, transcendentals=1_000_000),
        name="grads",
    )(core, tile, top, bottom, left, right, cot, taps, dw_bias, gain, shift, scale, w_in, b_in, w_out)


def norm_kernel(d_pre, w_in, x_hat, rstd, gain, pad, cot, scale, d_conv, rows_out, d_tile):
    d_normed = dot_nt(d_pre[...], w_in[...])
    hat = x_hat[...]
    rows_out[50:51, :] = jnp.sum(d_normed * hat, axis=0, keepdims=True)
    rows_out[51:52, :] = jnp.sum(d_normed, axis=0, keepdims=True)
    d_branch = (cot[...].astype(F32) * scale[...]).astype(BF16)
    rows_out[52:53, :] = jnp.sum(d_branch.astype(F32), axis=0, keepdims=True)
    d_hat = d_normed * gain[...]
    grad = rstd[...] * (
        d_hat
        - jnp.mean(d_hat, axis=-1, keepdims=True)
        - hat * jnp.mean(d_hat * hat, axis=-1, keepdims=True)
    )
    grad = grad.astype(BF16)
    d_conv[...] = grad.reshape(ROWS, COLS, CH)
    wide = grad.astype(F32)
    rows_out[49:50, :] = jnp.sum(wide, axis=0, keepdims=True)
    rows_out[53:56, :] = jnp.zeros((3, CH), F32)
    d_tile[...] = wide.reshape(ROWS, COLS, CH)

    def block(cb, carry):
        lanes = lanes_of(cb)
        for s in range(7):
            totals = [jnp.zeros((8, 128), F32) for _ in range(7)]
            for cg in range(COLS // 8):
                band = pad[:, 8 * cg + s : 8 * cg + s + 8, lanes]
                own = d_tile[:, 8 * cg : 8 * cg + 8, lanes]
                for r in range(7):
                    totals[r] = totals[r] + jnp.sum(band[r : r + ROWS] * own, axis=0)
            for r in range(7):
                rows_out[7 * r + s : 7 * r + s + 1, lanes] = jnp.sum(totals[r], axis=0, keepdims=True)
        return carry

    lax.fori_loop(0, CH // 128, block, 0)


def norm_back(d_pre, w_in, x_hat, rstd, gain, pad, cot, scale):
    return pl.pallas_call(
        norm_kernel,
        out_shape=[
            jax.ShapeDtypeStruct((ROWS, COLS, CH), BF16),
            jax.ShapeDtypeStruct((56, CH), F32),
        ],
        scratch_shapes=[pltpu.VMEM((ROWS, COLS, CH), F32)],
        compiler_params=pltpu.CompilerParams(vmem_limit_bytes=VMEM_BYTES),
        cost_estimate=pl.CostEstimate(flops=600_000_000, bytes_accessed=8_000_000, transcendentals=0),
        name="norm_back",
    )(d_pre, w_in, x_hat, rstd, gain, pad, cot, scale)


def branch_kernel(act, w_out, b_out, tile, cot, scale, block_out, g_scale):
    branch = dot_nn(act[...], w_out[...]) + b_out[...]
    block_out[...] = (tile[...].astype(F32) + scale[...] * branch).astype(BF16)
    g_scale[...] = jnp.sum(cot[...].astype(F32) * branch, axis=0, keepdims=True)


def branch_part(act, w_out, b_out, tile, cot, scale):
    return pl.pallas_call(
        branch_kernel,
        out_shape=[
            jax.ShapeDtypeStruct((COUNT, CH), BF16),
            jax.ShapeDtypeStruct((1, CH), F32),
        ],
        compiler_params=pltpu.CompilerParams(vmem_limit_bytes=VMEM_BYTES),
        cost_estimate=pl.CostEstimate(flops=540_000_000, bytes_accessed=4_000_000, transcendentals=0),
        name="branch_part",
    )(act, w_out, b_out, tile, cot, scale)


def features_kernel(d_conv, top, bottom, left, right, cot, taps, out, pad):
    assemble(pad, d_conv, top, bottom, left, right)

    def finish(cg, lanes, total):
        columns = slice(8 * cg, 8 * cg + 8)
        pad[0:ROWS, columns, lanes] = total

    depthwise(pad, taps, finish, True)
    out[...] = (cot[...].astype(F32) + pad[0:ROWS, 0:COLS, :]).astype(BF16)


def features_part(d_conv, top, bottom, left, right, cot, taps):
    return pl.pallas_call(
        features_kernel,
        out_shape=jax.ShapeDtypeStruct((ROWS, COLS, CH), BF16),
        scratch_shapes=[pltpu.VMEM(PAD, F32)],
        compiler_params=pltpu.CompilerParams(vmem_limit_bytes=VMEM_BYTES),
        cost_estimate=pl.CostEstimate(flops=30_000_000, bytes_accessed=2_000_000, transcendentals=0),
        name="features_part",
    )(d_conv, top, bottom, left, right, cot, taps)


def shift_by(value, axis, way):
    count = lax.axis_size(axis)
    pairs = [(i, i + way) for i in range(count) if 0 <= i + way < count]
    return lax.ppermute(value, axis, pairs)


def halo(tile):
    top = shift_by(tile[ROWS - 3 :], ROW, 1)
    bottom = shift_by(tile[:3], ROW, -1)
    tail = [part[:, COLS - 3 :] for part in (top, tile, bottom)]
    head = [part[:, :3] for part in (top, tile, bottom)]
    left = shift_by(jnp.concatenate(tail, axis=0), COL, 1)
    right = shift_by(jnp.concatenate(head, axis=0), COL, -1)
    return top, bottom, left, right


def shards(
    features, cotangent, dw_kernel, dw_bias, norm_gain_vector, norm_bias,
    pw_in_weight, pw_in_bias, pw_out_weight, pw_out_bias, layer_scale,
):
    factor = 1.0 / math.sqrt(COUNT * lax.axis_size(EVERY))
    core = lax.axis_index("c").astype(jnp.int32).reshape(1)
    row = lambda vector: vector.reshape(1, -1)
    gain, scale = row(norm_gain_vector), row(layer_scale)
    flat_cot = cotangent.reshape(COUNT, CH)
    pad, x_hat, rstd, act, d_pre, g_in_bias, mine, theirs = grads(
        core, features, *halo(features), flat_cot, dw_kernel, row(dw_bias), gain, row(norm_bias), scale,
        pw_in_weight, row(pw_in_bias), pw_out_weight,
    )
    met = lax.ppermute(theirs, "c", [(0, 1), (1, 0)])
    d_conv, rows = norm_back(d_pre, pw_in_weight, x_hat, rstd, gain, pad, flat_cot, scale)
    chip_sum = (mine.astype(F32) + met.astype(F32)).astype(BF16)
    spread = lax.all_to_all(chip_sum, CHIPS, 0, 0, tiled=True)
    block_rows, g_scale = branch_part(
        act, pw_out_weight, row(pw_out_bias), features.reshape(COUNT, CH), flat_cot, scale
    )
    grad_features = features_part(d_conv, *halo(d_conv), cotangent, dw_kernel)
    channel_rows = jnp.concatenate([rows[:53], g_scale], axis=0) * factor
    small = jnp.concatenate(
        [
            channel_rows.T.reshape(128, 4, 54),
            (g_in_bias * factor).reshape(128, 4, 4),
            jnp.zeros((128, 4, 70), F32),
        ],
        axis=2,
    )
    small = jnp.sum(lax.all_to_all(small, EVERY, 0, 0, tiled=True), axis=0)
    summed = jnp.sum(spread.astype(F32), axis=0) * factor
    return (
        block_rows.reshape(ROWS, COLS, CH),
        grad_features,
        summed[16:].reshape(2, 2, 4, CH).transpose(2, 0, 1, 3).reshape(4, HID),
        summed[:16],
        small[:, :54].T,
        small[:, 54:58].reshape(-1),
    )


def solution(mesh):
    fine = Mesh(mesh.devices.reshape(4, 2, 4, 2, 2), EVERY)
    return jax.shard_map(
        shards,
        mesh=fine,
        in_specs=(P(ROW, COL, None), P(ROW, COL, None)) + (P(),) * 9,
        out_specs=(
            P(ROW, COL, None),
            P(ROW, COL, None),
            P(EVERY, None),
            P(EVERY, None),
            P(None, EVERY),
            P(EVERY),
        ),
        check_vma=False,
    )
```

```python
import math

import jax
import jax.numpy as jnp
from jax import lax
from jax.experimental import pallas as pl
from jax.experimental.pallas import tpu as pltpu
from jax.sharding import Mesh
from jax.sharding import PartitionSpec as P

CHIPS = ("z", "yh", "x", "yl")
EVERY = CHIPS + ("c",)
ROW = ("z", "yh")
COL = ("x", "yl", "c")
ROWS, COLS, CH, HID, CHUNK = 8, 32, 512, 2048, 512
COUNT = ROWS * COLS
STEPS = HID // CHUNK
PAD = (ROWS + 6, COLS + 8, CH)
F32, BF16 = jnp.float32, jnp.bfloat16
VMEM_BYTES = 60 * 1024 * 1024


def dot_nn(left, right):
    return lax.dot_general(left, right, (((1,), (0,)), ((), ())), preferred_element_type=F32)


def dot_nt(left, right):
    return lax.dot_general(left, right, (((1,), (1,)), ((), ())), preferred_element_type=F32)


def dot_tn(left, right):
    return lax.dot_general(left, right, (((0,), (0,)), ((), ())), preferred_element_type=F32)


def assemble(pad, tile, top, bottom, left, right):
    pad[0:3, 3 : 3 + COLS, :] = top[...].astype(F32)
    pad[3 : 3 + ROWS, 3 : 3 + COLS, :] = tile[...].astype(F32)
    pad[3 + ROWS : 6 + ROWS, 3 : 3 + COLS, :] = bottom[...].astype(F32)
    pad[:, 0:3, :] = left[...].astype(F32)
    pad[:, 3 + COLS : 6 + COLS, :] = right[...].astype(F32)


def lanes_of(block):
    return pl.ds(pl.multiple_of(block * 128, 128), 128)


def depthwise(pad, taps, finish, flip):
    def block(cb, carry):
        lanes = lanes_of(cb)
        totals = [jnp.zeros((ROWS, 8, 128), F32) for _ in range(COLS // 8)]
        for s in range(7):
            weights = []
            for r in range(7):
                tap = 7 * (6 - r) + 6 - s if flip else 7 * r + s
                weights.append(taps[tap : tap + 1, lanes].reshape(1, 1, 128))
            for cg in range(COLS // 8):
                band = pad[:, 8 * cg + s : 8 * cg + s + 8, lanes]
                for r in range(7):
                    totals[cg] = totals[cg] + band[r : r + ROWS] * weights[r]
        for cg in range(COLS // 8):
            finish(cg, lanes, totals[cg])
        return carry

    lax.fori_loop(0, CH // 128, block, 0)


def grads_kernel(
    core_ref, tile, top, bottom, left, right, cot, taps, dw_bias, gain, shift, scale, b_out,
    w_in, b_in, w_out,
    pad, block_out, d_conv, d_first, d_last, rows_out, bias_out, mine_out, theirs_out, mine_in, theirs_in,
    conv, x_hat, rstd, normed, d_branch, branch, d_normed,
):
    step = pl.program_id(0)
    first = core_ref[0] == 0

    @pl.when(step == 0)
    def _():
        assemble(pad, tile, top, bottom, left, right)

        def finish(cg, lanes, total):
            conv[:, 8 * cg : 8 * cg + 8, lanes] = total

        depthwise(pad, taps, finish, False)
        rows = conv[...].reshape(COUNT, CH) + dw_bias[...]
        centred = rows - jnp.mean(rows, axis=-1, keepdims=True)
        inverse = lax.rsqrt(jnp.mean(centred * centred, axis=-1, keepdims=True) + 1e-06)
        hat = centred * inverse
        x_hat[...] = hat
        rstd[...] = inverse
        normed[...] = (hat * gain[...] + shift[...]).astype(BF16)
        d_branch[...] = (cot[...].astype(F32) * scale[...]).astype(BF16)
        branch[...] = jnp.broadcast_to(b_out[...], (COUNT, CH))
        d_normed[...] = jnp.zeros((COUNT, CH), F32)

    pre_act = dot_nn(normed[...], w_in[...]) + b_in[...]
    cumul = 0.5 * (1.0 + lax.erf(pre_act * 0.7071067811865476))
    act = (pre_act * cumul).astype(BF16)
    slope = cumul + pre_act * jnp.exp(-0.5 * pre_act * pre_act) * 0.3989422804014327
    d_pre = (dot_nt(d_branch[...], w_out[...]) * slope).astype(BF16)
    branch[...] += dot_nn(act, w_out[...])
    d_normed[...] += dot_nt(d_pre, w_in[...])

    bias = jnp.sum(d_pre.astype(F32), axis=0, keepdims=True)
    fourth = lax.broadcasted_iota(jnp.int32, (8, CHUNK), 1) % 4
    spaced = jnp.where(fourth == lax.broadcasted_iota(jnp.int32, (8, CHUNK), 0), bias, 0.0).astype(BF16)
    source = lax.broadcasted_iota(jnp.int32, (CHUNK, 128), 0) // 4
    pick = (source == lax.broadcasted_iota(jnp.int32, (CHUNK, 128), 1)).astype(F32).astype(BF16)
    bias_out[...] = dot_nn(spaced, pick)

    term = dot_tn(act, d_branch[...]).reshape(CHUNK // 32, 2, 16, CH)

    def by_lanes(part):
        return jnp.concatenate([part[:, :, 128 * k : 128 * k + 128] for k in range(4)], axis=1)

    mine_out[...] = by_lanes(jnp.where(first, term[:, 0], term[:, 1])).astype(BF16)
    theirs_out[...] = by_lanes(jnp.where(first, term[:, 1], term[:, 0])).astype(BF16)

    term = dot_tn(normed[...], d_pre).reshape(64, 8, CHUNK)
    upper = lax.broadcasted_iota(jnp.int32, (64, 8, 128), 1) < 4
    kept, given = [], []
    for k in range(2):
        low = term[:, :, 128 * k : 128 * k + 128]
        high = term[:, :, 256 + 128 * k : 384 + 128 * k]
        zero = jnp.where(upper, low, pltpu.roll(high, 4, 1))
        one = jnp.where(upper, pltpu.roll(low, 4, 1), high)
        kept.append(jnp.where(first, zero, one))
        given.append(jnp.where(first, one, zero))
    mine_in[...] = jnp.concatenate(kept, axis=1).astype(BF16)
    theirs_in[...] = jnp.concatenate(given, axis=1).astype(BF16)

    @pl.when(step == STEPS - 1)
    def _():
        hat = x_hat[...]
        d_norm = d_normed[...]
        d_hat = d_norm * gain[...]
        grad = rstd[...] * (
            d_hat
            - jnp.mean(d_hat, axis=-1, keepdims=True)
            - hat * jnp.mean(d_hat * hat, axis=-1, keepdims=True)
        )
        grad = grad.astype(BF16)
        out = grad.reshape(ROWS, COLS, CH)
        d_conv[...] = out
        d_first[...] = out[:3]
        d_last[...] = out[ROWS - 3 :]
        whole_branch = branch[...]
        block_out[...] = (tile[...].reshape(COUNT, CH).astype(F32) + scale[...] * whole_branch).astype(BF16)
        rows_out[0:1, :] = jnp.sum(grad.astype(F32), axis=0, keepdims=True)
        rows_out[1:2, :] = jnp.sum(d_norm * hat, axis=0, keepdims=True)
        rows_out[2:3, :] = jnp.sum(d_norm, axis=0, keepdims=True)
        rows_out[3:4, :] = jnp.sum(d_branch[...].astype(F32), axis=0, keepdims=True)
        rows_out[4:5, :] = jnp.sum(cot[...].astype(F32) * whole_branch, axis=0, keepdims=True)


def whole(shape):
    return pl.BlockSpec(shape, lambda *_: (0,) * len(shape))


def grads(*operands):
    vector = whole((1, CH))
    half = (64, 64, 128)
    by_chip = pl.BlockSpec((CHUNK // 32, 64, 128), lambda t: (t, 0, 0))
    by_row = pl.BlockSpec((64, 16, 128), lambda t: (0, t, 0))
    shape = jax.ShapeDtypeStruct
    return pl.pallas_call(
        grads_kernel,
        grid=(STEPS,),
        in_specs=[
            pl.BlockSpec(memory_space=pltpu.SMEM),
            whole((ROWS, COLS, CH)),
            whole((3, COLS, CH)),
            whole((3, COLS, CH)),
            whole((ROWS + 6, 3, CH)),
            whole((ROWS + 6, 3, CH)),
            whole((COUNT, CH)),
            whole((49, CH)),
            vector,
            vector,
            vector,
            vector,
            vector,
            pl.BlockSpec((CH, CHUNK), lambda t: (0, t)),
            pl.BlockSpec((1, CHUNK), lambda t: (0, t)),
            pl.BlockSpec((CHUNK, CH), lambda t: (t, 0)),
        ],
        out_specs=[
            whole(PAD),
            whole((COUNT, CH)),
            whole((ROWS, COLS, CH)),
            whole((3, COLS, CH)),
            whole((3, COLS, CH)),
            whole((8, CH)),
            pl.BlockSpec((8, 128), lambda t: (0, t)),
            by_chip,
            by_chip,
            by_row,
            by_row,
        ],
        out_shape=[
            shape(PAD, F32),
            shape((COUNT, CH), BF16),
            shape((ROWS, COLS, CH), BF16),
            shape((3, COLS, CH), BF16),
            shape((3, COLS, CH), BF16),
            shape((8, CH), F32),
            shape((8, CH), F32),
            shape(half, BF16),
            shape(half, BF16),
            shape(half, BF16),
            shape(half, BF16),
        ],
        scratch_shapes=[
            pltpu.VMEM((ROWS, COLS, CH), F32),
            pltpu.VMEM((COUNT, CH), F32),
            pltpu.VMEM((COUNT, 1), F32),
            pltpu.VMEM((COUNT, CH), BF16),
            pltpu.VMEM((COUNT, CH), BF16),
            pltpu.VMEM((COUNT, CH), F32),
            pltpu.VMEM((COUNT, CH), F32),
        ],
        compiler_params=pltpu.CompilerParams(vmem_limit_bytes=VMEM_BYTES),
        cost_estimate=pl.CostEstimate(flops=3_200_000_000, bytes_accessed=12_000_000, transcendentals=1_000_000),
        name="grads",
    )(*operands)


def taps_kernel(pad, d_conv, rows, bias, turned, d_tile, table):
    d_tile[...] = d_conv[...].astype(F32)
    table[48:128, :] = jnp.zeros((80, CH), F32)

    def block(cb, carry):
        lanes = lanes_of(cb)
        for s in range(7):
            totals = [jnp.zeros((8, 128), F32) for _ in range(7)]
            for cg in range(COLS // 8):
                band = pad[:, 8 * cg + s : 8 * cg + s + 8, lanes]
                own = d_tile[:, 8 * cg : 8 * cg + 8, lanes]
                for r in range(7):
                    totals[r] = totals[r] + jnp.sum(band[r : r + ROWS] * own, axis=0)
            for r in range(7):
                table[7 * r + s : 7 * r + s + 1, lanes] = jnp.sum(totals[r], axis=0, keepdims=True)
        return carry

    lax.fori_loop(0, CH // 128, block, 0)
    table[49:54, :] = rows[0:5, :]
    table[54:58, :] = bias[0:4, :]
    turned[...] = table[...].T.reshape(64, 8, 128)


def tap_rows(pad, d_conv, rows, bias):
    return pl.pallas_call(
        taps_kernel,
        out_shape=jax.ShapeDtypeStruct((64, 8, 128), F32),
        scratch_shapes=[pltpu.VMEM((ROWS, COLS, CH), F32), pltpu.VMEM((128, CH), F32)],
        compiler_params=pltpu.CompilerParams(vmem_limit_bytes=VMEM_BYTES),
        cost_estimate=pl.CostEstimate(flops=30_000_000, bytes_accessed=2_000_000, transcendentals=0),
        name="tap_rows",
    )(pad, d_conv, rows, bias)


def add_kernel(out_one, out_two, in_one, in_two, small_one, small_two, total):
    add = lambda one, two: (one[...].astype(F32) + two[...].astype(F32)).astype(BF16)
    total[:, 0:64, :] = add(out_one, out_two)
    total[:, 64:128, :] = add(in_one, in_two)
    total[:, 128:136, :] = add(small_one, small_two)


def add_pair(*operands):
    half = pl.BlockSpec((16, 64, 128), lambda t: (t, 0, 0))
    small = pl.BlockSpec((16, 8, 128), lambda t: (t, 0, 0))
    return pl.pallas_call(
        add_kernel,
        grid=(4,),
        in_specs=[half, half, half, half, small, small],
        out_specs=pl.BlockSpec((16, 136, 128), lambda t: (t, 0, 0)),
        out_shape=jax.ShapeDtypeStruct((64, 136, 128), BF16),
        compiler_params=pltpu.CompilerParams(vmem_limit_bytes=VMEM_BYTES),
        cost_estimate=pl.CostEstimate(flops=1_000_000, bytes_accessed=6_000_000, transcendentals=0),
        name="add_pair",
    )(*operands)


def sum_kernel(factor, core_ref, spread, g_in, g_out, g_channel, g_bias, total):
    step = pl.program_id(0)
    part = jnp.sum(spread[...].astype(F32), axis=0)

    @pl.when(step == 0)
    def _():
        total[...] = part

    @pl.when(step > 0)
    def _():
        total[...] += part

    @pl.when(step == pl.num_programs(0) - 1)
    def _():
        for k in range(4):
            g_out[:, 128 * k : 128 * k + 128] = total[16 * k : 16 * k + 16, :] * factor
        for t in range(STEPS):
            for k in range(2):
                own = total[64 + 16 * t + 8 * k : 72 + 16 * t + 8 * k, :] * factor
                at = CHUNK * t + 128 * k
                g_in[:, at : at + 128] = own[0:4]
                g_in[:, at + 256 : at + 384] = own[4:8]
        small = total[128:136, :] * factor
        small = jnp.where(core_ref[0] == 0, small, pltpu.roll(small, 4, 0))
        g_channel[...] = small.T[:54, :4]
        g_bias[...] = small[0:4, 54:58]


def sum_chips(core, spread, factor):
    shape = jax.ShapeDtypeStruct
    return pl.pallas_call(
        lambda *refs: sum_kernel(factor, *refs),
        grid=(4,),
        in_specs=[pl.BlockSpec(memory_space=pltpu.SMEM), pl.BlockSpec((16, 136, 128), lambda t: (t, 0, 0))],
        out_specs=[whole((4, HID)), whole((16, CH)), whole((54, 4)), whole((4, 4))],
        out_shape=[shape((4, HID), F32), shape((16, CH), F32), shape((54, 4), F32), shape((4, 4), F32)],
        scratch_shapes=[pltpu.VMEM((136, 128), F32)],
        compiler_params=pltpu.CompilerParams(vmem_limit_bytes=VMEM_BYTES),
        cost_estimate=pl.CostEstimate(flops=1_000_000, bytes_accessed=2_000_000, transcendentals=0),
        name="sum_chips",
    )(core, spread)


def features_kernel(d_conv, top, bottom, left, right, cot, taps, out, pad):
    assemble(pad, d_conv, top, bottom, left, right)

    def finish(cg, lanes, total):
        columns = slice(8 * cg, 8 * cg + 8)
        pad[0:ROWS, columns, lanes] = total

    depthwise(pad, taps, finish, True)
    out[...] = (cot[...].astype(F32) + pad[0:ROWS, 0:COLS, :]).astype(BF16)


def features_part(d_conv, top, bottom, left, right, cot, taps):
    return pl.pallas_call(
        features_kernel,
        out_shape=jax.ShapeDtypeStruct((ROWS, COLS, CH), BF16),
        scratch_shapes=[pltpu.VMEM(PAD, F32)],
        compiler_params=pltpu.CompilerParams(vmem_limit_bytes=VMEM_BYTES),
        cost_estimate=pl.CostEstimate(flops=30_000_000, bytes_accessed=2_000_000, transcendentals=0),
        name="features_part",
    )(d_conv, top, bottom, left, right, cot, taps)


def shift_by(value, axis, way):
    count = lax.axis_size(axis)
    pairs = [(i, i + way) for i in range(count) if 0 <= i + way < count]
    return lax.ppermute(value, axis, pairs)


def halo_rows(first, last):
    return shift_by(last, ROW, 1), shift_by(first, ROW, -1)


def halo_sides(top, tile, bottom):
    tail = [part[:, COLS - 3 :] for part in (top, tile, bottom)]
    head = [part[:, :3] for part in (top, tile, bottom)]
    return jnp.concatenate(tail, axis=0), jnp.concatenate(head, axis=0)


def halo_cols(tail, head):
    return shift_by(tail, COL, 1), shift_by(head, COL, -1)


def swap(value):
    return lax.ppermute(value, "c", [(0, 1), (1, 0)])


def shards(
    features, cotangent, dw_kernel, dw_bias, norm_gain_vector, norm_bias,
    pw_in_weight, pw_in_bias, pw_out_weight, pw_out_bias, layer_scale,
):
    factor = 1.0 / math.sqrt(COUNT * lax.axis_size(EVERY))
    core = lax.axis_index("c").astype(jnp.int32).reshape(1)
    row = lambda vector: vector.reshape(1, -1)
    top, bottom = halo_rows(features[:3], features[ROWS - 3 :])
    left, right = halo_cols(*halo_sides(top, features, bottom))
    pad, block_rows, d_conv, d_first, d_last, rows, bias, mine_out, theirs_out, mine_in, theirs_in = grads(
        core, features, top, bottom, left, right, cotangent.reshape(COUNT, CH), dw_kernel, row(dw_bias),
        row(norm_gain_vector), row(norm_bias), row(layer_scale), row(pw_out_bias),
        pw_in_weight, row(pw_in_bias), pw_out_weight,
    )
    met_out, met_in = swap(theirs_out), swap(theirs_in)
    d_top, d_bottom = halo_rows(d_first, d_last)
    small = tap_rows(pad, d_conv, rows, bias)
    met_small = swap(small)
    tail, head = halo_sides(d_top, d_conv, d_bottom)
    message = add_pair(mine_out, met_out, mine_in, met_in, small, met_small)
    message, tail, head = lax.optimization_barrier((message, tail, head))
    spread = lax.all_to_all(message, CHIPS, 0, 0, tiled=True)
    d_left, d_right = halo_cols(tail, head)
    grad_features = features_part(d_conv, d_top, d_bottom, d_left, d_right, cotangent, dw_kernel)
    grad_in, grad_out, grad_channel, grad_bias = sum_chips(core, spread, factor)
    return (
        block_rows.reshape(ROWS, COLS, CH),
        grad_features,
        grad_in,
        grad_out,
        grad_channel,
        grad_bias.reshape(-1),
    )


def solution(mesh):
    fine = Mesh(mesh.devices.reshape(4, 2, 4, 2, 2), EVERY)
    return jax.shard_map(
        shards,
        mesh=fine,
        in_specs=(P(ROW, COL, None), P(ROW, COL, None)) + (P(),) * 9,
        out_specs=(
            P(ROW, COL, None),
            P(ROW, COL, None),
            P(EVERY, None),
            P(EVERY, None),
            P(None, EVERY),
            P(EVERY),
        ),
        check_vma=False,
    )
```

```python
import math

import jax
import jax.numpy as jnp
from jax import lax
from jax.experimental import pallas as pl
from jax.experimental.pallas import tpu as pltpu
from jax.sharding import Mesh
from jax.sharding import PartitionSpec as P

EVERY = ("z", "yh", "xh", "xl", "yl", "c")
ROW = ("z", "yh")
COL = ("xh", "xl", "yl", "c")
GROUP = ("z", "yh", "xh", "yl")
ROWS, COLS, CH, HID, CHUNK = 8, 32, 512, 2048, 512
COUNT = ROWS * COLS
STEPS = HID // CHUNK
PAD = (ROWS + 6, COLS + 8, CH)
F32, BF16 = jnp.float32, jnp.bfloat16
VMEM_BYTES = 60 * 1024 * 1024


def dot_nn(left, right):
    return lax.dot_general(left, right, (((1,), (0,)), ((), ())), preferred_element_type=F32)


def dot_nt(left, right):
    return lax.dot_general(left, right, (((1,), (1,)), ((), ())), preferred_element_type=F32)


def dot_tn(left, right):
    return lax.dot_general(left, right, (((0,), (0,)), ((), ())), preferred_element_type=F32)


def assemble(pad, tile, row_one, row_two, col_one, col_two, even_row, even_col):
    rows = row_one[...].astype(F32), row_two[...].astype(F32)
    cols = col_one[...].astype(F32), col_two[...].astype(F32)
    pad[0:3, 3 : 3 + COLS, :] = jnp.where(even_row, rows[1], rows[0])
    pad[3 : 3 + ROWS, 3 : 3 + COLS, :] = tile[...].astype(F32)
    pad[3 + ROWS : 6 + ROWS, 3 : 3 + COLS, :] = jnp.where(even_row, rows[0], rows[1])
    pad[:, 0:3, :] = jnp.where(even_col, cols[1], cols[0])
    pad[:, 3 + COLS : 6 + COLS, :] = jnp.where(even_col, cols[0], cols[1])


def lanes_of(block):
    return pl.ds(pl.multiple_of(block * 128, 128), 128)


def depthwise(pad, taps, finish, flip):
    def block(cb, carry):
        lanes = lanes_of(cb)
        totals = [jnp.zeros((ROWS, 8, 128), F32) for _ in range(COLS // 8)]
        for s in range(7):
            weights = []
            for r in range(7):
                tap = 7 * (6 - r) + 6 - s if flip else 7 * r + s
                weights.append(taps[tap : tap + 1, lanes].reshape(1, 1, 128))
            for cg in range(COLS // 8):
                band = pad[:, 8 * cg + s : 8 * cg + s + 8, lanes]
                for r in range(7):
                    totals[cg] = totals[cg] + band[r : r + ROWS] * weights[r]
        for cg in range(COLS // 8):
            finish(cg, lanes, totals[cg])
        return carry

    lax.fori_loop(0, CH // 128, block, 0)


def grads_kernel(
    place, tile, row_one, row_two, col_one, col_two, cot, taps, dw_bias, gain, shift, scale, b_out,
    w_in, b_in, w_out,
    pad, block_out, d_conv, d_row_one, d_row_two, rows_out, bias_out, mine_out, theirs_out, mine_in, theirs_in,
    conv, x_hat, rstd, normed, d_branch, branch, d_normed,
):
    step = pl.program_id(0)
    first = place[0] == 0
    even_row = place[1] == 0

    @pl.when(step == 0)
    def _():
        assemble(pad, tile, row_one, row_two, col_one, col_two, even_row, first)

        def finish(cg, lanes, total):
            conv[:, 8 * cg : 8 * cg + 8, lanes] = total

        depthwise(pad, taps, finish, False)
        rows = conv[...].reshape(COUNT, CH) + dw_bias[...]
        centred = rows - jnp.mean(rows, axis=-1, keepdims=True)
        inverse = lax.rsqrt(jnp.mean(centred * centred, axis=-1, keepdims=True) + 1e-06)
        hat = centred * inverse
        x_hat[...] = hat
        rstd[...] = inverse
        normed[...] = (hat * gain[...] + shift[...]).astype(BF16)
        d_branch[...] = (cot[...].astype(F32) * scale[...]).astype(BF16)
        branch[...] = jnp.broadcast_to(b_out[...], (COUNT, CH))
        d_normed[...] = jnp.zeros((COUNT, CH), F32)

    pre_act = dot_nn(normed[...], w_in[...]) + b_in[...]
    cumul = 0.5 * (1.0 + lax.erf(pre_act * 0.7071067811865476))
    act = (pre_act * cumul).astype(BF16)
    slope = cumul + pre_act * jnp.exp(-0.5 * pre_act * pre_act) * 0.3989422804014327
    d_pre = (dot_nt(d_branch[...], w_out[...]) * slope).astype(BF16)
    branch[...] += dot_nn(act, w_out[...])
    d_normed[...] += dot_nt(d_pre, w_in[...])

    bias = jnp.sum(d_pre.astype(F32), axis=0, keepdims=True)
    fourth = lax.broadcasted_iota(jnp.int32, (8, CHUNK), 1) % 4
    spaced = jnp.where(fourth == lax.broadcasted_iota(jnp.int32, (8, CHUNK), 0), bias, 0.0).astype(BF16)
    source = lax.broadcasted_iota(jnp.int32, (CHUNK, 128), 0) // 4
    pick = (source == lax.broadcasted_iota(jnp.int32, (CHUNK, 128), 1)).astype(F32).astype(BF16)
    bias_out[...] = dot_nn(spaced, pick)

    term = dot_tn(act, d_branch[...]).reshape(CHUNK // 32, 2, 16, CH)

    def by_lanes(part):
        return jnp.concatenate([part[:, :, 128 * k : 128 * k + 128] for k in range(4)], axis=1)

    mine_out[...] = by_lanes(jnp.where(first, term[:, 0], term[:, 1])).astype(BF16)
    theirs_out[...] = by_lanes(jnp.where(first, term[:, 1], term[:, 0])).astype(BF16)

    term = dot_tn(normed[...], d_pre).reshape(64, 8, CHUNK)
    upper = lax.broadcasted_iota(jnp.int32, (64, 8, 128), 1) < 4
    kept, given = [], []
    for k in range(2):
        low = term[:, :, 128 * k : 128 * k + 128]
        high = term[:, :, 256 + 128 * k : 384 + 128 * k]
        zero = jnp.where(upper, low, pltpu.roll(high, 4, 1))
        one = jnp.where(upper, pltpu.roll(low, 4, 1), high)
        kept.append(jnp.where(first, zero, one))
        given.append(jnp.where(first, one, zero))
    mine_in[...] = jnp.concatenate(kept, axis=1).astype(BF16)
    theirs_in[...] = jnp.concatenate(given, axis=1).astype(BF16)

    @pl.when(step == STEPS - 1)
    def _():
        hat = x_hat[...]
        d_norm = d_normed[...]
        d_hat = d_norm * gain[...]
        grad = rstd[...] * (
            d_hat
            - jnp.mean(d_hat, axis=-1, keepdims=True)
            - hat * jnp.mean(d_hat * hat, axis=-1, keepdims=True)
        )
        grad = grad.astype(BF16)
        out = grad.reshape(ROWS, COLS, CH)
        d_conv[...] = out
        d_row_one[...] = jnp.where(even_row, out[ROWS - 3 :], out[:3])
        d_row_two[...] = jnp.where(even_row, out[:3], out[ROWS - 3 :])
        whole_branch = branch[...]
        block_out[...] = (tile[...].reshape(COUNT, CH).astype(F32) + scale[...] * whole_branch).astype(BF16)
        rows_out[0:1, :] = jnp.sum(grad.astype(F32), axis=0, keepdims=True)
        rows_out[1:2, :] = jnp.sum(d_norm * hat, axis=0, keepdims=True)
        rows_out[2:3, :] = jnp.sum(d_norm, axis=0, keepdims=True)
        rows_out[3:4, :] = jnp.sum(d_branch[...].astype(F32), axis=0, keepdims=True)
        rows_out[4:5, :] = jnp.sum(cot[...].astype(F32) * whole_branch, axis=0, keepdims=True)


def whole(shape):
    return pl.BlockSpec(shape, lambda *_: (0,) * len(shape))


def grads(*operands):
    vector = whole((1, CH))
    half = (64, 64, 128)
    by_chip = pl.BlockSpec((CHUNK // 32, 64, 128), lambda t: (t, 0, 0))
    by_row = pl.BlockSpec((64, 16, 128), lambda t: (0, t, 0))
    shape = jax.ShapeDtypeStruct
    return pl.pallas_call(
        grads_kernel,
        grid=(STEPS,),
        in_specs=[
            pl.BlockSpec(memory_space=pltpu.SMEM),
            whole((ROWS, COLS, CH)),
            whole((3, COLS, CH)),
            whole((3, COLS, CH)),
            whole((ROWS + 6, 3, CH)),
            whole((ROWS + 6, 3, CH)),
            whole((COUNT, CH)),
            whole((49, CH)),
            vector,
            vector,
            vector,
            vector,
            vector,
            pl.BlockSpec((CH, CHUNK), lambda t: (0, t)),
            pl.BlockSpec((1, CHUNK), lambda t: (0, t)),
            pl.BlockSpec((CHUNK, CH), lambda t: (t, 0)),
        ],
        out_specs=[
            whole(PAD),
            whole((COUNT, CH)),
            whole((ROWS, COLS, CH)),
            whole((3, COLS, CH)),
            whole((3, COLS, CH)),
            whole((8, CH)),
            pl.BlockSpec((8, 128), lambda t: (0, t)),
            by_chip,
            by_chip,
            by_row,
            by_row,
        ],
        out_shape=[
            shape(PAD, F32),
            shape((COUNT, CH), BF16),
            shape((ROWS, COLS, CH), BF16),
            shape((3, COLS, CH), BF16),
            shape((3, COLS, CH), BF16),
            shape((8, CH), F32),
            shape((8, CH), F32),
            shape(half, BF16),
            shape(half, BF16),
            shape(half, BF16),
            shape(half, BF16),
        ],
        scratch_shapes=[
            pltpu.VMEM((ROWS, COLS, CH), F32),
            pltpu.VMEM((COUNT, CH), F32),
            pltpu.VMEM((COUNT, 1), F32),
            pltpu.VMEM((COUNT, CH), BF16),
            pltpu.VMEM((COUNT, CH), BF16),
            pltpu.VMEM((COUNT, CH), F32),
            pltpu.VMEM((COUNT, CH), F32),
        ],
        compiler_params=pltpu.CompilerParams(vmem_limit_bytes=VMEM_BYTES),
        cost_estimate=pl.CostEstimate(flops=3_200_000_000, bytes_accessed=12_000_000, transcendentals=1_000_000),
        name="grads",
    )(*operands)


def taps_kernel(pad, d_conv, rows, bias, turned, d_tile, table):
    d_tile[...] = d_conv[...].astype(F32)
    table[48:128, :] = jnp.zeros((80, CH), F32)

    def block(cb, carry):
        lanes = lanes_of(cb)
        for s in range(7):
            totals = [jnp.zeros((8, 128), F32) for _ in range(7)]
            for cg in range(COLS // 8):
                band = pad[:, 8 * cg + s : 8 * cg + s + 8, lanes]
                own = d_tile[:, 8 * cg : 8 * cg + 8, lanes]
                for r in range(7):
                    totals[r] = totals[r] + jnp.sum(band[r : r + ROWS] * own, axis=0)
            for r in range(7):
                table[7 * r + s : 7 * r + s + 1, lanes] = jnp.sum(totals[r], axis=0, keepdims=True)
        return carry

    lax.fori_loop(0, CH // 128, block, 0)
    table[49:54, :] = rows[0:5, :]
    table[54:58, :] = bias[0:4, :]
    turned[...] = table[...].T.reshape(64, 8, 128)


def tap_rows(pad, d_conv, rows, bias):
    return pl.pallas_call(
        taps_kernel,
        out_shape=jax.ShapeDtypeStruct((64, 8, 128), F32),
        scratch_shapes=[pltpu.VMEM((ROWS, COLS, CH), F32), pltpu.VMEM((128, CH), F32)],
        compiler_params=pltpu.CompilerParams(vmem_limit_bytes=VMEM_BYTES),
        cost_estimate=pl.CostEstimate(flops=30_000_000, bytes_accessed=2_000_000, transcendentals=0),
        name="tap_rows",
    )(pad, d_conv, rows, bias)


def split_kernel(place, out_one, out_two, in_one, in_two, keep, give):
    even = place[2] == 0
    for at, one, two in ((0, out_one, out_two), (64, in_one, in_two)):
        total = (one[...] + two[...]).reshape(4, 2, 2, 64, 128)
        keep[:, at : at + 64, :] = jnp.where(even, total[:, 0], total[:, 1]).reshape(8, 64, 128)
        give[:, at : at + 64, :] = jnp.where(even, total[:, 1], total[:, 0]).reshape(8, 64, 128)


def split_pair(*operands):
    half = pl.BlockSpec((16, 64, 128), lambda t: (t, 0, 0))
    block = pl.BlockSpec((8, 128, 128), lambda t: (t, 0, 0))
    return pl.pallas_call(
        split_kernel,
        grid=(4,),
        in_specs=[pl.BlockSpec(memory_space=pltpu.SMEM), half, half, half, half],
        out_specs=[block, block],
        out_shape=[jax.ShapeDtypeStruct((32, 128, 128), BF16)] * 2,
        compiler_params=pltpu.CompilerParams(vmem_limit_bytes=VMEM_BYTES),
        cost_estimate=pl.CostEstimate(flops=1_000_000, bytes_accessed=6_000_000, transcendentals=0),
        name="split_pair",
    )(*operands)


def split_small_kernel(place, one, two, keep, give):
    total = (one[...] + two[...]).reshape(16, 2, 2, 8, 128)
    even = place[2] == 0
    keep[...] = jnp.where(even, total[:, 0], total[:, 1]).reshape(32, 8, 128)
    give[...] = jnp.where(even, total[:, 1], total[:, 0]).reshape(32, 8, 128)


def split_small(*operands):
    return pl.pallas_call(
        split_small_kernel,
        in_specs=[pl.BlockSpec(memory_space=pltpu.SMEM)] + [pl.BlockSpec(memory_space=pltpu.VMEM)] * 2,
        out_shape=[jax.ShapeDtypeStruct((32, 8, 128), F32)] * 2,
        compiler_params=pltpu.CompilerParams(vmem_limit_bytes=VMEM_BYTES),
        cost_estimate=pl.CostEstimate(flops=100_000, bytes_accessed=700_000, transcendentals=0),
        name="split_small",
    )(*operands)


def add_kernel(one, two, small_one, small_two, total):
    total[:, 0:128, :] = one[...] + two[...]
    total[:, 128:136, :] = (small_one[...] + small_two[...]).astype(BF16)


def add_pair(*operands):
    large = pl.BlockSpec((8, 128, 128), lambda t: (t, 0, 0))
    small = pl.BlockSpec((8, 8, 128), lambda t: (t, 0, 0))
    return pl.pallas_call(
        add_kernel,
        grid=(4,),
        in_specs=[large, large, small, small],
        out_specs=pl.BlockSpec((8, 136, 128), lambda t: (t, 0, 0)),
        out_shape=jax.ShapeDtypeStruct((32, 136, 128), BF16),
        compiler_params=pltpu.CompilerParams(vmem_limit_bytes=VMEM_BYTES),
        cost_estimate=pl.CostEstimate(flops=1_000_000, bytes_accessed=3_000_000, transcendentals=0),
        name="add_pair",
    )(*operands)


def sum_kernel(factor, place, spread, g_in, g_out, g_channel, g_bias):
    total = jnp.sum(spread[...].astype(F32), axis=0) * factor
    for k in range(4):
        g_out[:, 128 * k : 128 * k + 128] = total[16 * k : 16 * k + 16, :]
    for t in range(STEPS):
        for k in range(2):
            own = total[64 + 16 * t + 8 * k : 72 + 16 * t + 8 * k, :]
            at = CHUNK * t + 128 * k
            g_in[:, at : at + 128] = own[0:4]
            g_in[:, at + 256 : at + 384] = own[4:8]
    small = total[128:136, :]
    small = jnp.where(place[0] == 0, small, pltpu.roll(small, 4, 0))
    g_channel[...] = small[0:4, 0:54]
    g_bias[...] = jnp.concatenate([small[k : k + 1, 54:58] for k in range(4)], axis=1)


def sum_chips(place, spread, factor):
    shape = jax.ShapeDtypeStruct
    return pl.pallas_call(
        lambda *refs: sum_kernel(factor, *refs),
        in_specs=[pl.BlockSpec(memory_space=pltpu.SMEM), pl.BlockSpec(memory_space=pltpu.VMEM)],
        out_shape=[shape((4, HID), F32), shape((16, CH), F32), shape((4, 54), F32), shape((1, 16), F32)],
        compiler_params=pltpu.CompilerParams(vmem_limit_bytes=16 * 1024 * 1024),
        cost_estimate=pl.CostEstimate(flops=1_000_000, bytes_accessed=1_000_000, transcendentals=0),
        name="sum_chips",
    )(place, spread)


def features_kernel(place, d_conv, row_one, row_two, col_one, col_two, cot, taps, out, pad):
    assemble(pad, d_conv, row_one, row_two, col_one, col_two, place[1] == 0, place[0] == 0)

    def finish(cg, lanes, total):
        columns = slice(8 * cg, 8 * cg + 8)
        pad[0:ROWS, columns, lanes] = total

    depthwise(pad, taps, finish, True)
    out[...] = (cot[...].astype(F32) + pad[0:ROWS, 0:COLS, :]).astype(BF16)


def features_part(*operands):
    return pl.pallas_call(
        features_kernel,
        in_specs=[pl.BlockSpec(memory_space=pltpu.SMEM)] + [pl.BlockSpec(memory_space=pltpu.VMEM)] * 7,
        out_shape=jax.ShapeDtypeStruct((ROWS, COLS, CH), BF16),
        scratch_shapes=[pltpu.VMEM(PAD, F32)],
        compiler_params=pltpu.CompilerParams(vmem_limit_bytes=VMEM_BYTES),
        cost_estimate=pl.CostEstimate(flops=30_000_000, bytes_accessed=2_000_000, transcendentals=0),
        name="features_part",
    )(*operands)


def exchange(one, two, axis):
    count = lax.axis_size(axis)
    met = []
    for value, start in ((one, 0), (two, 1)):
        pairs = []
        for i in range(start, count - 1, 2):
            pairs += [(i, i + 1), (i + 1, i)]
        met.append(lax.ppermute(value, axis, pairs))
    return met


def halo_sides(row_one, row_two, tile, even_row, even_col):
    top = jnp.where(even_row, row_two, row_one)
    bottom = jnp.where(even_row, row_one, row_two)
    tail = jnp.concatenate([part[:, COLS - 3 :] for part in (top, tile, bottom)], axis=0)
    head = jnp.concatenate([part[:, :3] for part in (top, tile, bottom)], axis=0)
    return jnp.where(even_col, tail, head), jnp.where(even_col, head, tail)


def swap_cores(value):
    return lax.ppermute(value, "c", [(0, 1), (1, 0)])


def swap_chips(value):
    pairs = []
    for x in range(4):
        pairs += [(2 * x, 2 * (x ^ 1)), (2 * x + 1, 2 * (3 - x) + 1)]
    return lax.ppermute(value, ("xh", "xl", "c"), pairs)


def shards(
    features, cotangent, dw_kernel, dw_bias, norm_gain_vector, norm_bias,
    pw_in_weight, pw_in_bias, pw_out_weight, pw_out_bias, layer_scale,
):
    factor = 1.0 / math.sqrt(COUNT * lax.axis_size(EVERY))
    core, y_hi, x_lo = (lax.axis_index(name).astype(jnp.int32) for name in ("c", "yh", "xl"))
    place = jnp.stack([core, y_hi, x_lo])
    even_row, even_col = y_hi == 0, core == 0
    row = lambda vector: vector.reshape(1, -1)
    ends = features[:3], features[ROWS - 3 :]
    rows_met = exchange(jnp.where(even_row, ends[1], ends[0]), jnp.where(even_row, ends[0], ends[1]), ROW)
    cols_met = exchange(*halo_sides(*rows_met, features, even_row, even_col), COL)
    pad, block_rows, d_conv, d_one, d_two, rows, bias, mine_out, theirs_out, mine_in, theirs_in = grads(
        place, features, *rows_met, *cols_met, cotangent.reshape(COUNT, CH), dw_kernel, row(dw_bias),
        row(norm_gain_vector), row(norm_bias), row(layer_scale), row(pw_out_bias),
        pw_in_weight, row(pw_in_bias), pw_out_weight,
    )
    met_out, met_in = swap_cores(theirs_out), swap_cores(theirs_in)
    d_rows = exchange(d_one, d_two, ROW)
    keep, give = split_pair(place, mine_out, met_out, mine_in, met_in)
    give, d_rows = lax.optimization_barrier((give, d_rows))
    given = swap_chips(give)
    sides = halo_sides(*d_rows, d_conv, even_row, even_col)
    pad, give, sides = lax.optimization_barrier((pad, give, sides))
    d_cols = exchange(*sides, COL)
    small = tap_rows(pad, d_conv, rows, bias)
    small, d_cols = lax.optimization_barrier((small, d_cols))
    small_keep, small_give = split_small(place, small, swap_cores(small))
    small_given = swap_chips(small_give)
    message = add_pair(keep, given, small_keep, small_given)
    spread = lax.all_to_all(message, GROUP, 0, 0, tiled=True)
    d_conv, message = lax.optimization_barrier((d_conv, message))
    grad_features = features_part(place, d_conv, *d_rows, *d_cols, cotangent, dw_kernel)
    grad_in, grad_out, grad_channel, grad_bias = sum_chips(place, spread, factor)
    return (
        block_rows.reshape(ROWS, COLS, CH),
        grad_features,
        grad_in,
        grad_out,
        grad_channel.T,
        grad_bias.reshape(-1),
    )


def solution(mesh):
    fine = Mesh(mesh.devices.reshape(4, 2, 2, 2, 2, 2), EVERY)
    return jax.shard_map(
        shards,
        mesh=fine,
        in_specs=(P(ROW, COL, None), P(ROW, COL, None)) + (P(),) * 9,
        out_specs=(
            P(ROW, COL, None),
            P(ROW, COL, None),
            P(EVERY, None),
            P(EVERY, None),
            P(None, EVERY),
            P(EVERY),
        ),
        check_vma=False,
    )
```

```python
import math

import jax
import jax.numpy as jnp
from jax import lax
from jax.experimental import pallas as pl
from jax.experimental.pallas import tpu as pltpu
from jax.sharding import Mesh
from jax.sharding import PartitionSpec as P

EVERY = ("z", "yh", "xh", "xl", "yl", "c")
ROW = ("z", "yh")
COL = ("xh", "xl", "yl", "c")
GROUP = ("z", "yh", "xh", "yl")
ROWS, COLS, CH, HID, CHUNK = 8, 32, 512, 2048, 512
COUNT = ROWS * COLS
STEPS = HID // CHUNK
BLOCKS = CH // 128
PAD = (BLOCKS, ROWS + 6, COLS + 8, 128)
TILE = (BLOCKS, ROWS, COLS, 128)
F32, BF16 = jnp.float32, jnp.bfloat16
VMEM_BYTES = 28 * 1024 * 1024


def dot_nn(left, right):
    return lax.dot_general(left, right, (((1,), (0,)), ((), ())), preferred_element_type=F32)


def dot_nt(left, right):
    return lax.dot_general(left, right, (((1,), (1,)), ((), ())), preferred_element_type=F32)


def dot_tn(left, right):
    return lax.dot_general(left, right, (((0,), (0,)), ((), ())), preferred_element_type=F32)


def params(vmem=VMEM_BYTES):
    return pltpu.CompilerParams(vmem_limit_bytes=vmem)


def cost(flops, moved):
    return pl.CostEstimate(flops=flops, bytes_accessed=moved, transcendentals=0)


def near(value):
    return pltpu.with_memory_space_constraint(value, pltpu.VMEM)


SCALARS = pl.BlockSpec(memory_space=pltpu.SMEM)
WHOLE = pl.BlockSpec(memory_space=pltpu.VMEM)


def fetch_kernel(count, *refs):
    sources, targets, sem = refs[:count], refs[count : 2 * count], refs[2 * count]
    copies = [pltpu.make_async_copy(sources[k], targets[k], sem.at[k]) for k in range(count)]
    for copy in copies:
        copy.start()
    for copy in copies:
        copy.wait()


def fetch(*arrays):
    count = len(arrays)
    return pl.pallas_call(
        lambda *refs: fetch_kernel(count, *refs),
        in_specs=[pl.BlockSpec(memory_space=pl.ANY)] * count,
        out_specs=[WHOLE] * count,
        out_shape=[pltpu.VMEM(array.shape, array.dtype) for array in arrays],
        scratch_shapes=[pltpu.SemaphoreType.DMA((count,))],
        compiler_params=params(),
        cost_estimate=cost(0, 5_000_000),
        name="fetch",
    )(*arrays)


def assemble(pad, tile, row_one, row_two, col_one, col_two, even_row, even_col):
    for k in range(BLOCKS):
        lanes = slice(128 * k, 128 * k + 128)
        rows = row_one[:, :, lanes].astype(F32), row_two[:, :, lanes].astype(F32)
        cols = col_one[:, :, lanes].astype(F32), col_two[:, :, lanes].astype(F32)
        pad[k, 0:3, 3 : 3 + COLS, :] = jnp.where(even_row, rows[1], rows[0])
        pad[k, 3 : 3 + ROWS, 3 : 3 + COLS, :] = tile[:, :, lanes].astype(F32)
        pad[k, 3 + ROWS : 6 + ROWS, 3 : 3 + COLS, :] = jnp.where(even_row, rows[0], rows[1])
        pad[k, :, 0:3, :] = jnp.where(even_col, cols[1], cols[0])
        pad[k, :, 3 + COLS : 6 + COLS, :] = jnp.where(even_col, cols[0], cols[1])


def lanes_of(block):
    return pl.ds(pl.multiple_of(block * 128, 128), 128)


def depthwise(pad, taps, out, flip):
    def block(cb, carry):
        lanes = lanes_of(cb)
        for cg in range(COLS // 8):
            total = jnp.zeros((ROWS, 8, 128), F32)
            for s in range(7):
                band = pad[cb, :, 8 * cg + s : 8 * cg + s + 8, :]
                for r in range(7):
                    tap = 7 * (6 - r) + 6 - s if flip else 7 * r + s
                    total = total + band[r : r + ROWS] * taps[tap : tap + 1, lanes].reshape(1, 1, 128)
            out[cb, :, 8 * cg : 8 * cg + 8, :] = total
        return carry

    lax.fori_loop(0, BLOCKS, block, 0)


def grads_kernel(
    place, tile, row_one, row_two, col_one, col_two, cot, taps, vectors, w_in, b_in, w_out,
    pad, block_out, d_conv, d_row_one, d_row_two, rows_out, mine_out, theirs_out, mine_in, theirs_in,
    conv,
):
    first = place[0] == 0
    even_row = place[1] == 0
    assemble(pad, tile, row_one, row_two, col_one, col_two, even_row, first)
    depthwise(pad, taps, conv, False)
    dw_bias, gain, shift, scale, b_out = (vectors[k : k + 1, :] for k in range(5))
    rows = jnp.concatenate([conv[k].reshape(COUNT, 128) for k in range(BLOCKS)], axis=1) + dw_bias
    centred = rows - jnp.mean(rows, axis=-1, keepdims=True)
    inverse = lax.rsqrt(jnp.mean(centred * centred, axis=-1, keepdims=True) + 1e-06)
    hat = centred * inverse
    normed = (hat * gain + shift).astype(BF16)
    d_branch = (cot[...].astype(F32) * scale).astype(BF16)
    branch = b_out
    d_normed = 0.0

    fourth = lax.broadcasted_iota(jnp.int32, (8, CHUNK), 1) % 4
    fourth = fourth == lax.broadcasted_iota(jnp.int32, (8, CHUNK), 0)
    pick = lax.broadcasted_iota(jnp.int32, (CHUNK, 128), 0) // 4
    pick = (pick == lax.broadcasted_iota(jnp.int32, (CHUNK, 128), 1)).astype(F32).astype(BF16)
    upper = lax.broadcasted_iota(jnp.int32, (64, 8, 128), 1) < 4

    def by_lanes(part):
        return jnp.concatenate([part[:, :, 128 * k : 128 * k + 128] for k in range(BLOCKS)], axis=1)

    for step in range(STEPS):
        hidden = slice(CHUNK * step, CHUNK * step + CHUNK)
        pre_act = dot_nn(normed, w_in[:, hidden]) + b_in[:, hidden]
        cumul = 0.5 * (1.0 + lax.erf(pre_act * 0.7071067811865476))
        act = (pre_act * cumul).astype(BF16)
        slope = cumul + pre_act * jnp.exp(-0.5 * pre_act * pre_act) * 0.3989422804014327
        d_pre = (dot_nt(d_branch, w_out[hidden, :]) * slope).astype(BF16)
        branch = branch + dot_nn(act, w_out[hidden, :])
        d_normed = d_normed + dot_nt(d_pre, w_in[:, hidden])

        bias = jnp.sum(d_pre.astype(F32), axis=0, keepdims=True)
        rows_out[8:16, 128 * step : 128 * step + 128] = dot_nn(jnp.where(fourth, bias, 0.0).astype(BF16), pick)

        term = dot_tn(act, d_branch).reshape(CHUNK // 32, 2, 16, CH)
        chips = slice(CHUNK // 32 * step, CHUNK // 32 * (step + 1))
        mine_out[chips] = by_lanes(jnp.where(first, term[:, 0], term[:, 1])).astype(BF16)
        theirs_out[chips] = by_lanes(jnp.where(first, term[:, 1], term[:, 0])).astype(BF16)

        term = dot_tn(normed, d_pre).reshape(64, 8, CHUNK)
        kept, given = [], []
        for k in range(2):
            low = term[:, :, 128 * k : 128 * k + 128]
            high = term[:, :, 256 + 128 * k : 384 + 128 * k]
            zero = jnp.where(upper, low, pltpu.roll(high, 4, 1))
            one = jnp.where(upper, pltpu.roll(low, 4, 1), high)
            kept.append(jnp.where(first, zero, one))
            given.append(jnp.where(first, one, zero))
        mine_in[:, 16 * step : 16 * step + 16, :] = jnp.concatenate(kept, axis=1).astype(BF16)
        theirs_in[:, 16 * step : 16 * step + 16, :] = jnp.concatenate(given, axis=1).astype(BF16)

    d_hat = d_normed * gain
    grad = inverse * (
        d_hat
        - jnp.mean(d_hat, axis=-1, keepdims=True)
        - hat * jnp.mean(d_hat * hat, axis=-1, keepdims=True)
    )
    grad = grad.astype(BF16)
    out = grad.reshape(ROWS, COLS, CH)
    d_conv[...] = out
    d_row_one[...] = jnp.where(even_row, out[ROWS - 3 :], out[:3])
    d_row_two[...] = jnp.where(even_row, out[:3], out[ROWS - 3 :])
    block_out[...] = (tile[...].reshape(COUNT, CH).astype(F32) + scale * branch).astype(BF16)
    rows_out[0:1, :] = jnp.sum(grad.astype(F32), axis=0, keepdims=True)
    rows_out[1:2, :] = jnp.sum(d_normed * hat, axis=0, keepdims=True)
    rows_out[2:3, :] = jnp.sum(d_normed, axis=0, keepdims=True)
    rows_out[3:4, :] = jnp.sum(d_branch.astype(F32), axis=0, keepdims=True)
    rows_out[4:5, :] = jnp.sum(cot[...].astype(F32) * branch, axis=0, keepdims=True)


def grads(place, *operands):
    half = (64, 64, 128)
    return pl.pallas_call(
        grads_kernel,
        in_specs=[SCALARS] + [WHOLE] * len(operands),
        out_shape=[
            pltpu.VMEM(PAD, F32),
            jax.ShapeDtypeStruct((COUNT, CH), BF16),
            pltpu.VMEM((ROWS, COLS, CH), BF16),
            pltpu.VMEM((3, COLS, CH), BF16),
            pltpu.VMEM((3, COLS, CH), BF16),
            pltpu.VMEM((16, CH), F32),
            pltpu.VMEM(half, BF16),
            pltpu.VMEM(half, BF16),
            pltpu.VMEM(half, BF16),
            pltpu.VMEM(half, BF16),
        ],
        scratch_shapes=[pltpu.VMEM(TILE, F32)],
        compiler_params=params(),
        cost_estimate=cost(3_200_000_000, 12_000_000),
        name="grads",
    )(place, *(near(value) for value in operands))


def taps_kernel(place, pad, d_conv, rows, keep, give, d_tile, table):
    for k in range(BLOCKS):
        d_tile[k] = d_conv[:, :, 128 * k : 128 * k + 128].astype(F32)
    table[48:128, :] = jnp.zeros((80, CH), F32)

    def block(cb, carry):
        lanes = lanes_of(cb)
        for s in range(7):
            totals = [jnp.zeros((8, 128), F32) for _ in range(7)]
            for cg in range(COLS // 8):
                band = pad[cb, :, 8 * cg + s : 8 * cg + s + 8, :]
                own = d_tile[cb, :, 8 * cg : 8 * cg + 8, :]
                for r in range(7):
                    totals[r] = totals[r] + jnp.sum(band[r : r + ROWS] * own, axis=0)
            for r in range(7):
                table[7 * r + s : 7 * r + s + 1, lanes] = jnp.sum(totals[r], axis=0, keepdims=True)
        return carry

    lax.fori_loop(0, BLOCKS, block, 0)
    table[49:54, :] = rows[0:5, :]
    table[54:58, :] = rows[8:12, :]
    turned = table[...].T.reshape(16, 2, 2, 8, 128)
    even = place[2] == 0
    keep[...] = jnp.where(even, turned[:, 0], turned[:, 1]).reshape(32, 8, 128).astype(BF16)
    give[...] = jnp.where(even, turned[:, 1], turned[:, 0]).reshape(32, 8, 128).astype(BF16)


def tap_rows(place, *operands):
    return pl.pallas_call(
        taps_kernel,
        in_specs=[SCALARS] + [WHOLE] * len(operands),
        out_shape=[pltpu.VMEM((32, 8, 128), BF16)] * 2,
        scratch_shapes=[pltpu.VMEM(TILE, F32), pltpu.VMEM((128, CH), F32)],
        compiler_params=params(),
        cost_estimate=cost(30_000_000, 2_000_000),
        name="tap_rows",
    )(place, *(near(value) for value in operands))


def split_kernel(place, out_one, out_two, in_one, in_two, keep, give):
    even = place[2] == 0
    for at, one, two in ((0, out_one, out_two), (64, in_one, in_two)):
        for k in range(16):
            total = [(one[4 * k + 2 * p : 4 * k + 2 * p + 2] + two[4 * k + 2 * p : 4 * k + 2 * p + 2]) for p in range(2)]
            keep[2 * k : 2 * k + 2, at : at + 64, :] = jnp.where(even, total[0], total[1])
            give[2 * k : 2 * k + 2, at : at + 64, :] = jnp.where(even, total[1], total[0])


def split_pair(place, *operands):
    return pl.pallas_call(
        split_kernel,
        in_specs=[SCALARS] + [WHOLE] * len(operands),
        out_shape=[pltpu.VMEM((32, 128, 128), BF16)] * 2,
        compiler_params=params(),
        cost_estimate=cost(1_000_000, 6_000_000),
        name="split_pair",
    )(place, *(near(value) for value in operands))


def add_kernel(one, two, small_one, small_two, small_three, small_four, total):
    total[:, 0:128, :] = one[...] + two[...]
    small = small_one[...].astype(F32) + small_two[...].astype(F32)
    small = small + small_three[...].astype(F32) + small_four[...].astype(F32)
    total[:, 128:136, :] = small.astype(BF16)


def add_pair(*operands):
    return pl.pallas_call(
        add_kernel,
        in_specs=[WHOLE] * len(operands),
        out_shape=jax.ShapeDtypeStruct((32, 136, 128), BF16),
        compiler_params=params(),
        cost_estimate=cost(1_000_000, 3_000_000),
        name="add_pair",
    )(*(near(value) for value in operands))


def sum_kernel(factor, place, spread, g_in, g_out, g_channel, g_bias):
    total = jnp.sum(spread[...].astype(F32), axis=0) * factor
    for k in range(4):
        g_out[:, 128 * k : 128 * k + 128] = total[16 * k : 16 * k + 16, :]
    for t in range(STEPS):
        for k in range(2):
            own = total[64 + 16 * t + 8 * k : 72 + 16 * t + 8 * k, :]
            at = CHUNK * t + 128 * k
            g_in[:, at : at + 128] = own[0:4]
            g_in[:, at + 256 : at + 384] = own[4:8]
    small = total[128:136, :]
    small = jnp.where(place[0] == 0, small, pltpu.roll(small, 4, 0))
    g_channel[...] = small[0:4, 0:54]
    g_bias[...] = jnp.concatenate([small[k : k + 1, 54:58] for k in range(4)], axis=1)


def sum_chips(place, spread, factor):
    shape = jax.ShapeDtypeStruct
    return pl.pallas_call(
        lambda *refs: sum_kernel(factor, *refs),
        in_specs=[pl.BlockSpec(memory_space=pltpu.SMEM), pl.BlockSpec(memory_space=pltpu.VMEM)],
        out_shape=[shape((4, HID), F32), shape((16, CH), F32), shape((4, 54), F32), shape((1, 16), F32)],
        compiler_params=pltpu.CompilerParams(vmem_limit_bytes=16 * 1024 * 1024),
        cost_estimate=pl.CostEstimate(flops=1_000_000, bytes_accessed=1_000_000, transcendentals=0),
        name="sum_chips",
    )(place, spread)


def features_kernel(place, d_conv, row_one, row_two, col_one, col_two, cot, taps, out, pad, total):
    assemble(pad, d_conv, row_one, row_two, col_one, col_two, place[1] == 0, place[0] == 0)
    depthwise(pad, taps, total, True)
    cot_wide = cot[...].astype(F32).reshape(ROWS, COLS, CH)
    for k in range(BLOCKS):
        lanes = slice(128 * k, 128 * k + 128)
        out[:, :, lanes] = (cot_wide[:, :, lanes] + total[k]).astype(BF16)


def features_part(place, *operands):
    return pl.pallas_call(
        features_kernel,
        in_specs=[SCALARS] + [WHOLE] * len(operands),
        out_shape=jax.ShapeDtypeStruct((ROWS, COLS, CH), BF16),
        scratch_shapes=[pltpu.VMEM(PAD, F32), pltpu.VMEM(TILE, F32)],
        compiler_params=params(),
        cost_estimate=cost(30_000_000, 2_000_000),
        name="features_part",
    )(place, *(near(value) for value in operands))


def exchange(one, two, axis):
    count = lax.axis_size(axis)
    met = []
    for value, start in ((one, 0), (two, 1)):
        pairs = []
        for i in range(start, count - 1, 2):
            pairs += [(i, i + 1), (i + 1, i)]
        met.append(lax.ppermute(value, axis, pairs))
    return met


def halo_sides(row_one, row_two, tile, even_row, even_col):
    top = jnp.where(even_row, row_two, row_one)
    bottom = jnp.where(even_row, row_one, row_two)
    tail = jnp.concatenate([part[:, COLS - 3 :] for part in (top, tile, bottom)], axis=0)
    head = jnp.concatenate([part[:, :3] for part in (top, tile, bottom)], axis=0)
    return jnp.where(even_col, tail, head), jnp.where(even_col, head, tail)


def swap_cores(value):
    return lax.ppermute(value, "c", [(0, 1), (1, 0)])


def swap_chips(value):
    pairs = []
    for x in range(4):
        pairs += [(2 * x, 2 * (x ^ 1)), (2 * x + 1, 2 * (3 - x) + 1)]
    return lax.ppermute(value, ("xh", "xl", "c"), pairs)


def swap_across(value):
    pairs = []
    for x in range(4):
        pairs += [(2 * x, 2 * (3 - x) + 1), (2 * x + 1, 2 * (x ^ 1))]
    return lax.ppermute(value, ("xh", "xl", "c"), pairs)


def shards(
    features, cotangent, dw_kernel, dw_bias, norm_gain_vector, norm_bias,
    pw_in_weight, pw_in_bias, pw_out_weight, pw_out_bias, layer_scale,
):
    factor = 1.0 / math.sqrt(COUNT * lax.axis_size(EVERY))
    core, y_hi, x_lo = (lax.axis_index(name).astype(jnp.int32) for name in ("c", "yh", "xl"))
    place = jnp.stack([core, y_hi, x_lo])
    even_row, even_col = y_hi == 0, core == 0
    vectors = jnp.stack([dw_bias, norm_gain_vector, norm_bias, layer_scale, pw_out_bias])
    ends = features[:3], features[ROWS - 3 :]
    rows_met = exchange(jnp.where(even_row, ends[1], ends[0]), jnp.where(even_row, ends[0], ends[1]), ROW)
    tile, cot, taps, vectors, w_in, b_in, w_out = fetch(
        features, cotangent.reshape(COUNT, CH), dw_kernel, vectors, pw_in_weight,
        pw_in_bias.reshape(1, HID), pw_out_weight,
    )
    sides = halo_sides(*rows_met, features, even_row, even_col)
    sides, w_in = lax.optimization_barrier((sides, w_in))
    cols_met = exchange(*sides, COL)
    pad, block_rows, d_conv, d_one, d_two, rows, mine_out, theirs_out, mine_in, theirs_in = grads(
        place, tile, *rows_met, *cols_met, cot, taps, vectors, w_in, b_in, w_out
    )
    met_out, met_in = swap_cores(theirs_out), swap_cores(theirs_in)
    d_rows = exchange(d_one, d_two, ROW)
    small_keep, small_give = tap_rows(place, pad, d_conv, rows)
    met_out, met_in, small_keep, small_give = lax.optimization_barrier((met_out, met_in, small_keep, small_give))
    keep, give = split_pair(place, mine_out, met_out, mine_in, met_in)
    give, d_rows = lax.optimization_barrier((give, d_rows))
    given = swap_chips(give)
    sides = halo_sides(*d_rows, d_conv, even_row, even_col)
    small_keep, small_give, give, sides = lax.optimization_barrier((small_keep, small_give, give, sides))
    smalls = small_keep, swap_cores(small_keep), swap_chips(small_give), swap_across(small_give)
    d_cols = exchange(*sides, COL)
    smalls, d_cols = lax.optimization_barrier((smalls, d_cols))
    message = add_pair(keep, given, *smalls)
    spread = lax.all_to_all(message, GROUP, 0, 0, tiled=True)
    d_conv, message = lax.optimization_barrier((d_conv, message))
    grad_features = features_part(place, d_conv, *d_rows, *d_cols, cot, taps)
    grad_in, grad_out, grad_channel, grad_bias = sum_chips(place, spread, factor)
    return (
        block_rows.reshape(ROWS, COLS, CH),
        grad_features,
        grad_in,
        grad_out,
        grad_channel.T,
        grad_bias.reshape(-1),
    )


def solution(mesh):
    fine = Mesh(mesh.devices.reshape(4, 2, 2, 2, 2, 2), EVERY)
    return jax.shard_map(
        shards,
        mesh=fine,
        in_specs=(P(ROW, COL, None), P(ROW, COL, None)) + (P(),) * 9,
        out_specs=(
            P(ROW, COL, None),
            P(ROW, COL, None),
            P(EVERY, None),
            P(EVERY, None),
            P(None, EVERY),
            P(EVERY),
        ),
        check_vma=False,
    )
```

```python
import math

import jax
import jax.numpy as jnp
from jax import lax
from jax.experimental import pallas as pl
from jax.experimental.pallas import tpu as pltpu
from jax.sharding import Mesh
from jax.sharding import PartitionSpec as P

EVERY = ("z", "yh", "xh", "xl", "yl", "c")
ROW = ("z", "yh")
COL = ("xh", "xl", "yl", "c")
GROUP = ("z", "yh", "xh", "yl")
ROWS, COLS, CH, HID, CHUNK = 8, 32, 512, 2048, 512
COUNT = ROWS * COLS
STEPS = HID // CHUNK
BLOCKS = CH // 128
PAD = (BLOCKS, ROWS + 6, COLS + 8, 128)
TILE = (BLOCKS, ROWS, COLS, 128)
F32, BF16 = jnp.float32, jnp.bfloat16
VMEM_BYTES = 28 * 1024 * 1024


def dot_nn(left, right):
    return lax.dot_general(left, right, (((1,), (0,)), ((), ())), preferred_element_type=F32)


def dot_nt(left, right):
    return lax.dot_general(left, right, (((1,), (1,)), ((), ())), preferred_element_type=F32)


def dot_tn(left, right):
    return lax.dot_general(left, right, (((0,), (0,)), ((), ())), preferred_element_type=F32)


def params(vmem=VMEM_BYTES):
    return pltpu.CompilerParams(vmem_limit_bytes=vmem)


def cost(flops, moved):
    return pl.CostEstimate(flops=flops, bytes_accessed=moved, transcendentals=0)


def near(value):
    return pltpu.with_memory_space_constraint(value, pltpu.VMEM)


SCALARS = pl.BlockSpec(memory_space=pltpu.SMEM)
WHOLE = pl.BlockSpec(memory_space=pltpu.VMEM)


def fetch_kernel(count, *refs):
    sources, targets, sem = refs[:count], refs[count : 2 * count], refs[2 * count]
    copies = [pltpu.make_async_copy(sources[k], targets[k], sem.at[k]) for k in range(count)]
    for copy in copies:
        copy.start()
    for copy in copies:
        copy.wait()


def fetch(*arrays):
    count = len(arrays)
    return pl.pallas_call(
        lambda *refs: fetch_kernel(count, *refs),
        in_specs=[pl.BlockSpec(memory_space=pltpu.HBM)] * count,
        out_specs=[WHOLE] * count,
        out_shape=[pltpu.VMEM(array.shape, array.dtype) for array in arrays],
        scratch_shapes=[pltpu.SemaphoreType.DMA((count,))],
        compiler_params=params(),
        cost_estimate=cost(0, 5_000_000),
        name="fetch",
    )(*(pltpu.with_memory_space_constraint(array, pltpu.HBM) for array in arrays))


def assemble(pad, tile, row_one, row_two, col_one, col_two, even_row, even_col):
    for k in range(BLOCKS):
        lanes = slice(128 * k, 128 * k + 128)
        rows = row_one[:, :, lanes].astype(F32), row_two[:, :, lanes].astype(F32)
        cols = col_one[:, :, lanes].astype(F32), col_two[:, :, lanes].astype(F32)
        pad[k, 0:3, 3 : 3 + COLS, :] = jnp.where(even_row, rows[1], rows[0])
        pad[k, 3 : 3 + ROWS, 3 : 3 + COLS, :] = tile[:, :, lanes].astype(F32)
        pad[k, 3 + ROWS : 6 + ROWS, 3 : 3 + COLS, :] = jnp.where(even_row, rows[0], rows[1])
        pad[k, :, 0:3, :] = jnp.where(even_col, cols[1], cols[0])
        pad[k, :, 3 + COLS : 6 + COLS, :] = jnp.where(even_col, cols[0], cols[1])


def lanes_of(block):
    return pl.ds(pl.multiple_of(block * 128, 128), 128)


def depthwise(pad, taps, out, flip):
    def block(cb, carry):
        lanes = lanes_of(cb)
        for cg in range(COLS // 8):
            total = jnp.zeros((ROWS, 8, 128), F32)
            for s in range(7):
                band = pad[cb, :, 8 * cg + s : 8 * cg + s + 8, :]
                for r in range(7):
                    tap = 7 * (6 - r) + 6 - s if flip else 7 * r + s
                    total = total + band[r : r + ROWS] * taps[tap : tap + 1, lanes].reshape(1, 1, 128)
            out[cb, :, 8 * cg : 8 * cg + 8, :] = total
        return carry

    lax.fori_loop(0, BLOCKS, block, 0)


def grads_kernel(
    place, tile, row_one, row_two, col_one, col_two, cot, taps, vectors, w_in, b_in, w_out,
    pad, block_out, d_conv, d_row_one, d_row_two, rows_out, mine_out, theirs_out, mine_in, theirs_in,
    conv,
):
    first = place[0] == 0
    even_row = place[1] == 0
    assemble(pad, tile, row_one, row_two, col_one, col_two, even_row, first)
    depthwise(pad, taps, conv, False)
    dw_bias, gain, shift, scale, b_out = (vectors[k : k + 1, :] for k in range(5))
    rows = jnp.concatenate([conv[k].reshape(COUNT, 128) for k in range(BLOCKS)], axis=1) + dw_bias
    centred = rows - jnp.mean(rows, axis=-1, keepdims=True)
    inverse = lax.rsqrt(jnp.mean(centred * centred, axis=-1, keepdims=True) + 1e-06)
    hat = centred * inverse
    normed = (hat * gain + shift).astype(BF16)
    d_branch = (cot[...].astype(F32) * scale).astype(BF16)
    branch = b_out
    d_normed = 0.0

    fourth = lax.broadcasted_iota(jnp.int32, (8, CHUNK), 1) % 4
    fourth = fourth == lax.broadcasted_iota(jnp.int32, (8, CHUNK), 0)
    pick = lax.broadcasted_iota(jnp.int32, (CHUNK, 128), 0) // 4
    pick = (pick == lax.broadcasted_iota(jnp.int32, (CHUNK, 128), 1)).astype(F32).astype(BF16)
    upper = lax.broadcasted_iota(jnp.int32, (64, 8, 128), 1) < 4

    def by_lanes(part):
        return jnp.concatenate([part[:, :, 128 * k : 128 * k + 128] for k in range(BLOCKS)], axis=1)

    for step in range(STEPS):
        hidden = slice(CHUNK * step, CHUNK * step + CHUNK)
        pre_act = dot_nn(normed, w_in[:, hidden]) + b_in[:, hidden]
        cumul = 0.5 * (1.0 + lax.erf(pre_act * 0.7071067811865476))
        act = (pre_act * cumul).astype(BF16)
        slope = cumul + pre_act * jnp.exp(-0.5 * pre_act * pre_act) * 0.3989422804014327
        d_pre = (dot_nt(d_branch, w_out[hidden, :]) * slope).astype(BF16)
        branch = branch + dot_nn(act, w_out[hidden, :])
        d_normed = d_normed + dot_nt(d_pre, w_in[:, hidden])

        bias = jnp.sum(d_pre.astype(F32), axis=0, keepdims=True)
        rows_out[8:16, 128 * step : 128 * step + 128] = dot_nn(jnp.where(fourth, bias, 0.0).astype(BF16), pick)

        term = dot_tn(act, d_branch).reshape(CHUNK // 32, 2, 16, CH)
        chips = slice(CHUNK // 32 * step, CHUNK // 32 * (step + 1))
        mine_out[chips] = by_lanes(jnp.where(first, term[:, 0], term[:, 1])).astype(BF16)
        theirs_out[chips] = by_lanes(jnp.where(first, term[:, 1], term[:, 0])).astype(BF16)

        term = dot_tn(normed, d_pre).reshape(64, 8, CHUNK)
        kept, given = [], []
        for k in range(2):
            low = term[:, :, 128 * k : 128 * k + 128]
            high = term[:, :, 256 + 128 * k : 384 + 128 * k]
            zero = jnp.where(upper, low, pltpu.roll(high, 4, 1))
            one = jnp.where(upper, pltpu.roll(low, 4, 1), high)
            kept.append(jnp.where(first, zero, one))
            given.append(jnp.where(first, one, zero))
        mine_in[:, 16 * step : 16 * step + 16, :] = jnp.concatenate(kept, axis=1).astype(BF16)
        theirs_in[:, 16 * step : 16 * step + 16, :] = jnp.concatenate(given, axis=1).astype(BF16)

    d_hat = d_normed * gain
    grad = inverse * (
        d_hat
        - jnp.mean(d_hat, axis=-1, keepdims=True)
        - hat * jnp.mean(d_hat * hat, axis=-1, keepdims=True)
    )
    grad = grad.astype(BF16)
    out = grad.reshape(ROWS, COLS, CH)
    d_conv[...] = out
    d_row_one[...] = jnp.where(even_row, out[ROWS - 3 :], out[:3])
    d_row_two[...] = jnp.where(even_row, out[:3], out[ROWS - 3 :])
    block_out[...] = (tile[...].reshape(COUNT, CH).astype(F32) + scale * branch).astype(BF16)
    rows_out[0:1, :] = jnp.sum(grad.astype(F32), axis=0, keepdims=True)
    rows_out[1:2, :] = jnp.sum(d_normed * hat, axis=0, keepdims=True)
    rows_out[2:3, :] = jnp.sum(d_normed, axis=0, keepdims=True)
    rows_out[3:4, :] = jnp.sum(d_branch.astype(F32), axis=0, keepdims=True)
    rows_out[4:5, :] = jnp.sum(cot[...].astype(F32) * branch, axis=0, keepdims=True)


def grads(place, *operands):
    half = (64, 64, 128)
    return pl.pallas_call(
        grads_kernel,
        in_specs=[SCALARS] + [WHOLE] * len(operands),
        out_shape=[
            pltpu.VMEM(PAD, F32),
            jax.ShapeDtypeStruct((COUNT, CH), BF16),
            pltpu.VMEM((ROWS, COLS, CH), BF16),
            pltpu.VMEM((3, COLS, CH), BF16),
            pltpu.VMEM((3, COLS, CH), BF16),
            pltpu.VMEM((16, CH), F32),
            pltpu.VMEM(half, BF16),
            pltpu.VMEM(half, BF16),
            pltpu.VMEM(half, BF16),
            pltpu.VMEM(half, BF16),
        ],
        scratch_shapes=[pltpu.VMEM(TILE, F32)],
        compiler_params=params(),
        cost_estimate=cost(3_200_000_000, 12_000_000),
        name="grads",
    )(place, *(near(value) for value in operands))


def taps_kernel(place, pad, d_conv, rows, keep, give, d_tile, table):
    for k in range(BLOCKS):
        d_tile[k] = d_conv[:, :, 128 * k : 128 * k + 128].astype(F32)
    table[48:128, :] = jnp.zeros((80, CH), F32)

    def block(cb, carry):
        lanes = lanes_of(cb)
        for s in range(7):
            totals = [jnp.zeros((8, 128), F32) for _ in range(7)]
            for cg in range(COLS // 8):
                band = pad[cb, :, 8 * cg + s : 8 * cg + s + 8, :]
                own = d_tile[cb, :, 8 * cg : 8 * cg + 8, :]
                for r in range(7):
                    totals[r] = totals[r] + jnp.sum(band[r : r + ROWS] * own, axis=0)
            for r in range(7):
                table[7 * r + s : 7 * r + s + 1, lanes] = jnp.sum(totals[r], axis=0, keepdims=True)
        return carry

    lax.fori_loop(0, BLOCKS, block, 0)
    table[49:54, :] = rows[0:5, :]
    table[54:58, :] = rows[8:12, :]
    turned = table[...].T.reshape(16, 2, 2, 8, 128)
    even = place[2] == 0
    keep[...] = jnp.where(even, turned[:, 0], turned[:, 1]).reshape(32, 8, 128).astype(BF16)
    give[...] = jnp.where(even, turned[:, 1], turned[:, 0]).reshape(32, 8, 128).astype(BF16)


def tap_rows(place, *operands):
    return pl.pallas_call(
        taps_kernel,
        in_specs=[SCALARS] + [WHOLE] * len(operands),
        out_shape=[pltpu.VMEM((32, 8, 128), BF16)] * 2,
        scratch_shapes=[pltpu.VMEM(TILE, F32), pltpu.VMEM((128, CH), F32)],
        compiler_params=params(),
        cost_estimate=cost(30_000_000, 2_000_000),
        name="tap_rows",
    )(place, *(near(value) for value in operands))


def split_kernel(place, out_one, out_two, in_one, in_two, keep, give):
    even = place[2] == 0
    for at, one, two in ((0, out_one, out_two), (64, in_one, in_two)):
        for k in range(16):
            total = [(one[4 * k + 2 * p : 4 * k + 2 * p + 2] + two[4 * k + 2 * p : 4 * k + 2 * p + 2]) for p in range(2)]
            keep[2 * k : 2 * k + 2, at : at + 64, :] = jnp.where(even, total[0], total[1])
            give[2 * k : 2 * k + 2, at : at + 64, :] = jnp.where(even, total[1], total[0])


def split_pair(place, *operands):
    return pl.pallas_call(
        split_kernel,
        in_specs=[SCALARS] + [WHOLE] * len(operands),
        out_shape=[pltpu.VMEM((32, 128, 128), BF16)] * 2,
        compiler_params=params(),
        cost_estimate=cost(1_000_000, 6_000_000),
        name="split_pair",
    )(place, *(near(value) for value in operands))


def add_kernel(one, two, small_one, small_two, small_three, small_four, total):
    total[:, 0:128, :] = one[...] + two[...]
    small = small_one[...].astype(F32) + small_two[...].astype(F32)
    small = small + small_three[...].astype(F32) + small_four[...].astype(F32)
    total[:, 128:136, :] = small.astype(BF16)


def add_pair(*operands):
    return pl.pallas_call(
        add_kernel,
        in_specs=[WHOLE] * len(operands),
        out_shape=jax.ShapeDtypeStruct((32, 136, 128), BF16),
        compiler_params=params(),
        cost_estimate=cost(1_000_000, 3_000_000),
        name="add_pair",
    )(*(near(value) for value in operands))


def sum_kernel(factor, place, spread, g_in, g_out, g_channel, g_bias):
    total = jnp.sum(spread[...].astype(F32), axis=0) * factor
    for k in range(4):
        g_out[:, 128 * k : 128 * k + 128] = total[16 * k : 16 * k + 16, :]
    for t in range(STEPS):
        for k in range(2):
            own = total[64 + 16 * t + 8 * k : 72 + 16 * t + 8 * k, :]
            at = CHUNK * t + 128 * k
            g_in[:, at : at + 128] = own[0:4]
            g_in[:, at + 256 : at + 384] = own[4:8]
    small = total[128:136, :]
    small = jnp.where(place[0] == 0, small, pltpu.roll(small, 4, 0))
    g_channel[...] = small[0:4, 0:54]
    g_bias[...] = jnp.concatenate([small[k : k + 1, 54:58] for k in range(4)], axis=1)


def sum_chips(place, spread, factor):
    shape = jax.ShapeDtypeStruct
    return pl.pallas_call(
        lambda *refs: sum_kernel(factor, *refs),
        in_specs=[pl.BlockSpec(memory_space=pltpu.SMEM), pl.BlockSpec(memory_space=pltpu.VMEM)],
        out_shape=[shape((4, HID), F32), shape((16, CH), F32), shape((4, 54), F32), shape((1, 16), F32)],
        compiler_params=pltpu.CompilerParams(vmem_limit_bytes=16 * 1024 * 1024),
        cost_estimate=pl.CostEstimate(flops=1_000_000, bytes_accessed=1_000_000, transcendentals=0),
        name="sum_chips",
    )(place, spread)


def features_kernel(place, d_conv, row_one, row_two, col_one, col_two, cot, taps, out, pad, total):
    assemble(pad, d_conv, row_one, row_two, col_one, col_two, place[1] == 0, place[0] == 0)
    depthwise(pad, taps, total, True)
    cot_wide = cot[...].astype(F32).reshape(ROWS, COLS, CH)
    for k in range(BLOCKS):
        lanes = slice(128 * k, 128 * k + 128)
        out[:, :, lanes] = (cot_wide[:, :, lanes] + total[k]).astype(BF16)


def features_part(place, *operands):
    return pl.pallas_call(
        features_kernel,
        in_specs=[SCALARS] + [WHOLE] * len(operands),
        out_shape=jax.ShapeDtypeStruct((ROWS, COLS, CH), BF16),
        scratch_shapes=[pltpu.VMEM(PAD, F32), pltpu.VMEM(TILE, F32)],
        compiler_params=params(),
        cost_estimate=cost(30_000_000, 2_000_000),
        name="features_part",
    )(place, *(near(value) for value in operands))


def exchange(one, two, axis):
    count = lax.axis_size(axis)
    met = []
    for value, start in ((one, 0), (two, 1)):
        pairs = []
        for i in range(start, count - 1, 2):
            pairs += [(i, i + 1), (i + 1, i)]
        met.append(lax.ppermute(value, axis, pairs))
    return met


def halo_sides(row_one, row_two, tile, even_row, even_col):
    top = jnp.where(even_row, row_two, row_one)
    bottom = jnp.where(even_row, row_one, row_two)
    tail = jnp.concatenate([part[:, COLS - 3 :] for part in (top, tile, bottom)], axis=0)
    head = jnp.concatenate([part[:, :3] for part in (top, tile, bottom)], axis=0)
    return jnp.where(even_col, tail, head), jnp.where(even_col, head, tail)


def swap_cores(value):
    return lax.ppermute(value, "c", [(0, 1), (1, 0)])


def swap_chips(value):
    pairs = []
    for x in range(4):
        pairs += [(2 * x, 2 * (x ^ 1)), (2 * x + 1, 2 * (3 - x) + 1)]
    return lax.ppermute(value, ("xh", "xl", "c"), pairs)


def swap_across(value):
    pairs = []
    for x in range(4):
        pairs += [(2 * x, 2 * (3 - x) + 1), (2 * x + 1, 2 * (x ^ 1))]
    return lax.ppermute(value, ("xh", "xl", "c"), pairs)


def shards(
    features, cotangent, dw_kernel, dw_bias, norm_gain_vector, norm_bias,
    pw_in_weight, pw_in_bias, pw_out_weight, pw_out_bias, layer_scale,
):
    factor = 1.0 / math.sqrt(COUNT * lax.axis_size(EVERY))
    core, y_hi, x_lo = (lax.axis_index(name).astype(jnp.int32) for name in ("c", "yh", "xl"))
    place = jnp.stack([core, y_hi, x_lo])
    even_row, even_col = y_hi == 0, core == 0
    vectors = jnp.stack([dw_bias, norm_gain_vector, norm_bias, layer_scale, pw_out_bias])
    ends = features[:3], features[ROWS - 3 :]
    rows_met = exchange(jnp.where(even_row, ends[1], ends[0]), jnp.where(even_row, ends[0], ends[1]), ROW)
    tile, cot, taps, vectors, w_in, b_in, w_out = fetch(
        features, cotangent.reshape(COUNT, CH), dw_kernel, vectors, pw_in_weight,
        pw_in_bias.reshape(1, HID), pw_out_weight,
    )
    sides = halo_sides(*rows_met, features, even_row, even_col)
    sides, w_in = lax.optimization_barrier((sides, w_in))
    cols_met = exchange(*sides, COL)
    pad, block_rows, d_conv, d_one, d_two, rows, mine_out, theirs_out, mine_in, theirs_in = grads(
        place, tile, *rows_met, *cols_met, cot, taps, vectors, w_in, b_in, w_out
    )
    met_out, met_in = swap_cores(theirs_out), swap_cores(theirs_in)
    small_keep, small_give = tap_rows(place, pad, d_conv, rows)
    met_out, met_in, small_keep, small_give = lax.optimization_barrier((met_out, met_in, small_keep, small_give))
    keep, give = split_pair(place, mine_out, met_out, mine_in, met_in)
    given = swap_chips(give)
    small_keep, small_give, give, d_one, d_two = lax.optimization_barrier((small_keep, small_give, give, d_one, d_two))
    smalls = small_keep, swap_cores(small_keep), swap_chips(small_give), swap_across(small_give)
    d_rows = exchange(d_one, d_two, ROW)
    d_cols = exchange(*halo_sides(*d_rows, d_conv, even_row, even_col), COL)
    smalls, d_cols = lax.optimization_barrier((smalls, d_cols))
    message = add_pair(keep, given, *smalls)
    spread = lax.all_to_all(message, GROUP, 0, 0, tiled=True)
    d_conv, message = lax.optimization_barrier((d_conv, message))
    grad_features = features_part(place, d_conv, *d_rows, *d_cols, cot, taps)
    grad_in, grad_out, grad_channel, grad_bias = sum_chips(place, spread, factor)
    return (
        block_rows.reshape(ROWS, COLS, CH),
        grad_features,
        grad_in,
        grad_out,
        grad_channel.T,
        grad_bias.reshape(-1),
    )


def solution(mesh):
    fine = Mesh(mesh.devices.reshape(4, 2, 2, 2, 2, 2), EVERY)
    return jax.shard_map(
        shards,
        mesh=fine,
        in_specs=(P(ROW, COL, None), P(ROW, COL, None)) + (P(),) * 9,
        out_specs=(
            P(ROW, COL, None),
            P(ROW, COL, None),
            P(EVERY, None),
            P(EVERY, None),
            P(None, EVERY),
            P(EVERY),
        ),
        check_vma=False,
    )
```

```python
import math

import jax
import jax.numpy as jnp
from jax import lax
from jax.experimental import pallas as pl
from jax.experimental.pallas import tpu as pltpu
from jax.sharding import Mesh
from jax.sharding import PartitionSpec as P

EVERY = ("zh", "zl", "yh", "xh", "xl", "yl", "c")
ROW = ("zh", "zl", "yh")
COL = ("xh", "xl", "yl", "c")
GROUP = ("zh", "yh", "xh", "yl")
ROWS, COLS, CH, HID, CHUNK = 8, 32, 512, 2048, 512
COUNT = ROWS * COLS
STEPS = HID // CHUNK
BLOCKS = CH // 128
PAD = (BLOCKS, ROWS + 6, COLS + 8, 128)
TILE = (BLOCKS, ROWS, COLS, 128)
F32, BF16 = jnp.float32, jnp.bfloat16
VMEM_BYTES = 28 * 1024 * 1024


def dot_nn(left, right):
    return lax.dot_general(left, right, (((1,), (0,)), ((), ())), preferred_element_type=F32)


def dot_nt(left, right):
    return lax.dot_general(left, right, (((1,), (1,)), ((), ())), preferred_element_type=F32)


def dot_tn(left, right):
    return lax.dot_general(left, right, (((0,), (0,)), ((), ())), preferred_element_type=F32)


def params(vmem=VMEM_BYTES):
    return pltpu.CompilerParams(vmem_limit_bytes=vmem)


def cost(flops, moved):
    return pl.CostEstimate(flops=flops, bytes_accessed=moved, transcendentals=0)


def near(value):
    return pltpu.with_memory_space_constraint(value, pltpu.VMEM)


SCALARS = pl.BlockSpec(memory_space=pltpu.SMEM)
WHOLE = pl.BlockSpec(memory_space=pltpu.VMEM)


def fetch_kernel(count, *refs):
    sources, targets, sem = refs[:count], refs[count : 2 * count], refs[2 * count]
    copies = [pltpu.make_async_copy(sources[k], targets[k], sem.at[k]) for k in range(count)]
    for copy in copies:
        copy.start()
    for copy in copies:
        copy.wait()


def fetch(*arrays):
    count = len(arrays)
    return pl.pallas_call(
        lambda *refs: fetch_kernel(count, *refs),
        in_specs=[pl.BlockSpec(memory_space=pltpu.HBM)] * count,
        out_specs=[WHOLE] * count,
        out_shape=[pltpu.VMEM(array.shape, array.dtype) for array in arrays],
        scratch_shapes=[pltpu.SemaphoreType.DMA((count,))],
        compiler_params=params(),
        cost_estimate=cost(0, 5_000_000),
        name="fetch",
    )(*(pltpu.with_memory_space_constraint(array, pltpu.HBM) for array in arrays))


def assemble(pad, tile, row_one, row_two, col_one, col_two, even_row, even_col):
    for k in range(BLOCKS):
        lanes = slice(128 * k, 128 * k + 128)
        rows = row_one[:, :, lanes].astype(F32), row_two[:, :, lanes].astype(F32)
        cols = col_one[:, :, lanes].astype(F32), col_two[:, :, lanes].astype(F32)
        pad[k, 0:3, 3 : 3 + COLS, :] = jnp.where(even_row, rows[1], rows[0])
        pad[k, 3 : 3 + ROWS, 3 : 3 + COLS, :] = tile[:, :, lanes].astype(F32)
        pad[k, 3 + ROWS : 6 + ROWS, 3 : 3 + COLS, :] = jnp.where(even_row, rows[0], rows[1])
        pad[k, :, 0:3, :] = jnp.where(even_col, cols[1], cols[0])
        pad[k, :, 3 + COLS : 6 + COLS, :] = jnp.where(even_col, cols[0], cols[1])


def lanes_of(block):
    return pl.ds(pl.multiple_of(block * 128, 128), 128)


def depthwise(pad, taps, out, flip):
    def block(cb, carry):
        lanes = lanes_of(cb)
        for cg in range(COLS // 8):
            total = jnp.zeros((ROWS, 8, 128), F32)
            for s in range(7):
                band = pad[cb, :, 8 * cg + s : 8 * cg + s + 8, :]
                for r in range(7):
                    tap = 7 * (6 - r) + 6 - s if flip else 7 * r + s
                    total = total + band[r : r + ROWS] * taps[tap : tap + 1, lanes].reshape(1, 1, 128)
            out[cb, :, 8 * cg : 8 * cg + 8, :] = total
        return carry

    lax.fori_loop(0, BLOCKS, block, 0)


def grads_kernel(
    place, tile, row_one, row_two, col_one, col_two, cot, taps, vectors, w_in, b_in, w_out,
    pad, block_out, d_conv, d_row_one, d_row_two, rows_out, mine_out, theirs_out, mine_in, theirs_in,
    conv,
):
    first = place[0] == 0
    even_row = place[1] == 0
    assemble(pad, tile, row_one, row_two, col_one, col_two, even_row, first)
    depthwise(pad, taps, conv, False)
    dw_bias, gain, shift, scale, b_out = (vectors[k : k + 1, :] for k in range(5))
    rows = jnp.concatenate([conv[k].reshape(COUNT, 128) for k in range(BLOCKS)], axis=1) + dw_bias
    centred = rows - jnp.mean(rows, axis=-1, keepdims=True)
    inverse = lax.rsqrt(jnp.mean(centred * centred, axis=-1, keepdims=True) + 1e-06)
    hat = centred * inverse
    normed = (hat * gain + shift).astype(BF16)
    d_branch = (cot[...].astype(F32) * scale).astype(BF16)
    branch = b_out
    d_normed = 0.0

    fourth = lax.broadcasted_iota(jnp.int32, (8, CHUNK), 1) % 4
    fourth = fourth == lax.broadcasted_iota(jnp.int32, (8, CHUNK), 0)
    pick = lax.broadcasted_iota(jnp.int32, (CHUNK, 128), 0) // 4
    pick = (pick == lax.broadcasted_iota(jnp.int32, (CHUNK, 128), 1)).astype(F32).astype(BF16)
    upper = lax.broadcasted_iota(jnp.int32, (64, 8, 128), 1) < 4

    def by_lanes(part):
        return jnp.concatenate([part[:, :, 128 * k : 128 * k + 128] for k in range(BLOCKS)], axis=1)

    for step in range(STEPS):
        hidden = slice(CHUNK * step, CHUNK * step + CHUNK)
        pre_act = dot_nn(normed, w_in[:, hidden]) + b_in[:, hidden]
        cumul = 0.5 * (1.0 + lax.erf(pre_act * 0.7071067811865476))
        act = (pre_act * cumul).astype(BF16)
        slope = cumul + pre_act * jnp.exp(-0.5 * pre_act * pre_act) * 0.3989422804014327
        d_pre = (dot_nt(d_branch, w_out[hidden, :]) * slope).astype(BF16)
        branch = branch + dot_nn(act, w_out[hidden, :])
        d_normed = d_normed + dot_nt(d_pre, w_in[:, hidden])

        bias = jnp.sum(d_pre.astype(F32), axis=0, keepdims=True)
        rows_out[8:16, 128 * step : 128 * step + 128] = dot_nn(jnp.where(fourth, bias, 0.0).astype(BF16), pick)

        term = dot_tn(act, d_branch).reshape(CHUNK // 32, 2, 16, CH)
        chips = slice(CHUNK // 32 * step, CHUNK // 32 * (step + 1))
        mine_out[chips] = by_lanes(jnp.where(first, term[:, 0], term[:, 1])).astype(BF16)
        theirs_out[chips] = by_lanes(jnp.where(first, term[:, 1], term[:, 0])).astype(BF16)

        term = dot_tn(normed, d_pre).reshape(64, 8, CHUNK)
        kept, given = [], []
        for k in range(2):
            low = term[:, :, 128 * k : 128 * k + 128]
            high = term[:, :, 256 + 128 * k : 384 + 128 * k]
            zero = jnp.where(upper, low, pltpu.roll(high, 4, 1))
            one = jnp.where(upper, pltpu.roll(low, 4, 1), high)
            kept.append(jnp.where(first, zero, one))
            given.append(jnp.where(first, one, zero))
        mine_in[:, 16 * step : 16 * step + 16, :] = jnp.concatenate(kept, axis=1).astype(BF16)
        theirs_in[:, 16 * step : 16 * step + 16, :] = jnp.concatenate(given, axis=1).astype(BF16)

    d_hat = d_normed * gain
    grad = inverse * (
        d_hat
        - jnp.mean(d_hat, axis=-1, keepdims=True)
        - hat * jnp.mean(d_hat * hat, axis=-1, keepdims=True)
    )
    grad = grad.astype(BF16)
    out = grad.reshape(ROWS, COLS, CH)
    d_conv[...] = out
    d_row_one[...] = jnp.where(even_row, out[ROWS - 3 :], out[:3])
    d_row_two[...] = jnp.where(even_row, out[:3], out[ROWS - 3 :])
    block_out[...] = (tile[...].reshape(COUNT, CH).astype(F32) + scale * branch).astype(BF16)
    rows_out[0:1, :] = jnp.sum(grad.astype(F32), axis=0, keepdims=True)
    rows_out[1:2, :] = jnp.sum(d_normed * hat, axis=0, keepdims=True)
    rows_out[2:3, :] = jnp.sum(d_normed, axis=0, keepdims=True)
    rows_out[3:4, :] = jnp.sum(d_branch.astype(F32), axis=0, keepdims=True)
    rows_out[4:5, :] = jnp.sum(cot[...].astype(F32) * branch, axis=0, keepdims=True)


def grads(place, *operands):
    half = (64, 64, 128)
    return pl.pallas_call(
        grads_kernel,
        in_specs=[SCALARS] + [WHOLE] * len(operands),
        out_shape=[
            pltpu.VMEM(PAD, F32),
            jax.ShapeDtypeStruct((COUNT, CH), BF16),
            pltpu.VMEM((ROWS, COLS, CH), BF16),
            pltpu.VMEM((3, COLS, CH), BF16),
            pltpu.VMEM((3, COLS, CH), BF16),
            pltpu.VMEM((16, CH), F32),
            pltpu.VMEM(half, BF16),
            pltpu.VMEM(half, BF16),
            pltpu.VMEM(half, BF16),
            pltpu.VMEM(half, BF16),
        ],
        scratch_shapes=[pltpu.VMEM(TILE, F32)],
        compiler_params=params(),
        cost_estimate=cost(3_200_000_000, 12_000_000),
        name="grads",
    )(place, *(near(value) for value in operands))


def taps_kernel(place, pad, d_conv, rows, keep, give, d_tile, table):
    for k in range(BLOCKS):
        d_tile[k] = d_conv[:, :, 128 * k : 128 * k + 128].astype(F32)
    table[48:128, :] = jnp.zeros((80, CH), F32)

    def block(cb, carry):
        lanes = lanes_of(cb)
        for s in range(7):
            totals = [jnp.zeros((8, 128), F32) for _ in range(7)]
            for cg in range(COLS // 8):
                band = pad[cb, :, 8 * cg + s : 8 * cg + s + 8, :]
                own = d_tile[cb, :, 8 * cg : 8 * cg + 8, :]
                for r in range(7):
                    totals[r] = totals[r] + jnp.sum(band[r : r + ROWS] * own, axis=0)
            for r in range(7):
                table[7 * r + s : 7 * r + s + 1, lanes] = jnp.sum(totals[r], axis=0, keepdims=True)
        return carry

    lax.fori_loop(0, BLOCKS, block, 0)
    table[49:54, :] = rows[0:5, :]
    table[54:58, :] = rows[8:12, :]
    turned = table[...].T.reshape(16, 2, 2, 8, 128)
    even = place[2] == 0
    keep[...] = jnp.where(even, turned[:, 0], turned[:, 1]).reshape(32, 8, 128).astype(BF16)
    give[...] = jnp.where(even, turned[:, 1], turned[:, 0]).reshape(32, 8, 128).astype(BF16)


def tap_rows(place, *operands):
    return pl.pallas_call(
        taps_kernel,
        in_specs=[SCALARS] + [WHOLE] * len(operands),
        out_shape=[pltpu.VMEM((32, 8, 128), BF16)] * 2,
        scratch_shapes=[pltpu.VMEM(TILE, F32), pltpu.VMEM((128, CH), F32)],
        compiler_params=params(),
        cost_estimate=cost(30_000_000, 2_000_000),
        name="tap_rows",
    )(place, *(near(value) for value in operands))


def split_kernel(place, out_one, out_two, in_one, in_two, keep, give):
    even = place[2] == 0
    for at, one, two in ((0, out_one, out_two), (64, in_one, in_two)):
        for k in range(16):
            total = [(one[4 * k + 2 * p : 4 * k + 2 * p + 2] + two[4 * k + 2 * p : 4 * k + 2 * p + 2]) for p in range(2)]
            keep[2 * k : 2 * k + 2, at : at + 64, :] = jnp.where(even, total[0], total[1])
            give[2 * k : 2 * k + 2, at : at + 64, :] = jnp.where(even, total[1], total[0])


def split_pair(place, *operands):
    return pl.pallas_call(
        split_kernel,
        in_specs=[SCALARS] + [WHOLE] * len(operands),
        out_shape=[pltpu.VMEM((32, 128, 128), BF16)] * 2,
        compiler_params=params(),
        cost_estimate=cost(1_000_000, 6_000_000),
        name="split_pair",
    )(place, *(near(value) for value in operands))


def add_kernel(place, one, two, small_one, small_two, small_three, small_four, keep, give):
    even = place[3] == 0
    small = small_one[...].astype(F32) + small_two[...].astype(F32)
    small = (small + small_three[...].astype(F32) + small_four[...].astype(F32)).astype(BF16)
    for k in range(2):
        at = slice(8 * k, 8 * k + 8)
        low, high = slice(16 * k, 16 * k + 8), slice(16 * k + 8, 16 * k + 16)
        total = one[low] + two[low], one[high] + two[high]
        keep[at, 0:128, :] = jnp.where(even, total[0], total[1])
        give[at, 0:128, :] = jnp.where(even, total[1], total[0])
        keep[at, 128:136, :] = jnp.where(even, small[low], small[high])
        give[at, 128:136, :] = jnp.where(even, small[high], small[low])


def add_pair(place, *operands):
    return pl.pallas_call(
        add_kernel,
        in_specs=[SCALARS] + [WHOLE] * len(operands),
        out_shape=[pltpu.VMEM((16, 136, 128), BF16)] * 2,
        compiler_params=params(),
        cost_estimate=cost(1_000_000, 3_000_000),
        name="add_pair",
    )(place, *(near(value) for value in operands))


def add_last_kernel(one, two, total):
    total[...] = one[...] + two[...]


def add_last(*operands):
    return pl.pallas_call(
        add_last_kernel,
        in_specs=[WHOLE] * 2,
        out_shape=pltpu.VMEM((16, 136, 128), BF16),
        compiler_params=params(),
        cost_estimate=cost(1_000_000, 1_000_000),
        name="add_last",
    )(*(near(value) for value in operands))


def sum_kernel(factor, place, spread, g_in, g_out, g_channel, g_bias):
    total = jnp.sum(spread[...].astype(F32), axis=0) * factor
    for k in range(4):
        g_out[:, 128 * k : 128 * k + 128] = total[16 * k : 16 * k + 16, :]
    for t in range(STEPS):
        for k in range(2):
            own = total[64 + 16 * t + 8 * k : 72 + 16 * t + 8 * k, :]
            at = CHUNK * t + 128 * k
            g_in[:, at : at + 128] = own[0:4]
            g_in[:, at + 256 : at + 384] = own[4:8]
    small = total[128:136, :]
    small = jnp.where(place[0] == 0, small, pltpu.roll(small, 4, 0))
    g_channel[...] = small[0:4, 0:54]
    g_bias[...] = jnp.concatenate([small[k : k + 1, 54:58] for k in range(4)], axis=1)


def sum_chips(place, spread, factor):
    shape = jax.ShapeDtypeStruct
    return pl.pallas_call(
        lambda *refs: sum_kernel(factor, *refs),
        in_specs=[pl.BlockSpec(memory_space=pltpu.SMEM), pl.BlockSpec(memory_space=pltpu.VMEM)],
        out_shape=[shape((4, HID), F32), shape((16, CH), F32), shape((4, 54), F32), shape((1, 16), F32)],
        compiler_params=pltpu.CompilerParams(vmem_limit_bytes=16 * 1024 * 1024),
        cost_estimate=pl.CostEstimate(flops=1_000_000, bytes_accessed=1_000_000, transcendentals=0),
        name="sum_chips",
    )(place, spread)


def features_kernel(place, d_conv, row_one, row_two, col_one, col_two, cot, taps, out, pad, total):
    assemble(pad, d_conv, row_one, row_two, col_one, col_two, place[1] == 0, place[0] == 0)
    depthwise(pad, taps, total, True)
    cot_wide = cot[...].astype(F32).reshape(ROWS, COLS, CH)
    for k in range(BLOCKS):
        lanes = slice(128 * k, 128 * k + 128)
        out[:, :, lanes] = (cot_wide[:, :, lanes] + total[k]).astype(BF16)


def features_part(place, *operands):
    return pl.pallas_call(
        features_kernel,
        in_specs=[SCALARS] + [WHOLE] * len(operands),
        out_shape=jax.ShapeDtypeStruct((ROWS, COLS, CH), BF16),
        scratch_shapes=[pltpu.VMEM(PAD, F32), pltpu.VMEM(TILE, F32)],
        compiler_params=params(),
        cost_estimate=cost(30_000_000, 2_000_000),
        name="features_part",
    )(place, *(near(value) for value in operands))


def exchange(one, two, axis):
    count = lax.axis_size(axis)
    met = []
    for value, start in ((one, 0), (two, 1)):
        pairs = []
        for i in range(start, count - 1, 2):
            pairs += [(i, i + 1), (i + 1, i)]
        met.append(lax.ppermute(value, axis, pairs))
    return met


def halo_sides(row_one, row_two, tile, even_row, even_col):
    top = jnp.where(even_row, row_two, row_one)
    bottom = jnp.where(even_row, row_one, row_two)
    tail = jnp.concatenate([part[:, COLS - 3 :] for part in (top, tile, bottom)], axis=0)
    head = jnp.concatenate([part[:, :3] for part in (top, tile, bottom)], axis=0)
    return jnp.where(even_col, tail, head), jnp.where(even_col, head, tail)


def swap_cores(value):
    return lax.ppermute(value, "c", [(0, 1), (1, 0)])


def swap_chips(value, axes):
    pairs = []
    for at in range(4):
        pairs += [(2 * at, 2 * (at ^ 1)), (2 * at + 1, 2 * (3 - at) + 1)]
    return lax.ppermute(value, axes + ("c",), pairs)


def swap_across(value):
    pairs = []
    for x in range(4):
        pairs += [(2 * x, 2 * (3 - x) + 1), (2 * x + 1, 2 * (x ^ 1))]
    return lax.ppermute(value, ("xh", "xl", "c"), pairs)


def shards(
    features, cotangent, dw_kernel, dw_bias, norm_gain_vector, norm_bias,
    pw_in_weight, pw_in_bias, pw_out_weight, pw_out_bias, layer_scale,
):
    factor = 1.0 / math.sqrt(COUNT * lax.axis_size(EVERY))
    core, y_hi, x_lo, z_lo = (lax.axis_index(name).astype(jnp.int32) for name in ("c", "yh", "xl", "zl"))
    place = jnp.stack([core, y_hi, x_lo, z_lo])
    even_row, even_col = y_hi == 0, core == 0
    vectors = jnp.stack([dw_bias, norm_gain_vector, norm_bias, layer_scale, pw_out_bias])
    ends = features[:3], features[ROWS - 3 :]
    rows_met = exchange(jnp.where(even_row, ends[1], ends[0]), jnp.where(even_row, ends[0], ends[1]), ROW)
    tile, cot, taps, vectors, w_in, b_in, w_out = fetch(
        features, cotangent.reshape(COUNT, CH), dw_kernel, vectors, pw_in_weight,
        pw_in_bias.reshape(1, HID), pw_out_weight,
    )
    sides = halo_sides(*rows_met, features, even_row, even_col)
    sides, w_in = lax.optimization_barrier((sides, w_in))
    cols_met = exchange(*sides, COL)
    pad, block_rows, d_conv, d_one, d_two, rows, mine_out, theirs_out, mine_in, theirs_in = grads(
        place, tile, *rows_met, *cols_met, cot, taps, vectors, w_in, b_in, w_out
    )
    met_out, met_in = swap_cores(theirs_out), swap_cores(theirs_in)
    small_keep, small_give = tap_rows(place, pad, d_conv, rows)
    met_out, met_in, small_keep, small_give = lax.optimization_barrier((met_out, met_in, small_keep, small_give))
    keep, give = split_pair(place, mine_out, met_out, mine_in, met_in)
    along_x, along_z = ("xh", "xl"), ("zh", "zl")
    given = swap_chips(give, along_x)
    small_keep, small_give, give, d_one, d_two = lax.optimization_barrier((small_keep, small_give, give, d_one, d_two))
    smalls = small_keep, swap_cores(small_keep), swap_chips(small_give, along_x), swap_across(small_give)
    d_rows = exchange(d_one, d_two, ROW)
    smalls, d_rows = lax.optimization_barrier((smalls, d_rows))
    keep, give = add_pair(place, keep, given, *smalls)
    given = swap_chips(give, along_z)
    give, d_rows = lax.optimization_barrier((give, d_rows))
    d_cols = exchange(*halo_sides(*d_rows, d_conv, even_row, even_col), COL)
    given, d_cols = lax.optimization_barrier((given, d_cols))
    message = add_last(keep, given)
    spread = lax.all_to_all(message, GROUP, 0, 0, tiled=True)
    d_conv, message = lax.optimization_barrier((d_conv, message))
    grad_features = features_part(place, d_conv, *d_rows, *d_cols, cot, taps)
    grad_in, grad_out, grad_channel, grad_bias = sum_chips(place, spread, factor)
    return (
        block_rows.reshape(ROWS, COLS, CH),
        grad_features,
        grad_in,
        grad_out,
        grad_channel.T,
        grad_bias.reshape(-1),
    )


def solution(mesh):
    fine = Mesh(mesh.devices.reshape(2, 2, 2, 2, 2, 2, 2), EVERY)
    return jax.shard_map(
        shards,
        mesh=fine,
        in_specs=(P(ROW, COL, None), P(ROW, COL, None)) + (P(),) * 9,
        out_specs=(
            P(ROW, COL, None),
            P(ROW, COL, None),
            P(EVERY, None),
            P(EVERY, None),
            P(None, EVERY),
            P(EVERY),
        ),
        check_vma=False,
    )
```

```python
import itertools
import math

import jax
import jax.numpy as jnp
from jax import lax
from jax.experimental import pallas as pl
from jax.experimental.pallas import tpu as pltpu
from jax.sharding import Mesh
from jax.sharding import PartitionSpec as P

EVERY = ("zh", "zl", "yh", "xh", "xl", "yl", "c")
ROW = ("zh", "zl", "yh")
COL = ("xh", "xl", "yl", "c")
THIRDS = ((0, 48), (48, 96), (96, 136))
ROWS, COLS, CH, HID, CHUNK = 8, 32, 512, 2048, 512
COUNT = ROWS * COLS
STEPS = HID // CHUNK
BLOCKS = CH // 128
PAD = (BLOCKS, ROWS + 6, COLS + 8, 128)
TILE = (BLOCKS, ROWS, COLS, 128)
F32, BF16 = jnp.float32, jnp.bfloat16
VMEM_BYTES = 28 * 1024 * 1024


def dot_nn(left, right):
    return lax.dot_general(left, right, (((1,), (0,)), ((), ())), preferred_element_type=F32)


def dot_nt(left, right):
    return lax.dot_general(left, right, (((1,), (1,)), ((), ())), preferred_element_type=F32)


def dot_tn(left, right):
    return lax.dot_general(left, right, (((0,), (0,)), ((), ())), preferred_element_type=F32)


def params(vmem=VMEM_BYTES):
    return pltpu.CompilerParams(vmem_limit_bytes=vmem)


def cost(flops, moved):
    return pl.CostEstimate(flops=flops, bytes_accessed=moved, transcendentals=0)


def near(value):
    return pltpu.with_memory_space_constraint(value, pltpu.VMEM)


SCALARS = pl.BlockSpec(memory_space=pltpu.SMEM)
WHOLE = pl.BlockSpec(memory_space=pltpu.VMEM)


def fetch_kernel(count, *refs):
    sources, targets, sem = refs[:count], refs[count : 2 * count], refs[2 * count]
    copies = [pltpu.make_async_copy(sources[k], targets[k], sem.at[k]) for k in range(count)]
    for copy in copies:
        copy.start()
    for copy in copies:
        copy.wait()


def fetch(*arrays):
    count = len(arrays)
    return pl.pallas_call(
        lambda *refs: fetch_kernel(count, *refs),
        in_specs=[pl.BlockSpec(memory_space=pltpu.HBM)] * count,
        out_specs=[WHOLE] * count,
        out_shape=[pltpu.VMEM(array.shape, array.dtype) for array in arrays],
        scratch_shapes=[pltpu.SemaphoreType.DMA((count,))],
        compiler_params=params(),
        cost_estimate=cost(0, 5_000_000),
        name="fetch",
    )(*(pltpu.with_memory_space_constraint(array, pltpu.HBM) for array in arrays))


def assemble(pad, tile, row_one, row_two, col_one, col_two, even_row, even_col):
    for k in range(BLOCKS):
        lanes = slice(128 * k, 128 * k + 128)
        rows = row_one[:, :, lanes].astype(F32), row_two[:, :, lanes].astype(F32)
        cols = col_one[:, :, lanes].astype(F32), col_two[:, :, lanes].astype(F32)
        pad[k, 0:3, 3 : 3 + COLS, :] = jnp.where(even_row, rows[1], rows[0])
        pad[k, 3 : 3 + ROWS, 3 : 3 + COLS, :] = tile[:, :, lanes].astype(F32)
        pad[k, 3 + ROWS : 6 + ROWS, 3 : 3 + COLS, :] = jnp.where(even_row, rows[0], rows[1])
        pad[k, :, 0:3, :] = jnp.where(even_col, cols[1], cols[0])
        pad[k, :, 3 + COLS : 6 + COLS, :] = jnp.where(even_col, cols[0], cols[1])


def lanes_of(block):
    return pl.ds(pl.multiple_of(block * 128, 128), 128)


def depthwise(pad, taps, out, flip):
    def block(cb, carry):
        lanes = lanes_of(cb)
        for cg in range(COLS // 8):
            total = jnp.zeros((ROWS, 8, 128), F32)
            for s in range(7):
                band = pad[cb, :, 8 * cg + s : 8 * cg + s + 8, :]
                for r in range(7):
                    tap = 7 * (6 - r) + 6 - s if flip else 7 * r + s
                    total = total + band[r : r + ROWS] * taps[tap : tap + 1, lanes].reshape(1, 1, 128)
            out[cb, :, 8 * cg : 8 * cg + 8, :] = total
        return carry

    lax.fori_loop(0, BLOCKS, block, 0)


def grads_kernel(
    place, tile, row_one, row_two, col_one, col_two, cot, taps, vectors, w_in, b_in, w_out,
    pad, block_out, d_conv, d_row_one, d_row_two, rows_out, mine_out, theirs_out, mine_in, theirs_in,
    conv,
):
    first = place[0] == 0
    even_row = place[1] == 0
    assemble(pad, tile, row_one, row_two, col_one, col_two, even_row, first)
    depthwise(pad, taps, conv, False)
    dw_bias, gain, shift, scale, b_out = (vectors[k : k + 1, :] for k in range(5))
    rows = jnp.concatenate([conv[k].reshape(COUNT, 128) for k in range(BLOCKS)], axis=1) + dw_bias
    centred = rows - jnp.mean(rows, axis=-1, keepdims=True)
    inverse = lax.rsqrt(jnp.mean(centred * centred, axis=-1, keepdims=True) + 1e-06)
    hat = centred * inverse
    normed = (hat * gain + shift).astype(BF16)
    d_branch = (cot[...].astype(F32) * scale).astype(BF16)
    branch = b_out
    d_normed = 0.0

    fourth = lax.broadcasted_iota(jnp.int32, (8, CHUNK), 1) % 4
    fourth = fourth == lax.broadcasted_iota(jnp.int32, (8, CHUNK), 0)
    pick = lax.broadcasted_iota(jnp.int32, (CHUNK, 128), 0) // 4
    pick = (pick == lax.broadcasted_iota(jnp.int32, (CHUNK, 128), 1)).astype(F32).astype(BF16)
    upper = lax.broadcasted_iota(jnp.int32, (64, 8, 128), 1) < 4

    def by_lanes(part):
        return jnp.concatenate([part[:, :, 128 * k : 128 * k + 128] for k in range(BLOCKS)], axis=1)

    for step in range(STEPS):
        hidden = slice(CHUNK * step, CHUNK * step + CHUNK)
        pre_act = dot_nn(normed, w_in[:, hidden]) + b_in[:, hidden]
        cumul = 0.5 * (1.0 + lax.erf(pre_act * 0.7071067811865476))
        act = (pre_act * cumul).astype(BF16)
        slope = cumul + pre_act * jnp.exp(-0.5 * pre_act * pre_act) * 0.3989422804014327
        d_pre = (dot_nt(d_branch, w_out[hidden, :]) * slope).astype(BF16)
        branch = branch + dot_nn(act, w_out[hidden, :])
        d_normed = d_normed + dot_nt(d_pre, w_in[:, hidden])

        bias = jnp.sum(d_pre.astype(F32), axis=0, keepdims=True)
        rows_out[8:16, 128 * step : 128 * step + 128] = dot_nn(jnp.where(fourth, bias, 0.0).astype(BF16), pick)

        term = dot_tn(act, d_branch).reshape(CHUNK // 32, 2, 16, CH)
        chips = slice(CHUNK // 32 * step, CHUNK // 32 * (step + 1))
        mine_out[chips] = by_lanes(jnp.where(first, term[:, 0], term[:, 1])).astype(BF16)
        theirs_out[chips] = by_lanes(jnp.where(first, term[:, 1], term[:, 0])).astype(BF16)

        term = dot_tn(normed, d_pre).reshape(64, 8, CHUNK)
        kept, given = [], []
        for k in range(2):
            low = term[:, :, 128 * k : 128 * k + 128]
            high = term[:, :, 256 + 128 * k : 384 + 128 * k]
            zero = jnp.where(upper, low, pltpu.roll(high, 4, 1))
            one = jnp.where(upper, pltpu.roll(low, 4, 1), high)
            kept.append(jnp.where(first, zero, one))
            given.append(jnp.where(first, one, zero))
        mine_in[:, 16 * step : 16 * step + 16, :] = jnp.concatenate(kept, axis=1).astype(BF16)
        theirs_in[:, 16 * step : 16 * step + 16, :] = jnp.concatenate(given, axis=1).astype(BF16)

    d_hat = d_normed * gain
    grad = inverse * (
        d_hat
        - jnp.mean(d_hat, axis=-1, keepdims=True)
        - hat * jnp.mean(d_hat * hat, axis=-1, keepdims=True)
    )
    grad = grad.astype(BF16)
    out = grad.reshape(ROWS, COLS, CH)
    d_conv[...] = out
    d_row_one[...] = jnp.where(even_row, out[ROWS - 3 :], out[:3])
    d_row_two[...] = jnp.where(even_row, out[:3], out[ROWS - 3 :])
    block_out[...] = (tile[...].reshape(COUNT, CH).astype(F32) + scale * branch).astype(BF16)
    rows_out[0:1, :] = jnp.sum(grad.astype(F32), axis=0, keepdims=True)
    rows_out[1:2, :] = jnp.sum(d_normed * hat, axis=0, keepdims=True)
    rows_out[2:3, :] = jnp.sum(d_normed, axis=0, keepdims=True)
    rows_out[3:4, :] = jnp.sum(d_branch.astype(F32), axis=0, keepdims=True)
    rows_out[4:5, :] = jnp.sum(cot[...].astype(F32) * branch, axis=0, keepdims=True)


def grads(place, *operands):
    half = (64, 64, 128)
    return pl.pallas_call(
        grads_kernel,
        in_specs=[SCALARS] + [WHOLE] * len(operands),
        out_shape=[
            pltpu.VMEM(PAD, F32),
            jax.ShapeDtypeStruct((COUNT, CH), BF16),
            pltpu.VMEM((ROWS, COLS, CH), BF16),
            pltpu.VMEM((3, COLS, CH), BF16),
            pltpu.VMEM((3, COLS, CH), BF16),
            pltpu.VMEM((16, CH), F32),
            pltpu.VMEM(half, BF16),
            pltpu.VMEM(half, BF16),
            pltpu.VMEM(half, BF16),
            pltpu.VMEM(half, BF16),
        ],
        scratch_shapes=[pltpu.VMEM(TILE, F32)],
        compiler_params=params(),
        cost_estimate=cost(3_200_000_000, 12_000_000),
        name="grads",
    )(place, *(near(value) for value in operands))


def taps_kernel(pad, d_conv, rows, small, d_tile, table):
    for k in range(BLOCKS):
        d_tile[k] = d_conv[:, :, 128 * k : 128 * k + 128].astype(F32)
    table[48:128, :] = jnp.zeros((80, CH), F32)

    def block(cb, carry):
        lanes = lanes_of(cb)
        for s in range(7):
            totals = [jnp.zeros((8, 128), F32) for _ in range(7)]
            for cg in range(COLS // 8):
                band = pad[cb, :, 8 * cg + s : 8 * cg + s + 8, :]
                own = d_tile[cb, :, 8 * cg : 8 * cg + 8, :]
                for r in range(7):
                    totals[r] = totals[r] + jnp.sum(band[r : r + ROWS] * own, axis=0)
            for r in range(7):
                table[7 * r + s : 7 * r + s + 1, lanes] = jnp.sum(totals[r], axis=0, keepdims=True)
        return carry

    lax.fori_loop(0, BLOCKS, block, 0)
    table[49:54, :] = rows[0:5, :]
    table[54:58, :] = rows[8:12, :]
    small[...] = table[...].T.reshape(64, 8, 128)


def tap_rows(*operands):
    return pl.pallas_call(
        taps_kernel,
        in_specs=[WHOLE] * len(operands),
        out_shape=pltpu.VMEM((64, 8, 128), F32),
        scratch_shapes=[pltpu.VMEM(TILE, F32), pltpu.VMEM((128, CH), F32)],
        compiler_params=params(),
        cost_estimate=cost(30_000_000, 2_000_000),
        name="tap_rows",
    )(*(near(value) for value in operands))


def split_kernel(place, out_one, out_two, in_one, in_two, small_one, small_two, keep, *gives):
    even = place[2] == 0

    for k in range(32):
        kept, given = [], []
        for part in range(2):
            q = 2 * k + part
            rows = [out_one[q] + out_two[q], in_one[q] + in_two[q], (small_one[q] + small_two[q]).astype(BF16)]
            kept.append(rows)
        if (k ^ (k >> 3)) & 1:
            kept.reverse()
        at = 0
        for low, high in zip(*kept):
            size = low.shape[0]
            mine, theirs = jnp.where(even, low, high), jnp.where(even, high, low)
            keep[k, at : at + size, :] = mine
            for give, (start, end) in zip(gives, THIRDS):
                first, last = max(start, at), min(end, at + size)
                if first < last:
                    give[k, first - start : last - start, :] = theirs[first - at : last - at]
            at += size


def split_pair(place, *operands):
    return pl.pallas_call(
        split_kernel,
        in_specs=[SCALARS] + [WHOLE] * len(operands),
        out_shape=[pltpu.VMEM((32, 136, 128), BF16)]
        + [pltpu.VMEM((32, end - start, 128), BF16) for start, end in THIRDS],
        compiler_params=params(),
        cost_estimate=cost(1_000_000, 6_000_000),
        name="split_pair",
    )(place, *(near(value) for value in operands))


def add_kernel(keep, one, two, three, total):
    for given, (start, end) in zip((one, two, three), THIRDS):
        total[:, start:end, :] = keep[:, start:end, :] + given[...]


def add_pair(*operands):
    return pl.pallas_call(
        add_kernel,
        in_specs=[WHOLE] * len(operands),
        out_shape=jax.ShapeDtypeStruct((32, 136, 128), BF16),
        compiler_params=params(),
        cost_estimate=cost(1_000_000, 3_000_000),
        name="add_pair",
    )(*(near(value) for value in operands))


def sum_kernel(factor, place, spread, g_in, g_out, g_channel, g_bias):
    total = jnp.sum(spread[...].astype(F32), axis=0) * factor
    for k in range(4):
        g_out[:, 128 * k : 128 * k + 128] = total[16 * k : 16 * k + 16, :]
    for t in range(STEPS):
        for k in range(2):
            own = total[64 + 16 * t + 8 * k : 72 + 16 * t + 8 * k, :]
            at = CHUNK * t + 128 * k
            g_in[:, at : at + 128] = own[0:4]
            g_in[:, at + 256 : at + 384] = own[4:8]
    small = total[128:136, :]
    small = jnp.where(place[0] == 0, small, pltpu.roll(small, 4, 0))
    g_channel[...] = small[0:4, 0:54]
    g_bias[...] = jnp.concatenate([small[k : k + 1, 54:58] for k in range(4)], axis=1)


def sum_chips(place, spread, factor):
    shape = jax.ShapeDtypeStruct
    return pl.pallas_call(
        lambda *refs: sum_kernel(factor, *refs),
        in_specs=[pl.BlockSpec(memory_space=pltpu.SMEM), pl.BlockSpec(memory_space=pltpu.VMEM)],
        out_shape=[shape((4, HID), F32), shape((16, CH), F32), shape((4, 54), F32), shape((1, 16), F32)],
        compiler_params=pltpu.CompilerParams(vmem_limit_bytes=16 * 1024 * 1024),
        cost_estimate=pl.CostEstimate(flops=1_000_000, bytes_accessed=1_000_000, transcendentals=0),
        name="sum_chips",
    )(place, spread)


def features_kernel(place, d_conv, row_one, row_two, col_one, col_two, cot, taps, out, pad, total):
    assemble(pad, d_conv, row_one, row_two, col_one, col_two, place[1] == 0, place[0] == 0)
    depthwise(pad, taps, total, True)
    cot_wide = cot[...].astype(F32).reshape(ROWS, COLS, CH)
    for k in range(BLOCKS):
        lanes = slice(128 * k, 128 * k + 128)
        out[:, :, lanes] = (cot_wide[:, :, lanes] + total[k]).astype(BF16)


def features_part(place, *operands):
    return pl.pallas_call(
        features_kernel,
        in_specs=[SCALARS] + [WHOLE] * len(operands),
        out_shape=jax.ShapeDtypeStruct((ROWS, COLS, CH), BF16),
        scratch_shapes=[pltpu.VMEM(PAD, F32), pltpu.VMEM(TILE, F32)],
        compiler_params=params(),
        cost_estimate=cost(30_000_000, 2_000_000),
        name="features_part",
    )(place, *(near(value) for value in operands))


def exchange(one, two, axis):
    count = lax.axis_size(axis)
    met = []
    for value, start in ((one, 0), (two, 1)):
        pairs = []
        for i in range(start, count - 1, 2):
            pairs += [(i, i + 1), (i + 1, i)]
        met.append(lax.ppermute(value, axis, pairs))
    return met


def halo_sides(row_one, row_two, tile, even_row, even_col):
    top = jnp.where(even_row, row_two, row_one)
    bottom = jnp.where(even_row, row_one, row_two)
    tail = jnp.concatenate([part[:, COLS - 3 :] for part in (top, tile, bottom)], axis=0)
    head = jnp.concatenate([part[:, :3] for part in (top, tile, bottom)], axis=0)
    return jnp.where(even_col, tail, head), jnp.where(even_col, head, tail)


def swap_cores(value):
    return lax.ppermute(value, "c", [(0, 1), (1, 0)])


def places():
    for zh, zl, yh, xh, xl, yl, core in itertools.product(range(2), repeat=7):
        yield 2 * zh + zl, 2 * yh + yl, 2 * xh + xl, core


def swap_chips(value, axis):
    known = list(places())
    pairs = []
    for at, place in enumerate(known):
        met = list(place)
        met[axis] = 3 - met[axis] if place[3] else met[axis] ^ 1
        pairs.append((at, known.index(tuple(met))))
    return lax.ppermute(value, EVERY, pairs)


def spread_chips(value):
    groups = {}
    for at, (z, y, x, core) in enumerate(places()):
        groups.setdefault(((z + y + x) % 2, core), []).append(at)
    return lax.all_to_all(value, EVERY, 0, 0, axis_index_groups=list(groups.values()), tiled=True)


def shards(
    features, cotangent, dw_kernel, dw_bias, norm_gain_vector, norm_bias,
    pw_in_weight, pw_in_bias, pw_out_weight, pw_out_bias, layer_scale,
):
    factor = 1.0 / math.sqrt(COUNT * lax.axis_size(EVERY))
    core, y_hi, y_lo, x_lo, z_lo = (lax.axis_index(name).astype(jnp.int32) for name in ("c", "yh", "yl", "xl", "zl"))
    place = jnp.stack([core, y_hi, (x_lo + y_lo + z_lo) % 2])
    even_row, even_col = y_hi == 0, core == 0
    vectors = jnp.stack([dw_bias, norm_gain_vector, norm_bias, layer_scale, pw_out_bias])
    ends = features[:3], features[ROWS - 3 :]
    rows_met = exchange(jnp.where(even_row, ends[1], ends[0]), jnp.where(even_row, ends[0], ends[1]), ROW)
    tile, cot, taps, vectors, w_in, b_in, w_out = fetch(
        features, cotangent.reshape(COUNT, CH), dw_kernel, vectors, pw_in_weight,
        pw_in_bias.reshape(1, HID), pw_out_weight,
    )
    sides = halo_sides(*rows_met, features, even_row, even_col)
    sides, w_in = lax.optimization_barrier((sides, w_in))
    cols_met = exchange(*sides, COL)
    pad, block_rows, d_conv, d_one, d_two, rows, mine_out, theirs_out, mine_in, theirs_in = grads(
        place, tile, *rows_met, *cols_met, cot, taps, vectors, w_in, b_in, w_out
    )
    met_out, met_in = swap_cores(theirs_out), swap_cores(theirs_in)
    small = tap_rows(pad, d_conv, rows)
    keep, *gives = split_pair(place, mine_out, met_out, mine_in, met_in, small, swap_cores(small))
    given = [swap_chips(give, axis) for axis, give in enumerate(gives)]
    gives, d_one, d_two = lax.optimization_barrier((gives, d_one, d_two))
    d_rows = exchange(d_one, d_two, ROW)
    d_cols = exchange(*halo_sides(*d_rows, d_conv, even_row, even_col), COL)
    given, d_cols = lax.optimization_barrier((given, d_cols))
    message = add_pair(keep, *given)
    spread = spread_chips(message)
    d_conv, message = lax.optimization_barrier((d_conv, message))
    grad_features = features_part(place, d_conv, *d_rows, *d_cols, cot, taps)
    grad_in, grad_out, grad_channel, grad_bias = sum_chips(place, spread, factor)
    return (
        block_rows.reshape(ROWS, COLS, CH),
        grad_features,
        grad_in,
        grad_out,
        grad_channel.T,
        grad_bias.reshape(-1),
    )


def solution(mesh):
    fine = Mesh(mesh.devices.reshape(2, 2, 2, 2, 2, 2, 2), EVERY)
    return jax.shard_map(
        shards,
        mesh=fine,
        in_specs=(P(ROW, COL, None), P(ROW, COL, None)) + (P(),) * 9,
        out_specs=(
            P(ROW, COL, None),
            P(ROW, COL, None),
            P(EVERY, None),
            P(EVERY, None),
            P(None, EVERY),
            P(EVERY),
        ),
        check_vma=False,
    )
```

```python
import itertools
import math

import jax
import jax.numpy as jnp
from jax import lax
from jax.experimental import pallas as pl
from jax.experimental.pallas import tpu as pltpu
from jax.sharding import Mesh
from jax.sharding import PartitionSpec as P

EVERY = ("zh", "zl", "yh", "xh", "xl", "yl", "c")
ROW = ("zh", "zl", "yh")
COL = ("xh", "xl", "yl", "c")
THIRDS = ((0, 48), (48, 96), (96, 136))
ROWS, COLS, CH, HID, CHUNK = 8, 32, 512, 2048, 512
COUNT = ROWS * COLS
STEPS = HID // CHUNK
BLOCKS = CH // 128
PAD = (BLOCKS, ROWS + 6, COLS + 8, 128)
TILE = (BLOCKS, ROWS, COLS, 128)
F32, BF16 = jnp.float32, jnp.bfloat16
VMEM_BYTES = 28 * 1024 * 1024


def dot_nn(left, right):
    return lax.dot_general(left, right, (((1,), (0,)), ((), ())), preferred_element_type=F32)


def dot_nt(left, right):
    return lax.dot_general(left, right, (((1,), (1,)), ((), ())), preferred_element_type=F32)


def dot_tn(left, right):
    return lax.dot_general(left, right, (((0,), (0,)), ((), ())), preferred_element_type=F32)


def params(vmem=VMEM_BYTES):
    return pltpu.CompilerParams(vmem_limit_bytes=vmem)


def cost(flops, moved):
    return pl.CostEstimate(flops=flops, bytes_accessed=moved, transcendentals=0)


def near(value):
    return pltpu.with_memory_space_constraint(value, pltpu.VMEM)


SCALARS = pl.BlockSpec(memory_space=pltpu.SMEM)
WHOLE = pl.BlockSpec(memory_space=pltpu.VMEM)


def fetch_kernel(count, *refs):
    sources, targets, sem = refs[:count], refs[count : 2 * count], refs[2 * count]
    copies = [pltpu.make_async_copy(sources[k], targets[k], sem.at[k]) for k in range(count)]
    for copy in copies:
        copy.start()
    for copy in copies:
        copy.wait()


def fetch(*arrays):
    count = len(arrays)
    return pl.pallas_call(
        lambda *refs: fetch_kernel(count, *refs),
        in_specs=[pl.BlockSpec(memory_space=pltpu.HBM)] * count,
        out_specs=[WHOLE] * count,
        out_shape=[pltpu.VMEM(array.shape, array.dtype) for array in arrays],
        scratch_shapes=[pltpu.SemaphoreType.DMA((count,))],
        compiler_params=params(),
        cost_estimate=cost(0, 5_000_000),
        name="fetch",
    )(*(pltpu.with_memory_space_constraint(array, pltpu.HBM) for array in arrays))


def assemble(pad, tile, row_one, row_two, col_one, col_two, even_row, even_col):
    for k in range(BLOCKS):
        lanes = slice(128 * k, 128 * k + 128)
        rows = row_one[:, :, lanes].astype(F32), row_two[:, :, lanes].astype(F32)
        cols = col_one[:, :, lanes].astype(F32), col_two[:, :, lanes].astype(F32)
        pad[k, 0:3, 3 : 3 + COLS, :] = jnp.where(even_row, rows[1], rows[0])
        pad[k, 3 : 3 + ROWS, 3 : 3 + COLS, :] = tile[:, :, lanes].astype(F32)
        pad[k, 3 + ROWS : 6 + ROWS, 3 : 3 + COLS, :] = jnp.where(even_row, rows[0], rows[1])
        pad[k, :, 0:3, :] = jnp.where(even_col, cols[1], cols[0])
        pad[k, :, 3 + COLS : 6 + COLS, :] = jnp.where(even_col, cols[0], cols[1])


def lanes_of(block):
    return pl.ds(pl.multiple_of(block * 128, 128), 128)


def depthwise(pad, taps, out, flip):
    def block(cb, carry):
        lanes = lanes_of(cb)
        for cg in range(COLS // 8):
            total = jnp.zeros((ROWS, 8, 128), F32)
            for s in range(7):
                band = pad[cb, :, 8 * cg + s : 8 * cg + s + 8, :]
                for r in range(7):
                    tap = 7 * (6 - r) + 6 - s if flip else 7 * r + s
                    total = total + band[r : r + ROWS] * taps[tap : tap + 1, lanes].reshape(1, 1, 128)
            out[cb, :, 8 * cg : 8 * cg + 8, :] = total
        return carry

    lax.fori_loop(0, BLOCKS, block, 0)


def grads_kernel(
    place, tile, row_one, row_two, col_one, col_two, cot, taps, vectors, w_in, b_in, w_out,
    pad, block_out, d_conv, d_row_one, d_row_two, rows_out, mine_out, theirs_out, mine_in, theirs_in,
    conv,
):
    first = place[0] == 0
    even_row = place[1] == 0
    assemble(pad, tile, row_one, row_two, col_one, col_two, even_row, first)
    depthwise(pad, taps, conv, False)
    dw_bias, gain, shift, scale, b_out = (vectors[k : k + 1, :] for k in range(5))
    rows = jnp.concatenate([conv[k].reshape(COUNT, 128) for k in range(BLOCKS)], axis=1) + dw_bias
    centred = rows - jnp.mean(rows, axis=-1, keepdims=True)
    inverse = lax.rsqrt(jnp.mean(centred * centred, axis=-1, keepdims=True) + 1e-06)
    hat = centred * inverse
    normed = (hat * gain + shift).astype(BF16)
    d_branch = (cot[...].astype(F32) * scale).astype(BF16)
    branch = b_out
    d_normed = 0.0

    fourth = lax.broadcasted_iota(jnp.int32, (8, CHUNK), 1) % 4
    fourth = fourth == lax.broadcasted_iota(jnp.int32, (8, CHUNK), 0)
    pick = lax.broadcasted_iota(jnp.int32, (CHUNK, 128), 0) // 4
    pick = (pick == lax.broadcasted_iota(jnp.int32, (CHUNK, 128), 1)).astype(F32).astype(BF16)
    upper = lax.broadcasted_iota(jnp.int32, (64, 8, 128), 1) < 4

    def by_lanes(part):
        return jnp.concatenate([part[:, :, 128 * k : 128 * k + 128] for k in range(BLOCKS)], axis=1)

    for step in range(STEPS):
        hidden = slice(CHUNK * step, CHUNK * step + CHUNK)
        pre_act = dot_nn(normed, w_in[:, hidden]) + b_in[:, hidden]
        cumul = 0.5 * (1.0 + lax.erf(pre_act * 0.7071067811865476))
        act = (pre_act * cumul).astype(BF16)
        slope = cumul + pre_act * jnp.exp(-0.5 * pre_act * pre_act) * 0.3989422804014327
        d_pre = (dot_nt(d_branch, w_out[hidden, :]) * slope).astype(BF16)
        branch = branch + dot_nn(act, w_out[hidden, :])
        d_normed = d_normed + dot_nt(d_pre, w_in[:, hidden])

        bias = jnp.sum(d_pre.astype(F32), axis=0, keepdims=True)
        rows_out[8:16, 128 * step : 128 * step + 128] = dot_nn(jnp.where(fourth, bias, 0.0).astype(BF16), pick)

        term = dot_tn(act, d_branch).reshape(CHUNK // 32, 2, 16, CH)
        chips = slice(CHUNK // 32 * step, CHUNK // 32 * (step + 1))
        mine_out[chips] = by_lanes(jnp.where(first, term[:, 0], term[:, 1])).astype(BF16)
        theirs_out[chips] = by_lanes(jnp.where(first, term[:, 1], term[:, 0])).astype(BF16)

        term = dot_tn(normed, d_pre).reshape(64, 8, CHUNK)
        kept, given = [], []
        for k in range(2):
            low = term[:, :, 128 * k : 128 * k + 128]
            high = term[:, :, 256 + 128 * k : 384 + 128 * k]
            zero = jnp.where(upper, low, pltpu.roll(high, 4, 1))
            one = jnp.where(upper, pltpu.roll(low, 4, 1), high)
            kept.append(jnp.where(first, zero, one))
            given.append(jnp.where(first, one, zero))
        mine_in[:, 16 * step : 16 * step + 16, :] = jnp.concatenate(kept, axis=1).astype(BF16)
        theirs_in[:, 16 * step : 16 * step + 16, :] = jnp.concatenate(given, axis=1).astype(BF16)

    d_hat = d_normed * gain
    grad = inverse * (
        d_hat
        - jnp.mean(d_hat, axis=-1, keepdims=True)
        - hat * jnp.mean(d_hat * hat, axis=-1, keepdims=True)
    )
    grad = grad.astype(BF16)
    out = grad.reshape(ROWS, COLS, CH)
    d_conv[...] = out
    d_row_one[...] = jnp.where(even_row, out[ROWS - 3 :], out[:3])
    d_row_two[...] = jnp.where(even_row, out[:3], out[ROWS - 3 :])
    block_out[...] = (tile[...].reshape(COUNT, CH).astype(F32) + scale * branch).astype(BF16)
    rows_out[0:1, :] = jnp.sum(grad.astype(F32), axis=0, keepdims=True)
    rows_out[1:2, :] = jnp.sum(d_normed * hat, axis=0, keepdims=True)
    rows_out[2:3, :] = jnp.sum(d_normed, axis=0, keepdims=True)
    rows_out[3:4, :] = jnp.sum(d_branch.astype(F32), axis=0, keepdims=True)
    rows_out[4:5, :] = jnp.sum(cot[...].astype(F32) * branch, axis=0, keepdims=True)


def grads(place, *operands):
    half = (64, 64, 128)
    return pl.pallas_call(
        grads_kernel,
        in_specs=[SCALARS] + [WHOLE] * len(operands),
        out_shape=[
            pltpu.VMEM(PAD, F32),
            jax.ShapeDtypeStruct((COUNT, CH), BF16),
            pltpu.VMEM((ROWS, COLS, CH), BF16),
            pltpu.VMEM((3, COLS, CH), BF16),
            pltpu.VMEM((3, COLS, CH), BF16),
            pltpu.VMEM((16, CH), F32),
            pltpu.VMEM(half, BF16),
            pltpu.VMEM(half, BF16),
            pltpu.VMEM(half, BF16),
            pltpu.VMEM(half, BF16),
        ],
        scratch_shapes=[pltpu.VMEM(TILE, F32)],
        compiler_params=params(),
        cost_estimate=cost(3_200_000_000, 12_000_000),
        name="grads",
    )(place, *(near(value) for value in operands))


def taps_kernel(pad, d_conv, rows, small, d_tile, table):
    for k in range(BLOCKS):
        d_tile[k] = d_conv[:, :, 128 * k : 128 * k + 128].astype(F32)
    table[48:128, :] = jnp.zeros((80, CH), F32)

    def block(cb, carry):
        lanes = lanes_of(cb)
        for s in range(7):
            totals = [jnp.zeros((8, 128), F32) for _ in range(7)]
            for cg in range(COLS // 8):
                band = pad[cb, :, 8 * cg + s : 8 * cg + s + 8, :]
                own = d_tile[cb, :, 8 * cg : 8 * cg + 8, :]
                for r in range(7):
                    totals[r] = totals[r] + jnp.sum(band[r : r + ROWS] * own, axis=0)
            for r in range(7):
                table[7 * r + s : 7 * r + s + 1, lanes] = jnp.sum(totals[r], axis=0, keepdims=True)
        return carry

    lax.fori_loop(0, BLOCKS, block, 0)
    table[49:54, :] = rows[0:5, :]
    table[54:58, :] = rows[8:12, :]
    small[...] = table[...].T.reshape(64, 8, 128)


def tap_rows(*operands):
    return pl.pallas_call(
        taps_kernel,
        in_specs=[WHOLE] * len(operands),
        out_shape=pltpu.VMEM((64, 8, 128), F32),
        scratch_shapes=[pltpu.VMEM(TILE, F32), pltpu.VMEM((128, CH), F32)],
        compiler_params=params(),
        cost_estimate=cost(30_000_000, 2_000_000),
        name="tap_rows",
    )(*(near(value) for value in operands))


def split_kernel(place, out_one, out_two, in_one, in_two, small_one, small_two, keep, *gives):
    even = place[2] == 0

    for k in range(32):
        kept, given = [], []
        for part in range(2):
            q = 2 * k + part
            rows = [out_one[q] + out_two[q], in_one[q] + in_two[q], (small_one[q] + small_two[q]).astype(BF16)]
            kept.append(rows)
        if (k ^ (k >> 3)) & 1:
            kept.reverse()
        at = 0
        for low, high in zip(*kept):
            size = low.shape[0]
            mine, theirs = jnp.where(even, low, high), jnp.where(even, high, low)
            keep[k, at : at + size, :] = mine
            for give, (start, end) in zip(gives, THIRDS):
                first, last = max(start, at), min(end, at + size)
                if first < last:
                    give[k, first - start : last - start, :] = theirs[first - at : last - at]
            at += size


def split_pair(place, *operands):
    return pl.pallas_call(
        split_kernel,
        in_specs=[SCALARS] + [WHOLE] * len(operands),
        out_shape=[pltpu.VMEM((32, 136, 128), BF16)]
        + [pltpu.VMEM((32, end - start, 128), BF16) for start, end in THIRDS],
        compiler_params=params(),
        cost_estimate=cost(1_000_000, 6_000_000),
        name="split_pair",
    )(place, *(near(value) for value in operands))


def add_kernel(keep, one, two, three, total):
    for given, (start, end) in zip((one, two, three), THIRDS):
        total[:, start:end, :] = keep[:, start:end, :] + given[...]


def add_pair(*operands):
    return pl.pallas_call(
        add_kernel,
        in_specs=[WHOLE] * len(operands),
        out_shape=jax.ShapeDtypeStruct((32, 136, 128), BF16),
        compiler_params=params(),
        cost_estimate=cost(1_000_000, 3_000_000),
        name="add_pair",
    )(*(near(value) for value in operands))


def sum_kernel(factor, place, spread, g_in, g_out, g_channel, g_bias):
    total = jnp.sum(spread[...].astype(F32), axis=0) * factor
    for k in range(4):
        g_out[:, 128 * k : 128 * k + 128] = total[16 * k : 16 * k + 16, :]
    for t in range(STEPS):
        for k in range(2):
            own = total[64 + 16 * t + 8 * k : 72 + 16 * t + 8 * k, :]
            at = CHUNK * t + 128 * k
            g_in[:, at : at + 128] = own[0:4]
            g_in[:, at + 256 : at + 384] = own[4:8]
    small = total[128:136, :]
    small = jnp.where(place[0] == 0, small, pltpu.roll(small, 4, 0))
    g_channel[...] = small[0:4, 0:54]
    g_bias[...] = jnp.concatenate([small[k : k + 1, 54:58] for k in range(4)], axis=1)


def sum_chips(place, spread, factor):
    shape = jax.ShapeDtypeStruct
    return pl.pallas_call(
        lambda *refs: sum_kernel(factor, *refs),
        in_specs=[pl.BlockSpec(memory_space=pltpu.SMEM), pl.BlockSpec(memory_space=pltpu.VMEM)],
        out_shape=[shape((4, HID), F32), shape((16, CH), F32), shape((4, 54), F32), shape((1, 16), F32)],
        compiler_params=pltpu.CompilerParams(vmem_limit_bytes=16 * 1024 * 1024),
        cost_estimate=pl.CostEstimate(flops=1_000_000, bytes_accessed=1_000_000, transcendentals=0),
        name="sum_chips",
    )(place, spread)


def features_kernel(place, d_conv, row_one, row_two, col_one, col_two, cot, taps, out, pad, total):
    assemble(pad, d_conv, row_one, row_two, col_one, col_two, place[1] == 0, place[0] == 0)
    depthwise(pad, taps, total, True)
    cot_wide = cot[...].astype(F32).reshape(ROWS, COLS, CH)
    for k in range(BLOCKS):
        lanes = slice(128 * k, 128 * k + 128)
        out[:, :, lanes] = (cot_wide[:, :, lanes] + total[k]).astype(BF16)


def features_part(place, *operands):
    return pl.pallas_call(
        features_kernel,
        in_specs=[SCALARS] + [WHOLE] * len(operands),
        out_shape=jax.ShapeDtypeStruct((ROWS, COLS, CH), BF16),
        scratch_shapes=[pltpu.VMEM(PAD, F32), pltpu.VMEM(TILE, F32)],
        compiler_params=params(),
        cost_estimate=cost(30_000_000, 2_000_000),
        name="features_part",
    )(place, *(near(value) for value in operands))


def exchange(one, two, axis):
    count = lax.axis_size(axis)
    met = []
    for value, start in ((one, 0), (two, 1)):
        pairs = []
        for i in range(start, count - 1, 2):
            pairs += [(i, i + 1), (i + 1, i)]
        met.append(lax.ppermute(value, axis, pairs))
    return met


def halo_sides(row_one, row_two, tile, even_row, even_col):
    top = jnp.where(even_row, row_two, row_one)
    bottom = jnp.where(even_row, row_one, row_two)
    tail = jnp.concatenate([part[:, COLS - 3 :] for part in (top, tile, bottom)], axis=0)
    head = jnp.concatenate([part[:, :3] for part in (top, tile, bottom)], axis=0)
    return jnp.where(even_col, tail, head), jnp.where(even_col, head, tail)


def swap_cores(value):
    return lax.ppermute(value, "c", [(0, 1), (1, 0)])


def places():
    for zh, zl, yh, xh, xl, yl, core in itertools.product(range(2), repeat=7):
        yield 2 * zh + zl, 2 * yh + yl, 2 * xh + xl, core


def swap_chips(value, axis):
    known = list(places())
    pairs = []
    for at, place in enumerate(known):
        met = list(place)
        met[axis] = 3 - met[axis] if place[3] else met[axis] ^ 1
        pairs.append((at, known.index(tuple(met))))
    return lax.ppermute(value, EVERY, pairs)


def spread_chips(value):
    groups = {}
    for at, (z, y, x, core) in enumerate(places()):
        groups.setdefault(((z + y + x) % 2, core), []).append(at)
    return lax.all_to_all(value, EVERY, 0, 0, axis_index_groups=list(groups.values()), tiled=True)


def shards(
    features, cotangent, dw_kernel, dw_bias, norm_gain_vector, norm_bias,
    pw_in_weight, pw_in_bias, pw_out_weight, pw_out_bias, layer_scale,
):
    factor = 1.0 / math.sqrt(COUNT * lax.axis_size(EVERY))
    core, y_hi, y_lo, x_lo, z_lo = (lax.axis_index(name).astype(jnp.int32) for name in ("c", "yh", "yl", "xl", "zl"))
    place = jnp.stack([core, y_hi, (x_lo + y_lo + z_lo) % 2])
    even_row, even_col = y_hi == 0, core == 0
    vectors = jnp.stack([dw_bias, norm_gain_vector, norm_bias, layer_scale, pw_out_bias])
    ends = features[:3], features[ROWS - 3 :]
    rows_met = exchange(jnp.where(even_row, ends[1], ends[0]), jnp.where(even_row, ends[0], ends[1]), ROW)
    sides = halo_sides(*rows_met, features, even_row, even_col)
    sides, pw_in_weight = lax.optimization_barrier((sides, pw_in_weight))
    cols_met = exchange(*sides, COL)
    tile, cot, taps, vectors, w_in, b_in, w_out = fetch(
        features, cotangent.reshape(COUNT, CH), dw_kernel, vectors, pw_in_weight,
        pw_in_bias.reshape(1, HID), pw_out_weight,
    )
    pad, block_rows, d_conv, d_one, d_two, rows, mine_out, theirs_out, mine_in, theirs_in = grads(
        place, tile, *rows_met, *cols_met, cot, taps, vectors, w_in, b_in, w_out
    )
    met_out, met_in = swap_cores(theirs_out), swap_cores(theirs_in)
    small = tap_rows(pad, d_conv, rows)
    keep, *gives = split_pair(place, mine_out, met_out, mine_in, met_in, small, swap_cores(small))
    given = [swap_chips(give, axis) for axis, give in enumerate(gives)]
    gives, d_one, d_two = lax.optimization_barrier((gives, d_one, d_two))
    d_rows = exchange(d_one, d_two, ROW)
    given, d_rows = lax.optimization_barrier((given, d_rows))
    message = add_pair(keep, *given)
    message, d_rows = lax.optimization_barrier((message, d_rows))
    spread = spread_chips(message)
    d_cols = exchange(*halo_sides(*d_rows, d_conv, even_row, even_col), COL)
    d_conv, message = lax.optimization_barrier((d_conv, message))
    grad_features = features_part(place, d_conv, *d_rows, *d_cols, cot, taps)
    grad_in, grad_out, grad_channel, grad_bias = sum_chips(place, spread, factor)
    return (
        block_rows.reshape(ROWS, COLS, CH),
        grad_features,
        grad_in,
        grad_out,
        grad_channel.T,
        grad_bias.reshape(-1),
    )


def solution(mesh):
    fine = Mesh(mesh.devices.reshape(2, 2, 2, 2, 2, 2, 2), EVERY)
    return jax.shard_map(
        shards,
        mesh=fine,
        in_specs=(P(ROW, COL, None), P(ROW, COL, None)) + (P(),) * 9,
        out_specs=(
            P(ROW, COL, None),
            P(ROW, COL, None),
            P(EVERY, None),
            P(EVERY, None),
            P(None, EVERY),
            P(EVERY),
        ),
        check_vma=False,
    )
```

```python
import itertools
import math

import jax
import jax.numpy as jnp
from jax import lax
from jax.experimental import pallas as pl
from jax.experimental.pallas import tpu as pltpu
from jax.sharding import Mesh
from jax.sharding import PartitionSpec as P

EVERY = ("zh", "zl", "yh", "xh", "xl", "yl", "c")
ROW = ("zh", "zl", "yh")
COL = ("xh", "xl", "yl", "c")
THIRDS = ((0, 48), (48, 96), (96, 136))
ROWS, COLS, CH, HID, CHUNK = 8, 32, 512, 2048, 512
COUNT = ROWS * COLS
STEPS = HID // CHUNK
BLOCKS = CH // 128
PAD = (BLOCKS, ROWS + 6, COLS + 8, 128)
TILE = (BLOCKS, ROWS, COLS, 128)
F32, BF16 = jnp.float32, jnp.bfloat16
VMEM_BYTES = 28 * 1024 * 1024


def dot_nn(left, right):
    return lax.dot_general(left, right, (((1,), (0,)), ((), ())), preferred_element_type=F32)


def dot_nt(left, right):
    return lax.dot_general(left, right, (((1,), (1,)), ((), ())), preferred_element_type=F32)


def dot_tn(left, right):
    return lax.dot_general(left, right, (((0,), (0,)), ((), ())), preferred_element_type=F32)


def params(vmem=VMEM_BYTES):
    return pltpu.CompilerParams(vmem_limit_bytes=vmem)


def cost(flops, moved):
    return pl.CostEstimate(flops=flops, bytes_accessed=moved, transcendentals=0)


def near(value):
    return pltpu.with_memory_space_constraint(value, pltpu.VMEM)


SCALARS = pl.BlockSpec(memory_space=pltpu.SMEM)
WHOLE = pl.BlockSpec(memory_space=pltpu.VMEM)


def fetch_kernel(count, *refs):
    sources, targets, sem = refs[:count], refs[count : 2 * count], refs[2 * count]
    copies = [pltpu.make_async_copy(sources[k], targets[k], sem.at[k]) for k in range(count)]
    for copy in copies:
        copy.start()
    for copy in copies:
        copy.wait()


def fetch(*arrays):
    count = len(arrays)
    return pl.pallas_call(
        lambda *refs: fetch_kernel(count, *refs),
        in_specs=[pl.BlockSpec(memory_space=pltpu.HBM)] * count,
        out_specs=[WHOLE] * count,
        out_shape=[pltpu.VMEM(array.shape, array.dtype) for array in arrays],
        scratch_shapes=[pltpu.SemaphoreType.DMA((count,))],
        compiler_params=params(),
        cost_estimate=cost(0, 5_000_000),
        name="fetch",
    )(*(pltpu.with_memory_space_constraint(array, pltpu.HBM) for array in arrays))


def assemble(pad, tile, row_one, row_two, col_one, col_two, even_row, even_col):
    for k in range(BLOCKS):
        lanes = slice(128 * k, 128 * k + 128)
        rows = row_one[:, :, lanes].astype(F32), row_two[:, :, lanes].astype(F32)
        cols = col_one[:, :, lanes].astype(F32), col_two[:, :, lanes].astype(F32)
        pad[k, 0:3, 3 : 3 + COLS, :] = jnp.where(even_row, rows[1], rows[0])
        pad[k, 3 : 3 + ROWS, 3 : 3 + COLS, :] = tile[:, :, lanes].astype(F32)
        pad[k, 3 + ROWS : 6 + ROWS, 3 : 3 + COLS, :] = jnp.where(even_row, rows[0], rows[1])
        pad[k, :, 0:3, :] = jnp.where(even_col, cols[1], cols[0])
        pad[k, :, 3 + COLS : 6 + COLS, :] = jnp.where(even_col, cols[0], cols[1])


def lanes_of(block):
    return pl.ds(pl.multiple_of(block * 128, 128), 128)


def depthwise(pad, taps, out, flip):
    def block(cb, carry):
        lanes = lanes_of(cb)
        for cg in range(COLS // 8):
            total = jnp.zeros((ROWS, 8, 128), F32)
            for s in range(7):
                band = pad[cb, :, 8 * cg + s : 8 * cg + s + 8, :]
                for r in range(7):
                    tap = 7 * (6 - r) + 6 - s if flip else 7 * r + s
                    total = total + band[r : r + ROWS] * taps[tap : tap + 1, lanes].reshape(1, 1, 128)
            out[cb, :, 8 * cg : 8 * cg + 8, :] = total
        return carry

    lax.fori_loop(0, BLOCKS, block, 0)


def grads_kernel(
    place, tile, row_one, row_two, col_one, col_two, cot, taps, vectors, w_in, b_in, w_out,
    pad, block_out, d_conv, d_row_one, d_row_two, rows_out, mine_out, theirs_out, mine_in, theirs_in,
    conv,
):
    first = place[0] == 0
    even_row = place[1] == 0
    assemble(pad, tile, row_one, row_two, col_one, col_two, even_row, first)
    depthwise(pad, taps, conv, False)
    dw_bias, gain, shift, scale, b_out = (vectors[k : k + 1, :] for k in range(5))
    rows = jnp.concatenate([conv[k].reshape(COUNT, 128) for k in range(BLOCKS)], axis=1) + dw_bias
    centred = rows - jnp.mean(rows, axis=-1, keepdims=True)
    inverse = lax.rsqrt(jnp.mean(centred * centred, axis=-1, keepdims=True) + 1e-06)
    hat = centred * inverse
    normed = (hat * gain + shift).astype(BF16)
    d_branch = (cot[...].astype(F32) * scale).astype(BF16)
    branch = b_out
    d_normed = 0.0

    fourth = lax.broadcasted_iota(jnp.int32, (8, CHUNK), 1) % 4
    fourth = fourth == lax.broadcasted_iota(jnp.int32, (8, CHUNK), 0)
    pick = lax.broadcasted_iota(jnp.int32, (CHUNK, 128), 0) // 4
    pick = (pick == lax.broadcasted_iota(jnp.int32, (CHUNK, 128), 1)).astype(F32).astype(BF16)
    upper = lax.broadcasted_iota(jnp.int32, (64, 8, 128), 1) < 4

    def by_lanes(part):
        return jnp.concatenate([part[:, :, 128 * k : 128 * k + 128] for k in range(BLOCKS)], axis=1)

    for step in range(STEPS):
        hidden = slice(CHUNK * step, CHUNK * step + CHUNK)
        pre_act = dot_nn(normed, w_in[:, hidden]) + b_in[:, hidden]
        cumul = 0.5 * (1.0 + lax.erf(pre_act * 0.7071067811865476))
        act = (pre_act * cumul).astype(BF16)
        slope = cumul + pre_act * jnp.exp(-0.5 * pre_act * pre_act) * 0.3989422804014327
        d_pre = (dot_nt(d_branch, w_out[hidden, :]) * slope).astype(BF16)
        branch = branch + dot_nn(act, w_out[hidden, :])
        d_normed = d_normed + dot_nt(d_pre, w_in[:, hidden])

        bias = jnp.sum(d_pre.astype(F32), axis=0, keepdims=True)
        rows_out[8:16, 128 * step : 128 * step + 128] = dot_nn(jnp.where(fourth, bias, 0.0).astype(BF16), pick)

        term = dot_tn(act, d_branch).reshape(CHUNK // 32, 2, 16, CH)
        chips = slice(CHUNK // 32 * step, CHUNK // 32 * (step + 1))
        mine_out[chips] = by_lanes(jnp.where(first, term[:, 0], term[:, 1])).astype(BF16)
        theirs_out[chips] = by_lanes(jnp.where(first, term[:, 1], term[:, 0])).astype(BF16)

        term = dot_tn(normed, d_pre).reshape(64, 8, CHUNK)
        kept, given = [], []
        for k in range(2):
            low = term[:, :, 128 * k : 128 * k + 128]
            high = term[:, :, 256 + 128 * k : 384 + 128 * k]
            zero = jnp.where(upper, low, pltpu.roll(high, 4, 1))
            one = jnp.where(upper, pltpu.roll(low, 4, 1), high)
            kept.append(jnp.where(first, zero, one))
            given.append(jnp.where(first, one, zero))
        mine_in[:, 16 * step : 16 * step + 16, :] = jnp.concatenate(kept, axis=1).astype(BF16)
        theirs_in[:, 16 * step : 16 * step + 16, :] = jnp.concatenate(given, axis=1).astype(BF16)

    d_hat = d_normed * gain
    grad = inverse * (
        d_hat
        - jnp.mean(d_hat, axis=-1, keepdims=True)
        - hat * jnp.mean(d_hat * hat, axis=-1, keepdims=True)
    )
    grad = grad.astype(BF16)
    out = grad.reshape(ROWS, COLS, CH)
    d_conv[...] = out
    d_row_one[...] = jnp.where(even_row, out[ROWS - 3 :], out[:3])
    d_row_two[...] = jnp.where(even_row, out[:3], out[ROWS - 3 :])
    block_out[...] = (tile[...].reshape(COUNT, CH).astype(F32) + scale * branch).astype(BF16)
    rows_out[0:1, :] = jnp.sum(grad.astype(F32), axis=0, keepdims=True)
    rows_out[1:2, :] = jnp.sum(d_normed * hat, axis=0, keepdims=True)
    rows_out[2:3, :] = jnp.sum(d_normed, axis=0, keepdims=True)
    rows_out[3:4, :] = jnp.sum(d_branch.astype(F32), axis=0, keepdims=True)
    rows_out[4:5, :] = jnp.sum(cot[...].astype(F32) * branch, axis=0, keepdims=True)


def grads(place, *operands):
    half = (64, 64, 128)
    return pl.pallas_call(
        grads_kernel,
        in_specs=[SCALARS] + [WHOLE] * len(operands),
        out_shape=[
            pltpu.VMEM(PAD, F32),
            jax.ShapeDtypeStruct((COUNT, CH), BF16),
            pltpu.VMEM((ROWS, COLS, CH), BF16),
            pltpu.VMEM((3, COLS, CH), BF16),
            pltpu.VMEM((3, COLS, CH), BF16),
            pltpu.VMEM((16, CH), F32),
            pltpu.VMEM(half, BF16),
            pltpu.VMEM(half, BF16),
            pltpu.VMEM(half, BF16),
            pltpu.VMEM(half, BF16),
        ],
        scratch_shapes=[pltpu.VMEM(TILE, F32)],
        compiler_params=params(),
        cost_estimate=cost(3_200_000_000, 12_000_000),
        name="grads",
    )(place, *(near(value) for value in operands))


def taps_kernel(pad, d_conv, rows, small, d_tile, table):
    for k in range(BLOCKS):
        d_tile[k] = d_conv[:, :, 128 * k : 128 * k + 128].astype(F32)
    table[48:128, :] = jnp.zeros((80, CH), F32)

    def block(cb, carry):
        lanes = lanes_of(cb)
        for s in range(7):
            totals = [jnp.zeros((8, 128), F32) for _ in range(7)]
            for cg in range(COLS // 8):
                band = pad[cb, :, 8 * cg + s : 8 * cg + s + 8, :]
                own = d_tile[cb, :, 8 * cg : 8 * cg + 8, :]
                for r in range(7):
                    totals[r] = totals[r] + jnp.sum(band[r : r + ROWS] * own, axis=0)
            for r in range(7):
                table[7 * r + s : 7 * r + s + 1, lanes] = jnp.sum(totals[r], axis=0, keepdims=True)
        return carry

    lax.fori_loop(0, BLOCKS, block, 0)
    table[49:54, :] = rows[0:5, :]
    table[54:58, :] = rows[8:12, :]
    small[...] = table[...].T.reshape(64, 8, 128)


def tap_rows(*operands):
    return pl.pallas_call(
        taps_kernel,
        in_specs=[WHOLE] * len(operands),
        out_shape=pltpu.VMEM((64, 8, 128), F32),
        scratch_shapes=[pltpu.VMEM(TILE, F32), pltpu.VMEM((128, CH), F32)],
        compiler_params=params(),
        cost_estimate=cost(30_000_000, 2_000_000),
        name="tap_rows",
    )(*(near(value) for value in operands))


def split_kernel(place, out_one, out_two, in_one, in_two, small_one, small_two, keep, *gives):
    even = place[2] == 0

    for k in range(32):
        kept, given = [], []
        for part in range(2):
            q = 2 * k + part
            rows = [out_one[q] + out_two[q], in_one[q] + in_two[q], (small_one[q] + small_two[q]).astype(BF16)]
            kept.append(rows)
        if (k ^ (k >> 3)) & 1:
            kept.reverse()
        at = 0
        for low, high in zip(*kept):
            size = low.shape[0]
            mine, theirs = jnp.where(even, low, high), jnp.where(even, high, low)
            keep[k, at : at + size, :] = mine
            for give, (start, end) in zip(gives, THIRDS):
                first, last = max(start, at), min(end, at + size)
                if first < last:
                    give[k, first - start : last - start, :] = theirs[first - at : last - at]
            at += size


def split_pair(place, *operands):
    return pl.pallas_call(
        split_kernel,
        in_specs=[SCALARS] + [WHOLE] * len(operands),
        out_shape=[pltpu.VMEM((32, 136, 128), BF16)]
        + [pltpu.VMEM((32, end - start, 128), BF16) for start, end in THIRDS],
        compiler_params=params(),
        cost_estimate=cost(1_000_000, 6_000_000),
        name="split_pair",
    )(place, *(near(value) for value in operands))


def add_kernel(keep, one, two, three, total):
    for given, (start, end) in zip((one, two, three), THIRDS):
        total[:, start:end, :] = keep[:, start:end, :] + given[...]


def add_pair(*operands):
    return pl.pallas_call(
        add_kernel,
        in_specs=[WHOLE] * len(operands),
        out_shape=jax.ShapeDtypeStruct((32, 136, 128), BF16),
        compiler_params=params(),
        cost_estimate=cost(1_000_000, 3_000_000),
        name="add_pair",
    )(*(near(value) for value in operands))


def sum_kernel(factor, place, spread, g_in, g_out, g_channel, g_bias):
    total = jnp.sum(spread[...].astype(F32), axis=0) * factor
    for k in range(4):
        g_out[:, 128 * k : 128 * k + 128] = total[16 * k : 16 * k + 16, :]
    for t in range(STEPS):
        for k in range(2):
            own = total[64 + 16 * t + 8 * k : 72 + 16 * t + 8 * k, :]
            at = CHUNK * t + 128 * k
            g_in[:, at : at + 128] = own[0:4]
            g_in[:, at + 256 : at + 384] = own[4:8]
    small = total[128:136, :]
    small = jnp.where(place[0] == 0, small, pltpu.roll(small, 4, 0))
    g_channel[...] = small[0:4, 0:54]
    g_bias[...] = jnp.concatenate([small[k : k + 1, 54:58] for k in range(4)], axis=1)


def sum_chips(place, spread, factor):
    shape = jax.ShapeDtypeStruct
    return pl.pallas_call(
        lambda *refs: sum_kernel(factor, *refs),
        in_specs=[pl.BlockSpec(memory_space=pltpu.SMEM), pl.BlockSpec(memory_space=pltpu.VMEM)],
        out_shape=[shape((4, HID), F32), shape((16, CH), F32), shape((4, 54), F32), shape((1, 16), F32)],
        compiler_params=pltpu.CompilerParams(vmem_limit_bytes=16 * 1024 * 1024),
        cost_estimate=pl.CostEstimate(flops=1_000_000, bytes_accessed=1_000_000, transcendentals=0),
        name="sum_chips",
    )(place, spread)


def main_kernel(place, d_conv, row_one, row_two, cot, taps, total, pad):
    even_row = place[1] == 0
    cot_wide = cot[...].astype(F32).reshape(ROWS, COLS, CH)
    for k in range(BLOCKS):
        lanes = slice(128 * k, 128 * k + 128)
        rows = row_one[:, :, lanes].astype(F32), row_two[:, :, lanes].astype(F32)
        pad[k, :, 0:3, :] = jnp.zeros((ROWS + 6, 3, 128), F32)
        pad[k, :, 3 + COLS : 6 + COLS, :] = jnp.zeros((ROWS + 6, 3, 128), F32)
        pad[k, 0:3, 3 : 3 + COLS, :] = jnp.where(even_row, rows[1], rows[0])
        pad[k, 3 : 3 + ROWS, 3 : 3 + COLS, :] = d_conv[:, :, lanes].astype(F32)
        pad[k, 3 + ROWS : 6 + ROWS, 3 : 3 + COLS, :] = jnp.where(even_row, rows[0], rows[1])
    depthwise(pad, taps, total, True)
    for k in range(BLOCKS):
        total[k] = total[k] + cot_wide[:, :, 128 * k : 128 * k + 128]


def features_main(place, *operands):
    return pl.pallas_call(
        main_kernel,
        in_specs=[SCALARS] + [WHOLE] * len(operands),
        out_shape=pltpu.VMEM(TILE, F32),
        scratch_shapes=[pltpu.VMEM(PAD, F32)],
        compiler_params=params(),
        cost_estimate=cost(30_000_000, 2_000_000),
        name="features_main",
    )(place, *(near(value) for value in operands))


def edge_kernel(place, total, col_one, col_two, taps, out, left, right, edges):
    even_col = place[0] == 0
    left[...] = jnp.zeros(left.shape, F32)
    right[...] = jnp.zeros(right.shape, F32)
    for k in range(BLOCKS):
        lanes = slice(128 * k, 128 * k + 128)
        cols = col_one[:, :, lanes].astype(F32), col_two[:, :, lanes].astype(F32)
        left[k, :, 0:3, :] = jnp.where(even_col, cols[1], cols[0])
        right[k, :, 7:10, :] = jnp.where(even_col, cols[0], cols[1])

    def block(cb, carry):
        lanes = lanes_of(cb)
        for at, halo, start in ((0, left, 0), (8, right, 4)):
            column = 0 if at == 0 else COLS - 8
            value = total[cb, :, column : column + 8, :]
            for s in range(3):
                band = halo[cb, :, s : s + 8, :]
                for r in range(7):
                    tap = 7 * (6 - r) + 6 - s - start
                    value = value + band[r : r + ROWS] * taps[tap : tap + 1, lanes].reshape(1, 1, 128)
            edges[cb, :, at : at + 8, :] = value
        return carry

    lax.fori_loop(0, BLOCKS, block, 0)
    for k in range(BLOCKS):
        parts = [edges[k, :, 0:8, :], total[k, :, 8 : COLS - 8, :], edges[k, :, 8:16, :]]
        out[:, :, 128 * k : 128 * k + 128] = jnp.concatenate(parts, axis=1).astype(BF16)


def features_edge(place, *operands):
    side = (BLOCKS, ROWS + 6, 16, 128)
    return pl.pallas_call(
        edge_kernel,
        in_specs=[SCALARS] + [WHOLE] * len(operands),
        out_shape=jax.ShapeDtypeStruct((ROWS, COLS, CH), BF16),
        scratch_shapes=[pltpu.VMEM(side, F32), pltpu.VMEM(side, F32), pltpu.VMEM((BLOCKS, ROWS, 16, 128), F32)],
        compiler_params=params(),
        cost_estimate=cost(6_000_000, 1_000_000),
        name="features_edge",
    )(place, *(near(value) for value in operands))


def exchange(one, two, axis):
    count = lax.axis_size(axis)
    met = []
    for value, start in ((one, 0), (two, 1)):
        pairs = []
        for i in range(start, count - 1, 2):
            pairs += [(i, i + 1), (i + 1, i)]
        met.append(lax.ppermute(value, axis, pairs))
    return met


def halo_sides(row_one, row_two, tile, even_row, even_col):
    top = jnp.where(even_row, row_two, row_one)
    bottom = jnp.where(even_row, row_one, row_two)
    tail = jnp.concatenate([part[:, COLS - 3 :] for part in (top, tile, bottom)], axis=0)
    head = jnp.concatenate([part[:, :3] for part in (top, tile, bottom)], axis=0)
    return jnp.where(even_col, tail, head), jnp.where(even_col, head, tail)


def swap_cores(value):
    return lax.ppermute(value, "c", [(0, 1), (1, 0)])


def places():
    for zh, zl, yh, xh, xl, yl, core in itertools.product(range(2), repeat=7):
        yield 2 * zh + zl, 2 * yh + yl, 2 * xh + xl, core


def swap_chips(value, axis):
    known = list(places())
    pairs = []
    for at, place in enumerate(known):
        met = list(place)
        met[axis] = 3 - met[axis] if place[3] else met[axis] ^ 1
        pairs.append((at, known.index(tuple(met))))
    return lax.ppermute(value, EVERY, pairs)


def spread_chips(value):
    groups = {}
    for at, (z, y, x, core) in enumerate(places()):
        groups.setdefault(((z + y + x) % 2, core), []).append(at)
    return lax.all_to_all(value, EVERY, 0, 0, axis_index_groups=list(groups.values()), tiled=True)


def shards(
    features, cotangent, dw_kernel, dw_bias, norm_gain_vector, norm_bias,
    pw_in_weight, pw_in_bias, pw_out_weight, pw_out_bias, layer_scale,
):
    factor = 1.0 / math.sqrt(COUNT * lax.axis_size(EVERY))
    core, y_hi, y_lo, x_lo, z_lo = (lax.axis_index(name).astype(jnp.int32) for name in ("c", "yh", "yl", "xl", "zl"))
    place = jnp.stack([core, y_hi, (x_lo + y_lo + z_lo) % 2])
    even_row, even_col = y_hi == 0, core == 0
    vectors = jnp.stack([dw_bias, norm_gain_vector, norm_bias, layer_scale, pw_out_bias])
    ends = features[:3], features[ROWS - 3 :]
    rows_met = exchange(jnp.where(even_row, ends[1], ends[0]), jnp.where(even_row, ends[0], ends[1]), ROW)
    tile, cot, taps, vectors, w_in, b_in, w_out = fetch(
        features, cotangent.reshape(COUNT, CH), dw_kernel, vectors, pw_in_weight,
        pw_in_bias.reshape(1, HID), pw_out_weight,
    )
    sides = halo_sides(*rows_met, features, even_row, even_col)
    sides, w_in = lax.optimization_barrier((sides, w_in))
    cols_met = exchange(*sides, COL)
    pad, block_rows, d_conv, d_one, d_two, rows, mine_out, theirs_out, mine_in, theirs_in = grads(
        place, tile, *rows_met, *cols_met, cot, taps, vectors, w_in, b_in, w_out
    )
    met_out, met_in = swap_cores(theirs_out), swap_cores(theirs_in)
    small = tap_rows(pad, d_conv, rows)
    keep, *gives = split_pair(place, mine_out, met_out, mine_in, met_in, small, swap_cores(small))
    given = [swap_chips(give, axis) for axis, give in enumerate(gives)]
    gives, d_one, d_two = lax.optimization_barrier((gives, d_one, d_two))
    d_rows = exchange(d_one, d_two, ROW)
    message = add_pair(keep, *given)
    message, d_rows = lax.optimization_barrier((message, d_rows))
    spread = spread_chips(message)
    d_cols = exchange(*halo_sides(*d_rows, d_conv, even_row, even_col), COL)
    total = features_main(place, d_conv, *d_rows, cot, taps)
    grad_features = features_edge(place, total, *d_cols, taps)
    grad_in, grad_out, grad_channel, grad_bias = sum_chips(place, spread, factor)
    return (
        block_rows.reshape(ROWS, COLS, CH),
        grad_features,
        grad_in,
        grad_out,
        grad_channel.T,
        grad_bias.reshape(-1),
    )


def solution(mesh):
    fine = Mesh(mesh.devices.reshape(2, 2, 2, 2, 2, 2, 2), EVERY)
    return jax.shard_map(
        shards,
        mesh=fine,
        in_specs=(P(ROW, COL, None), P(ROW, COL, None)) + (P(),) * 9,
        out_specs=(
            P(ROW, COL, None),
            P(ROW, COL, None),
            P(EVERY, None),
            P(EVERY, None),
            P(None, EVERY),
            P(EVERY),
        ),
        check_vma=False,
    )
```

```python
import itertools
import math

import jax
import jax.numpy as jnp
from jax import lax
from jax.experimental import pallas as pl
from jax.experimental.pallas import tpu as pltpu
from jax.sharding import Mesh
from jax.sharding import PartitionSpec as P

EVERY = ("zh", "zl", "yh", "xh", "xl", "yl", "c")
ROW = ("zh", "zl", "yh")
COL = ("xh", "xl", "yl", "c")
THIRDS = ((0, 48), (48, 96), (96, 136))
ROWS, COLS, CH, HID, CHUNK = 8, 32, 512, 2048, 512
COUNT = ROWS * COLS
STEPS = HID // CHUNK
BLOCKS = CH // 128
PAD = (BLOCKS, ROWS + 6, COLS + 8, 128)
TILE = (BLOCKS, ROWS, COLS, 128)
F32, BF16 = jnp.float32, jnp.bfloat16
VMEM_BYTES = 28 * 1024 * 1024


def dot_nn(left, right):
    return lax.dot_general(left, right, (((1,), (0,)), ((), ())), preferred_element_type=F32)


def dot_nt(left, right):
    return lax.dot_general(left, right, (((1,), (1,)), ((), ())), preferred_element_type=F32)


def dot_tn(left, right):
    return lax.dot_general(left, right, (((0,), (0,)), ((), ())), preferred_element_type=F32)


def params(vmem=VMEM_BYTES):
    return pltpu.CompilerParams(vmem_limit_bytes=vmem)


def cost(flops, moved):
    return pl.CostEstimate(flops=flops, bytes_accessed=moved, transcendentals=0)


def near(value):
    return pltpu.with_memory_space_constraint(value, pltpu.VMEM)


SCALARS = pl.BlockSpec(memory_space=pltpu.SMEM)
WHOLE = pl.BlockSpec(memory_space=pltpu.VMEM)


def fetch_kernel(count, *refs):
    sources, targets, sem = refs[:count], refs[count : 2 * count], refs[2 * count]
    copies = [pltpu.make_async_copy(sources[k], targets[k], sem.at[k]) for k in range(count)]
    for copy in copies:
        copy.start()
    for copy in copies:
        copy.wait()


def fetch(*arrays):
    count = len(arrays)
    return pl.pallas_call(
        lambda *refs: fetch_kernel(count, *refs),
        in_specs=[pl.BlockSpec(memory_space=pltpu.HBM)] * count,
        out_specs=[WHOLE] * count,
        out_shape=[pltpu.VMEM(array.shape, array.dtype) for array in arrays],
        scratch_shapes=[pltpu.SemaphoreType.DMA((count,))],
        compiler_params=params(),
        cost_estimate=cost(0, 5_000_000),
        name="fetch",
    )(*(pltpu.with_memory_space_constraint(array, pltpu.HBM) for array in arrays))


def assemble(pad, tile, row_one, row_two, col_one, col_two, even_row, even_col):
    for k in range(BLOCKS):
        lanes = slice(128 * k, 128 * k + 128)
        rows = row_one[:, :, lanes].astype(F32), row_two[:, :, lanes].astype(F32)
        cols = col_one[:, :, lanes].astype(F32), col_two[:, :, lanes].astype(F32)
        pad[k, 0:3, 3 : 3 + COLS, :] = jnp.where(even_row, rows[1], rows[0])
        pad[k, 3 : 3 + ROWS, 3 : 3 + COLS, :] = tile[:, :, lanes].astype(F32)
        pad[k, 3 + ROWS : 6 + ROWS, 3 : 3 + COLS, :] = jnp.where(even_row, rows[0], rows[1])
        pad[k, :, 0:3, :] = jnp.where(even_col, cols[1], cols[0])
        pad[k, :, 3 + COLS : 6 + COLS, :] = jnp.where(even_col, cols[0], cols[1])


def lanes_of(block):
    return pl.ds(pl.multiple_of(block * 128, 128), 128)


def depthwise(pad, taps, out, flip):
    def block(cb, carry):
        lanes = lanes_of(cb)
        for cg in range(COLS // 8):
            total = jnp.zeros((ROWS, 8, 128), F32)
            for s in range(7):
                band = pad[cb, :, 8 * cg + s : 8 * cg + s + 8, :]
                for r in range(7):
                    tap = 7 * (6 - r) + 6 - s if flip else 7 * r + s
                    total = total + band[r : r + ROWS] * taps[tap : tap + 1, lanes].reshape(1, 1, 128)
            out[cb, :, 8 * cg : 8 * cg + 8, :] = total
        return carry

    lax.fori_loop(0, BLOCKS, block, 0)


def grads_kernel(
    place, tile, row_one, row_two, col_one, col_two, cot, taps, vectors, w_in, b_in, w_out,
    pad, block_out, d_conv, d_row_one, d_row_two, rows_out, mine_out, theirs_out, mine_in, theirs_in,
    conv,
):
    first = place[0] == 0
    even_row = place[1] == 0
    assemble(pad, tile, row_one, row_two, col_one, col_two, even_row, first)
    depthwise(pad, taps, conv, False)
    dw_bias, gain, shift, scale, b_out = (vectors[k : k + 1, :] for k in range(5))
    rows = jnp.concatenate([conv[k].reshape(COUNT, 128) for k in range(BLOCKS)], axis=1) + dw_bias
    centred = rows - jnp.mean(rows, axis=-1, keepdims=True)
    inverse = lax.rsqrt(jnp.mean(centred * centred, axis=-1, keepdims=True) + 1e-06)
    hat = centred * inverse
    normed = (hat * gain + shift).astype(BF16)
    d_branch = (cot[...].astype(F32) * scale).astype(BF16)
    branch = b_out
    d_normed = 0.0

    fourth = lax.broadcasted_iota(jnp.int32, (8, CHUNK), 1) % 4
    fourth = fourth == lax.broadcasted_iota(jnp.int32, (8, CHUNK), 0)
    pick = lax.broadcasted_iota(jnp.int32, (CHUNK, 128), 0) // 4
    pick = (pick == lax.broadcasted_iota(jnp.int32, (CHUNK, 128), 1)).astype(F32).astype(BF16)
    upper = lax.broadcasted_iota(jnp.int32, (64, 8, 128), 1) < 4

    def by_lanes(part):
        return jnp.concatenate([part[:, :, 128 * k : 128 * k + 128] for k in range(BLOCKS)], axis=1)

    for step in range(STEPS):
        hidden = slice(CHUNK * step, CHUNK * step + CHUNK)
        pre_act = dot_nn(normed, w_in[:, hidden]) + b_in[:, hidden]
        cumul = 0.5 * (1.0 + lax.erf(pre_act * 0.7071067811865476))
        act = (pre_act * cumul).astype(BF16)
        slope = cumul + pre_act * jnp.exp(-0.5 * pre_act * pre_act) * 0.3989422804014327
        d_pre = (dot_nt(d_branch, w_out[hidden, :]) * slope).astype(BF16)
        branch = branch + dot_nn(act, w_out[hidden, :])
        d_normed = d_normed + dot_nt(d_pre, w_in[:, hidden])

        bias = jnp.sum(d_pre.astype(F32), axis=0, keepdims=True)
        rows_out[8:16, 128 * step : 128 * step + 128] = dot_nn(jnp.where(fourth, bias, 0.0).astype(BF16), pick)

        term = dot_tn(act, d_branch).reshape(CHUNK // 32, 2, 16, CH)
        chips = slice(CHUNK // 32 * step, CHUNK // 32 * (step + 1))
        mine_out[chips] = by_lanes(jnp.where(first, term[:, 0], term[:, 1])).astype(BF16)
        theirs_out[chips] = by_lanes(jnp.where(first, term[:, 1], term[:, 0])).astype(BF16)

        term = dot_tn(normed, d_pre).reshape(64, 8, CHUNK)
        kept, given = [], []
        for k in range(2):
            low = term[:, :, 128 * k : 128 * k + 128]
            high = term[:, :, 256 + 128 * k : 384 + 128 * k]
            zero = jnp.where(upper, low, pltpu.roll(high, 4, 1))
            one = jnp.where(upper, pltpu.roll(low, 4, 1), high)
            kept.append(jnp.where(first, zero, one))
            given.append(jnp.where(first, one, zero))
        mine_in[:, 16 * step : 16 * step + 16, :] = jnp.concatenate(kept, axis=1).astype(BF16)
        theirs_in[:, 16 * step : 16 * step + 16, :] = jnp.concatenate(given, axis=1).astype(BF16)

    d_hat = d_normed * gain
    grad = inverse * (
        d_hat
        - jnp.mean(d_hat, axis=-1, keepdims=True)
        - hat * jnp.mean(d_hat * hat, axis=-1, keepdims=True)
    )
    grad = grad.astype(BF16)
    out = grad.reshape(ROWS, COLS, CH)
    d_conv[...] = out
    d_row_one[...] = jnp.where(even_row, out[ROWS - 3 :], out[:3])
    d_row_two[...] = jnp.where(even_row, out[:3], out[ROWS - 3 :])
    block_out[...] = (tile[...].reshape(COUNT, CH).astype(F32) + scale * branch).astype(BF16)
    rows_out[0:1, :] = jnp.sum(grad.astype(F32), axis=0, keepdims=True)
    rows_out[1:2, :] = jnp.sum(d_normed * hat, axis=0, keepdims=True)
    rows_out[2:3, :] = jnp.sum(d_normed, axis=0, keepdims=True)
    rows_out[3:4, :] = jnp.sum(d_branch.astype(F32), axis=0, keepdims=True)
    rows_out[4:5, :] = jnp.sum(cot[...].astype(F32) * branch, axis=0, keepdims=True)


def grads(place, *operands):
    half = (64, 64, 128)
    return pl.pallas_call(
        grads_kernel,
        in_specs=[SCALARS] + [WHOLE] * len(operands),
        out_shape=[
            pltpu.VMEM(PAD, F32),
            jax.ShapeDtypeStruct((COUNT, CH), BF16),
            pltpu.VMEM((ROWS, COLS, CH), BF16),
            pltpu.VMEM((3, COLS, CH), BF16),
            pltpu.VMEM((3, COLS, CH), BF16),
            pltpu.VMEM((16, CH), F32),
            pltpu.VMEM(half, BF16),
            pltpu.VMEM(half, BF16),
            pltpu.VMEM(half, BF16),
            pltpu.VMEM(half, BF16),
        ],
        scratch_shapes=[pltpu.VMEM(TILE, F32)],
        compiler_params=params(),
        cost_estimate=cost(3_200_000_000, 12_000_000),
        name="grads",
    )(place, *(near(value) for value in operands))


def taps_kernel(pad, d_conv, rows, small, d_tile, table):
    for k in range(BLOCKS):
        d_tile[k] = d_conv[:, :, 128 * k : 128 * k + 128].astype(F32)
    table[48:128, :] = jnp.zeros((80, CH), F32)

    def block(cb, carry):
        lanes = lanes_of(cb)
        for s in range(7):
            totals = [jnp.zeros((8, 128), F32) for _ in range(7)]
            for cg in range(COLS // 8):
                band = pad[cb, :, 8 * cg + s : 8 * cg + s + 8, :]
                own = d_tile[cb, :, 8 * cg : 8 * cg + 8, :]
                for r in range(7):
                    totals[r] = totals[r] + jnp.sum(band[r : r + ROWS] * own, axis=0)
            for r in range(7):
                table[7 * r + s : 7 * r + s + 1, lanes] = jnp.sum(totals[r], axis=0, keepdims=True)
        return carry

    lax.fori_loop(0, BLOCKS, block, 0)
    table[49:54, :] = rows[0:5, :]
    table[54:58, :] = rows[8:12, :]
    small[...] = table[...].T.reshape(64, 8, 128)


def tap_rows(*operands):
    return pl.pallas_call(
        taps_kernel,
        in_specs=[WHOLE] * len(operands),
        out_shape=pltpu.VMEM((64, 8, 128), F32),
        scratch_shapes=[pltpu.VMEM(TILE, F32), pltpu.VMEM((128, CH), F32)],
        compiler_params=params(),
        cost_estimate=cost(30_000_000, 2_000_000),
        name="tap_rows",
    )(*(near(value) for value in operands))


def split_kernel(place, out_one, out_two, in_one, in_two, small_one, small_two, keep, *gives):
    even = place[2] == 0

    for k in range(32):
        kept, given = [], []
        for part in range(2):
            q = 2 * k + part
            rows = [out_one[q] + out_two[q], in_one[q] + in_two[q], (small_one[q] + small_two[q]).astype(BF16)]
            kept.append(rows)
        if (k ^ (k >> 3)) & 1:
            kept.reverse()
        at = 0
        for low, high in zip(*kept):
            size = low.shape[0]
            mine, theirs = jnp.where(even, low, high), jnp.where(even, high, low)
            keep[k, at : at + size, :] = mine
            for give, (start, end) in zip(gives, THIRDS):
                first, last = max(start, at), min(end, at + size)
                if first < last:
                    give[k, first - start : last - start, :] = theirs[first - at : last - at]
            at += size


def split_pair(place, *operands):
    return pl.pallas_call(
        split_kernel,
        in_specs=[SCALARS] + [WHOLE] * len(operands),
        out_shape=[pltpu.VMEM((32, 136, 128), BF16)]
        + [pltpu.VMEM((32, end - start, 128), BF16) for start, end in THIRDS],
        compiler_params=params(),
        cost_estimate=cost(1_000_000, 6_000_000),
        name="split_pair",
    )(place, *(near(value) for value in operands))


def add_kernel(keep, one, two, three, total):
    for given, (start, end) in zip((one, two, three), THIRDS):
        total[:, start:end, :] = keep[:, start:end, :] + given[...]


def add_pair(*operands):
    return pl.pallas_call(
        add_kernel,
        in_specs=[WHOLE] * len(operands),
        out_shape=jax.ShapeDtypeStruct((32, 136, 128), BF16),
        compiler_params=params(),
        cost_estimate=cost(1_000_000, 3_000_000),
        name="add_pair",
    )(*(near(value) for value in operands))


def sum_kernel(factor, place, spread, g_in, g_out, g_channel, g_bias):
    total = jnp.sum(spread[...].astype(F32), axis=0) * factor
    for k in range(4):
        g_out[:, 128 * k : 128 * k + 128] = total[16 * k : 16 * k + 16, :]
    for t in range(STEPS):
        for k in range(2):
            own = total[64 + 16 * t + 8 * k : 72 + 16 * t + 8 * k, :]
            at = CHUNK * t + 128 * k
            g_in[:, at : at + 128] = own[0:4]
            g_in[:, at + 256 : at + 384] = own[4:8]
    small = total[128:136, :]
    small = jnp.where(place[0] == 0, small, pltpu.roll(small, 4, 0))
    g_channel[...] = small[0:4, 0:54]
    g_bias[...] = jnp.concatenate([small[k : k + 1, 54:58] for k in range(4)], axis=1)


def sum_chips(place, spread, factor):
    shape = jax.ShapeDtypeStruct
    return pl.pallas_call(
        lambda *refs: sum_kernel(factor, *refs),
        in_specs=[pl.BlockSpec(memory_space=pltpu.SMEM), pl.BlockSpec(memory_space=pltpu.VMEM)],
        out_shape=[shape((4, HID), F32), shape((16, CH), F32), shape((4, 54), F32), shape((1, 16), F32)],
        compiler_params=pltpu.CompilerParams(vmem_limit_bytes=16 * 1024 * 1024),
        cost_estimate=pl.CostEstimate(flops=1_000_000, bytes_accessed=1_000_000, transcendentals=0),
        name="sum_chips",
    )(place, spread)


def main_kernel(place, d_conv, row_one, row_two, cot, taps, total, pad):
    even_row = place[1] == 0
    cot_wide = cot[...].astype(F32).reshape(ROWS, COLS, CH)
    for k in range(BLOCKS):
        lanes = slice(128 * k, 128 * k + 128)
        rows = row_one[:, :, lanes].astype(F32), row_two[:, :, lanes].astype(F32)
        pad[k, :, 0:3, :] = jnp.zeros((ROWS + 6, 3, 128), F32)
        pad[k, :, 3 + COLS : 6 + COLS, :] = jnp.zeros((ROWS + 6, 3, 128), F32)
        pad[k, 0:3, 3 : 3 + COLS, :] = jnp.where(even_row, rows[1], rows[0])
        pad[k, 3 : 3 + ROWS, 3 : 3 + COLS, :] = d_conv[:, :, lanes].astype(F32)
        pad[k, 3 + ROWS : 6 + ROWS, 3 : 3 + COLS, :] = jnp.where(even_row, rows[0], rows[1])
    depthwise(pad, taps, total, True)
    for k in range(BLOCKS):
        total[k] = total[k] + cot_wide[:, :, 128 * k : 128 * k + 128]


def features_main(place, *operands):
    return pl.pallas_call(
        main_kernel,
        in_specs=[SCALARS] + [WHOLE] * len(operands),
        out_shape=pltpu.VMEM(TILE, F32),
        scratch_shapes=[pltpu.VMEM(PAD, F32)],
        compiler_params=params(),
        cost_estimate=cost(30_000_000, 2_000_000),
        name="features_main",
    )(place, *(near(value) for value in operands))


def edge_kernel(place, total, col_one, col_two, taps, out, left, right, edges):
    even_col = place[0] == 0
    left[...] = jnp.zeros(left.shape, F32)
    right[...] = jnp.zeros(right.shape, F32)
    for k in range(BLOCKS):
        lanes = slice(128 * k, 128 * k + 128)
        cols = col_one[:, :, lanes].astype(F32), col_two[:, :, lanes].astype(F32)
        left[k, :, 0:3, :] = jnp.where(even_col, cols[1], cols[0])
        right[k, :, 7:10, :] = jnp.where(even_col, cols[0], cols[1])

    def block(cb, carry):
        lanes = lanes_of(cb)
        for at, halo, start in ((0, left, 0), (8, right, 4)):
            column = 0 if at == 0 else COLS - 8
            value = total[cb, :, column : column + 8, :]
            for s in range(3):
                band = halo[cb, :, s : s + 8, :]
                for r in range(7):
                    tap = 7 * (6 - r) + 6 - s - start
                    value = value + band[r : r + ROWS] * taps[tap : tap + 1, lanes].reshape(1, 1, 128)
            edges[cb, :, at : at + 8, :] = value
        return carry

    lax.fori_loop(0, BLOCKS, block, 0)
    for k in range(BLOCKS):
        parts = [edges[k, :, 0:8, :], total[k, :, 8 : COLS - 8, :], edges[k, :, 8:16, :]]
        out[:, :, 128 * k : 128 * k + 128] = jnp.concatenate(parts, axis=1).astype(BF16)


def features_edge(place, *operands):
    side = (BLOCKS, ROWS + 6, 16, 128)
    return pl.pallas_call(
        edge_kernel,
        in_specs=[SCALARS] + [WHOLE] * len(operands),
        out_shape=jax.ShapeDtypeStruct((ROWS, COLS, CH), BF16),
        scratch_shapes=[pltpu.VMEM(side, F32), pltpu.VMEM(side, F32), pltpu.VMEM((BLOCKS, ROWS, 16, 128), F32)],
        compiler_params=params(),
        cost_estimate=cost(6_000_000, 1_000_000),
        name="features_edge",
    )(place, *(near(value) for value in operands))


def exchange(one, two, axis):
    count = lax.axis_size(axis)
    met = []
    for value, start in ((one, 0), (two, 1)):
        pairs = []
        for i in range(start, count - 1, 2):
            pairs += [(i, i + 1), (i + 1, i)]
        met.append(lax.ppermute(value, axis, pairs))
    return met


def halo_sides(row_one, row_two, tile, even_row, even_col):
    top = jnp.where(even_row, row_two, row_one)
    bottom = jnp.where(even_row, row_one, row_two)
    tail = jnp.concatenate([part[:, COLS - 3 :] for part in (top, tile, bottom)], axis=0)
    head = jnp.concatenate([part[:, :3] for part in (top, tile, bottom)], axis=0)
    return jnp.where(even_col, tail, head), jnp.where(even_col, head, tail)


def swap_cores(value):
    return lax.ppermute(value, "c", [(0, 1), (1, 0)])


def places():
    for zh, zl, yh, xh, xl, yl, core in itertools.product(range(2), repeat=7):
        yield 2 * zh + zl, 2 * yh + yl, 2 * xh + xl, core


def swap_chips(value, axis):
    known = list(places())
    pairs = []
    for at, place in enumerate(known):
        met = list(place)
        met[axis] = 3 - met[axis] if place[3] else met[axis] ^ 1
        pairs.append((at, known.index(tuple(met))))
    return lax.ppermute(value, EVERY, pairs)


def spread_chips(value):
    groups = {}
    for at, (z, y, x, core) in enumerate(places()):
        groups.setdefault(((z + y + x) % 2, core), []).append(at)
    return lax.all_to_all(value, EVERY, 0, 0, axis_index_groups=list(groups.values()), tiled=True)


def shards(
    features, cotangent, dw_kernel, dw_bias, norm_gain_vector, norm_bias,
    pw_in_weight, pw_in_bias, pw_out_weight, pw_out_bias, layer_scale,
):
    factor = 1.0 / math.sqrt(COUNT * lax.axis_size(EVERY))
    core, y_hi, y_lo, x_lo, z_lo = (lax.axis_index(name).astype(jnp.int32) for name in ("c", "yh", "yl", "xl", "zl"))
    place = jnp.stack([core, y_hi, (x_lo + y_lo + z_lo) % 2])
    even_row, even_col = y_hi == 0, core == 0
    vectors = jnp.stack([dw_bias, norm_gain_vector, norm_bias, layer_scale, pw_out_bias])
    ends = features[:3], features[ROWS - 3 :]
    rows_met = exchange(jnp.where(even_row, ends[1], ends[0]), jnp.where(even_row, ends[0], ends[1]), ROW)
    tile, cot, taps, vectors, w_in, b_in, w_out = fetch(
        features, cotangent.reshape(COUNT, CH), dw_kernel, vectors, pw_in_weight,
        pw_in_bias.reshape(1, HID), pw_out_weight,
    )
    sides = halo_sides(*rows_met, features, even_row, even_col)
    sides, w_in = lax.optimization_barrier((sides, w_in))
    cols_met = exchange(*sides, COL)
    pad, block_rows, d_conv, d_one, d_two, rows, mine_out, theirs_out, mine_in, theirs_in = grads(
        place, tile, *rows_met, *cols_met, cot, taps, vectors, w_in, b_in, w_out
    )
    met_out, met_in = swap_cores(theirs_out), swap_cores(theirs_in)
    small = tap_rows(pad, d_conv, rows)
    d_rows = exchange(d_one, d_two, ROW)
    met_small = swap_cores(small)
    met_out, met_in, met_small, d_rows = lax.optimization_barrier((met_out, met_in, met_small, d_rows))
    keep, *gives = split_pair(place, mine_out, met_out, mine_in, met_in, small, met_small)
    given = [swap_chips(give, axis) for axis, give in enumerate(gives)]
    gives, sides = lax.optimization_barrier((gives, halo_sides(*d_rows, d_conv, even_row, even_col)))
    d_cols = exchange(*sides, COL)
    given, d_cols = lax.optimization_barrier((given, d_cols))
    message = add_pair(keep, *given)
    spread = spread_chips(message)
    d_conv, message = lax.optimization_barrier((d_conv, message))
    total = features_main(place, d_conv, *d_rows, cot, taps)
    grad_features = features_edge(place, total, *d_cols, taps)
    grad_in, grad_out, grad_channel, grad_bias = sum_chips(place, spread, factor)
    return (
        block_rows.reshape(ROWS, COLS, CH),
        grad_features,
        grad_in,
        grad_out,
        grad_channel.T,
        grad_bias.reshape(-1),
    )


def solution(mesh):
    fine = Mesh(mesh.devices.reshape(2, 2, 2, 2, 2, 2, 2), EVERY)
    return jax.shard_map(
        shards,
        mesh=fine,
        in_specs=(P(ROW, COL, None), P(ROW, COL, None)) + (P(),) * 9,
        out_specs=(
            P(ROW, COL, None),
            P(ROW, COL, None),
            P(EVERY, None),
            P(EVERY, None),
            P(None, EVERY),
            P(EVERY),
        ),
        check_vma=False,
    )
```
